32 devices in a mesh: orbit: 2 (over x), lon: 16 (over z, y, core).
Axes of the slice: x: 2, y: 2, z: 4, core: 2. Of those that a mesh axis runs over, the one named last changes fastest.
Arguments:
- interp: bfloat16 [64, 16, 256, 128], P('orbit', 'lon'), may hold values from -0.5 to 0.5
- obs_value: float32 [64, 16, 256], P('orbit', 'lon'), may hold values from -20 to 20
- obs_weight: float32 [64, 16, 256], P('orbit', 'lon'), may hold values from 0.5 to 4
- block_map: int32 [64, 16], P('orbit', 'lon'), may hold values from 0 to 511
- live_count: int32 [2, 16], P('orbit', 'lon'), may hold values from 4 to 32, as said below
- kappa2: float32 [1024, 1024], P('lon'), may hold values from 0.01 to 1
Outputs:
- solution: float32 [1024, 1024], P('lon')
- residual: float32 [1024, 1024], P('lon')
The draws below stay inside these ranges and needn't reach their ends.
Inputs may be any that keep to these rules, and one draw needn't show every extreme that they name: `live_count`: live blocks of the device of orbit group o in band l; its slots at or beyond this count are padding; some device holds exactly 32.
All inputs are finite; a program needn't handle non-finite values.
Results may differ from the reference program's by a relative error of at most 0.014.
Values sent between devices are 32-bit elements; how exact they have to be, the bound alone decides.
No kernel may reach another device: no remote copies, remote signals or barrier semaphores. Data moves between devices by JAX's collectives and lax.ppermute only.
A program may use at most 64 MiB of HBM per device.

```python
import math
import jax
import jax.numpy as jnp
from jax import lax

LAT = 1024
OB_DEV = 32
OBS_BLK = 256
CELL_BLK = 128
ITERS = 2
BANDS = 16
ORBITS = 2
NLON = 1024
OBS_BLOCKS = 64
NB_DEV = 512


def draw_obs_value(key, part):
    ramp = 1.0 + 2.0 * jnp.arange(BANDS, dtype=jnp.float32) / max(BANDS - 1, 1)
    base = jnp.clip(jax.random.normal(key, (OBS_BLOCKS, BANDS, OBS_BLK), jnp.float32), -4.0, 4.0)
    return base * ramp[None, :, None]


def draw_live_count(key, part):
    lowest = max(1, OB_DEV // 8)
    first_key, second_key, orbit_key, band_key = jax.random.split(jax.random.fold_in(key, 17), 4)
    first = jax.random.randint(first_key, (ORBITS, BANDS), lowest, OB_DEV + 1)
    second = jax.random.randint(second_key, (ORBITS, BANDS), lowest, OB_DEV + 1)
    counts = jnp.minimum(first, second).astype(jnp.int32)
    orbit_pick = jax.random.randint(orbit_key, (), 0, ORBITS)
    band_pick = jax.random.randint(band_key, (), 0, BANDS)
    return counts.at[orbit_pick, band_pick].set(OB_DEV)


def place_ends(values, key, smallest, largest):
    index_at = [jax.random.randint(jax.random.fold_in(key, axis), (), 0, length) for axis, length in enumerate(values.shape)]
    widest = values.shape.index(max(values.shape))
    neighbour = index_at[:widest] + [(index_at[widest] + 1) % values.shape[widest]] + index_at[widest + 1:]
    return values.at[tuple(index_at)].set(smallest).at[tuple(neighbour)].set(largest)


def steps_of(key, extent, pieces, least, largest):
    gain = 1.0
    for position, blocks in pieces:
        steps = jax.random.uniform(jax.random.fold_in(jax.random.fold_in(key, 6), position), (blocks,), jnp.float32, least / len(pieces), largest / len(pieces))
        gain = gain * jnp.repeat(jnp.exp(steps), extent[position] // blocks).reshape((-1,) + (1,) * (len(extent) - 1 - position))
    return gain


def noise(stream_key, dims, width, limit, pieces=(), held_as=jnp.bfloat16):
    values = jax.random.normal(stream_key, dims, jnp.float32) * width
    if len(pieces) > 0:
        values = steps_of(stream_key, dims, pieces, -0.22, 0.18) * values
    return jnp.clip(values, min=-limit, max=limit).astype(held_as)


def setup_inputs(seed: int = 0) -> dict:
    key_list = jax.random.split(jax.random.key(seed), 7)
    interp = noise(key_list[0], (OBS_BLOCKS, BANDS, OBS_BLK, CELL_BLK), CELL_BLK ** -0.5, 0.5, ((0, 2), (1, 16)))
    obs_value = draw_obs_value(jax.random.fold_in(key_list[6], 71), 0)
    obs_weight = jnp.clip(jnp.exp(math.log(4.0) - 2.0794415 * jax.random.uniform(key_list[2], (OBS_BLOCKS, BANDS, OBS_BLK), jnp.float32) ** steps_of(key_list[2], (OBS_BLOCKS, BANDS, OBS_BLK), ((0, 2), (1, 16)), -0.2, 0.2)), 0.5, 4.0)
    block_map = place_ends(jax.random.randint(key_list[3], (OBS_BLOCKS, BANDS), 0, NB_DEV), jax.random.fold_in(key_list[3], 1), 0, NB_DEV - 1).astype(jnp.int32)
    live_count = draw_live_count(jax.random.fold_in(key_list[6], 71), 0)
    kappa2 = jnp.clip(jnp.exp(math.log(1.0) - 4.6051702 * jax.random.uniform(key_list[5], (NLON, LAT), jnp.float32) ** steps_of(key_list[5], (NLON, LAT), ((0, 16),), -0.2, 0.2)), 0.01, 1.0)
    return dict(interp=interp, obs_value=obs_value, obs_weight=obs_weight, block_map=block_map, live_count=live_count, kappa2=kappa2)


prior_weight = 0.0625


def stencil(field, kappa2):
    padded = jnp.pad(field, ((0, 0), (1, 1)))
    lat_pair = padded[:, 2:] + padded[:, :-2]
    return (kappa2 + 4.0) * field - jnp.roll(field, 1, 0) - jnp.roll(field, -1, 0) - lat_pair


def prior_term(field, kappa2):
    return prior_weight * stencil(stencil(field, kappa2), kappa2)


def live_mask(live_count):
    slot_index = jnp.arange(OBS_BLOCKS) % OB_DEV
    group_index = jnp.arange(OBS_BLOCKS) // OB_DEV
    return (slot_index[:, None] < live_count[group_index, :]).astype(jnp.float32)


def take_band(array, band):
    return lax.dynamic_index_in_dim(array, band, 1, keepdims=False)


def data_terms(interp, obs_value, obs_weight, block_map, live):
    scaled = lax.optimization_barrier((obs_weight * obs_value).astype(jnp.bfloat16)).astype(jnp.float32)

    def per_band(band):
        matrices = take_band(interp, band).astype(jnp.float32)
        weights = take_band(obs_weight, band)
        targets = take_band(block_map, band)
        active = take_band(live, band)
        first = jnp.einsum('sqc,sq->sc', matrices, take_band(scaled, band), precision=lax.Precision.HIGHEST) * active[:, None]
        second = jnp.einsum('sqc,sq->sc', matrices * matrices, weights, precision=lax.Precision.HIGHEST) * active[:, None]
        zeros = jnp.zeros((NB_DEV, CELL_BLK), jnp.float32)
        return zeros.at[targets].add(first), zeros.at[targets].add(second)

    right_side, obs_diag = lax.map(per_band, jnp.arange(BANDS))
    return right_side.reshape(NLON, LAT), obs_diag.reshape(NLON, LAT)


def normal_term(field, interp, obs_weight, block_map, live):
    rounded = lax.optimization_barrier(field.astype(jnp.bfloat16)).astype(jnp.float32)
    cell_rows = rounded.reshape(BANDS, NB_DEV, CELL_BLK)

    def per_band(band):
        matrices = take_band(interp, band).astype(jnp.float32)
        weights = take_band(obs_weight, band)
        targets = take_band(block_map, band)
        active = take_band(live, band)
        band_cells = lax.dynamic_index_in_dim(cell_rows, band, 0, keepdims=False)
        picked = band_cells[targets]
        predicted = jnp.einsum('sqc,sc->sq', matrices, picked, precision=lax.Precision.HIGHEST)
        scaled = lax.optimization_barrier((weights * predicted).astype(jnp.bfloat16)).astype(jnp.float32)
        back = jnp.einsum('sqc,sq->sc', matrices, scaled, precision=lax.Precision.HIGHEST) * active[:, None]
        return jnp.zeros((NB_DEV, CELL_BLK), jnp.float32).at[targets].add(back)

    return lax.map(per_band, jnp.arange(BANDS)).reshape(NLON, LAT)


def reference(interp, obs_value, obs_weight, block_map, live_count, kappa2):
    live = live_mask(live_count)
    right_side, obs_diag = data_terms(interp, obs_value, obs_weight, block_map, live)
    precond = prior_weight * ((kappa2 + 4.0) ** 2 + 4.0) + obs_diag

    def system(field):
        return prior_term(field, kappa2) + normal_term(field, interp, obs_weight, block_map, live)

    solution = jnp.zeros_like(right_side)
    residual = right_side
    scaled_res = residual / precond
    direction = scaled_res
    product_now = jnp.sum(residual * scaled_res)
    for turn in range(ITERS):
        image = system(direction)
        alpha = product_now / jnp.sum(direction * image)
        solution = solution + alpha * direction
        residual = residual - alpha * image
        if turn + 1 < ITERS:
            scaled_res = residual / precond
            product_next = jnp.sum(residual * scaled_res)
            direction = scaled_res + (product_next / product_now) * direction
            product_now = product_next
    return solution, residual
```

```python
import functools

import jax
import jax.numpy as jnp
from jax import lax
from jax.experimental import pallas as pl
from jax.experimental.pallas import tpu as pltpu
from jax.sharding import PartitionSpec as P

PRIOR_WEIGHT = 0.0625
GROUP = 8
LANES = 128
F32 = jnp.float32
BF16 = jnp.bfloat16
VMEM_BYTES = 48 * 1024 * 1024


def two_terms(value):
    high = value.astype(BF16)
    low = (value - high.astype(F32)).astype(BF16)
    return high, low


def stacked_terms(value):
    return jnp.concatenate(two_terms(value), axis=0)


def fold_terms(product):
    half = product.shape[0] // 2
    return product[:half] + product[half:]


def dot(left, right):
    return lax.dot_general(left, right, (((1,), (0,)), ((), ())), preferred_element_type=F32)


def dot_transposed(left, right):
    return lax.dot_general(left, right, (((1,), (1,)), ((), ())), preferred_element_type=F32)


def pick_row(total, product, slot):
    rows = lax.broadcasted_iota(jnp.int32, product.shape, 0)
    return jnp.where(rows == slot, product, total)


def lat_pair(field):
    pieces = field.shape[1]
    piece = lax.broadcasted_iota(jnp.int32, field.shape, 1)
    lane = lax.broadcasted_iota(jnp.int32, field.shape, 2)
    south = pltpu.roll(field, 1, 2)
    north = pltpu.roll(field, LANES - 1, 2)
    south_over = jnp.where(piece == 0, 0.0, pltpu.roll(south, 1, 1))
    north_over = jnp.where(piece == pieces - 1, 0.0, pltpu.roll(north, pieces - 1, 1))
    return jnp.where(lane == 0, south_over, south) + jnp.where(lane == LANES - 1, north_over, north)


def stencil(field, shifted):
    center = field[1:-1]
    return shifted * center - field[2:] - field[:-2] - lat_pair(center)


def data_kernel(
    orbits, count_ref, map_ref, interp_ref, value_ref, weight_ref, message_ref, matrices_ref, sems
):
    slots = matrices_ref.shape[0]
    groups = slots // GROUP
    copies = []
    for group in range(groups):
        part = pl.ds(group * GROUP, GROUP)
        copies.append(
            pltpu.make_async_copy(interp_ref.at[part], matrices_ref.at[part], sems.at[group])
        )
        copies[-1].start()
    orbit = lax.axis_index("orbit")
    total = orbits * slots
    place = lax.broadcasted_iota(jnp.int32, (GROUP, LANES), 0) * LANES
    place = place + lax.broadcasted_iota(jnp.int32, (GROUP, LANES), 1)
    slot_here = jnp.where(place >= total, place - total, place) - orbit * slots
    target_row = jnp.zeros((GROUP, LANES), jnp.int32)
    count = count_ref[0]
    for slot in range(slots):
        live_target = jnp.where(slot < count, map_ref[slot] + 1, 0)
        target_row = jnp.where(slot_here == slot, live_target, target_row)
    target_row = jnp.where(place < 2 * total, target_row, 0)
    message_ref[pl.ds(2 * slots, GROUP), :] = target_row.astype(F32)
    for group in range(groups):
        part = pl.ds(group * GROUP, GROUP)
        weights = weight_ref[part, 0, :]
        scaled = (weights * value_ref[part, 0, :]).astype(BF16)
        scaled = jnp.concatenate([scaled, scaled], axis=0)
        weight_terms = stacked_terms(weights)
        first = jnp.zeros((2 * GROUP, LANES), F32)
        second = jnp.zeros((GROUP, LANES), F32)
        copies[group].wait()
        for slot in range(GROUP):
            matrix = matrices_ref[group * GROUP + slot]
            first = pick_row(first, dot(scaled, matrix), slot)
            wide = matrix.astype(F32)
            square_high, square_low = two_terms(wide * wide)
            product = dot(weight_terms, square_high) + dot(weight_terms, square_low)
            second = pick_row(second, fold_terms(product), slot)
        message_ref[part, :] = first[:GROUP]
        message_ref[pl.ds(slots + group * GROUP, GROUP), :] = second


def kappa_kernel(kappa_ref, shifted_ref):
    columns, pieces, _ = shifted_ref.shape
    for piece in range(pieces):
        part = kappa_ref[:, pl.ds(piece * LANES, LANES)]
        shifted_ref[:, piece, :] = part + 4.0


def gather_messages(orbits, slots, message_refs, order_ref):
    orbit = lax.axis_index("orbit")
    for step in range(orbits):
        source = lax.rem(orbit + step, orbits)
        rows = pl.ds(pl.multiple_of(source * slots, slots), slots)
        order_ref[rows, :] = message_refs[step]


def start_kernel(
    orbits, parity, shifted_ref, *refs
):
    message_refs = refs[:orbits]
    field_ref, right_ref, precond_ref, scatter_ref, even_ref, odd_ref, order_ref = refs[orbits:]
    slots = (message_refs[0].shape[0] - GROUP) // 2
    cells = scatter_ref.shape[0]
    targets = message_refs[0][pl.ds(2 * slots, GROUP), :]
    for ref in message_refs[1:]:
        targets = targets + ref[pl.ds(2 * slots, GROUP), :]
    targets = targets.astype(jnp.int32) - 1
    row = lax.broadcasted_iota(jnp.int32, (cells, LANES), 0)
    for piece in range(scatter_ref.shape[1] // LANES):
        hit = row == targets[piece : piece + 1, :]
        scatter_ref[:, pl.ds(piece * LANES, LANES)] = jnp.where(hit, 1.0, 0.0).astype(BF16)
    sums = []
    for part in range(2):
        rows = pl.ds(part * slots, slots)
        gather_messages(orbits, slots, [ref[rows, :] for ref in message_refs], order_ref)
        sums.append(scattered(scatter_ref[...], order_ref[...]))
    right_side, obs_diag = (value.reshape(field_ref.shape) for value in sums)
    shifted = shifted_ref[...]
    precond = PRIOR_WEIGHT * (shifted * shifted + 4.0) + obs_diag
    field = right_side / precond
    right_ref[...] = right_side
    precond_ref[...] = precond
    field_ref[...] = field
    columns = field.shape[0]
    top = jnp.concatenate([field[:2], shifted[:1]], axis=0)
    bottom = jnp.concatenate([field[columns - 2 :], shifted[columns - 1 :]], axis=0)
    store_edges(parity, top, bottom, even_ref, odd_ref)


def scattered(one_hot, slots):
    terms = stacked_terms(slots)
    spare = one_hot.shape[1] - terms.shape[0]
    if spare:
        terms = jnp.concatenate([terms, jnp.zeros((spare, LANES), BF16)], axis=0)
    return dot(one_hot, terms)


def store_edges(parity, top, bottom, even_ref, odd_ref):
    flip = parity()
    even_ref[...] = jnp.where(flip, top, bottom)
    odd_ref[...] = jnp.where(flip, bottom, top)


def load_edges(parity, even_ref, odd_ref):
    flip = parity()
    even, odd = even_ref[...], odd_ref[...]
    return jnp.where(flip, even, odd), jnp.where(flip, odd, even)


def normal_kernel(map_ref, field_ref, weight_ref, matrices_ref, out_ref, picked_ref):
    slots = matrices_ref.shape[0]
    for slot in range(slots):
        picked_ref[pl.ds(slot, 1), :] = field_ref[pl.ds(map_ref[slot], 1), :]
    for group in range(slots // GROUP):
        part = pl.ds(group * GROUP, GROUP)
        cells = stacked_terms(picked_ref[part, :])
        predicted = jnp.zeros((GROUP, matrices_ref.shape[1]), F32)
        for slot in range(GROUP):
            product = dot_transposed(cells, matrices_ref[group * GROUP + slot])
            predicted = pick_row(predicted, fold_terms(product), slot)
        scaled = stacked_terms(weight_ref[part, 0, :] * predicted)
        back = jnp.zeros((GROUP, LANES), F32)
        for slot in range(GROUP):
            product = dot(scaled, matrices_ref[group * GROUP + slot])
            back = pick_row(back, fold_terms(product), slot)
        out_ref[part, :] = back


def extended(field, top, bottom):
    return jnp.concatenate([top, field, bottom], axis=0)


def prior_parts(field, shifted, top, bottom, shifted_top, shifted_bottom):
    first = stencil(
        extended(field, top, bottom), extended(shifted, shifted_top, shifted_bottom)
    )
    return PRIOR_WEIGHT * stencil(first, shifted)


def system(parity, orbits, refs):
    (field_ref, shifted_ref, even_ref, odd_ref, rim_even_ref, rim_odd_ref, scatter_ref) = refs[:7]
    slot_refs = refs[7 : 7 + orbits]
    order_ref = refs[-1]
    slots = slot_refs[0].shape[0]
    gather_messages(orbits, slots, [ref[...] for ref in slot_refs], order_ref)
    normal = scattered(scatter_ref[...], order_ref[...]).reshape(field_ref.shape)
    top, bottom = load_edges(parity, even_ref, odd_ref)
    rim_top, rim_bottom = load_edges(parity, rim_even_ref, rim_odd_ref)
    prior = prior_parts(
        field_ref[...], shifted_ref[...], top[:2], bottom[:2], rim_top[2:], rim_bottom[2:]
    )
    return prior + normal, refs[7 + orbits : -1]


def first_kernel(parity, orbits, *refs):
    image, rest = system(parity, orbits, refs)
    precond_ref, image_ref, next_ref, even_ref, odd_ref = rest
    following = image / precond_ref[...]
    image_ref[...] = image
    next_ref[...] = following
    store_edges(parity, following[:2], following[following.shape[0] - 2 :], even_ref, odd_ref)


def second_kernel(parity, orbits, *refs):
    image, rest = system(parity, orbits, refs)
    start_ref, right_ref, first_ref, image_ref, sums_ref = rest
    field = refs[0][...]
    start, first = start_ref[...], first_ref[...]
    own = jnp.where(lax.axis_index("orbit") == 0, 1.0, 0.0)
    lane = lax.broadcasted_iota(jnp.int32, (1, LANES), 1)
    line = jnp.zeros((1, LANES), F32)
    pairs = ((right_ref[...], start), (start, first), (first, field), (field, image))
    for index, (left, right) in enumerate(pairs):
        by_lane = jnp.sum(jnp.sum(left * right, axis=0), axis=0, keepdims=True)
        value = jnp.sum(by_lane, axis=1, keepdims=True) * own
        line = jnp.where(lane == index, value, line)
    sums_ref[...] = jnp.broadcast_to(line[None], sums_ref.shape)
    image_ref[...] = image


def last_kernel(
    sums_ref, start_ref, next_ref, right_ref, first_ref, second_ref, out_ref, residual_ref
):
    line = jnp.sum(sums_ref[...], axis=0)
    lane = lax.broadcasted_iota(jnp.int32, line.shape, 1)
    product, energy, cross, following = (
        jnp.sum(jnp.where(lane == index, line, 0.0), axis=1, keepdims=True) for index in range(4)
    )
    alpha = product / energy
    later = product - 2.0 * alpha * energy + alpha * alpha * cross
    grown = 1.0 + later / product
    later_energy = (
        grown * grown * energy - 2.0 * alpha * grown * cross + alpha * alpha * following
    )
    later_alpha = later / later_energy
    on_start = alpha + later_alpha * grown
    on_next = -alpha * later_alpha
    columns, pieces, _ = start_ref.shape
    for piece in range(pieces):
        lanes = pl.ds(piece * LANES, LANES)
        out_ref[:, lanes] = on_start * start_ref[:, piece, :] + on_next * next_ref[:, piece, :]
        residual_ref[:, lanes] = (
            right_ref[:, piece, :]
            - on_start * first_ref[:, piece, :]
            - on_next * second_ref[:, piece, :]
        )


def per_device(orbits, bands, interp, obs_value, obs_weight, block_map, live_count, kappa2):
    slots, _, observations, width = interp.shape
    columns, latitudes = kappa2.shape
    pieces = latitudes // width
    cells = columns * pieces
    field_shape = (columns, pieces, width)
    paired = bands % 2 == 0

    def parity():
        return lax.rem(lax.axis_index("lon"), 2) == 1 if paired else False

    vmem = pl.BlockSpec(memory_space=pltpu.VMEM)
    smem = pl.BlockSpec(memory_space=pltpu.SMEM)

    def call(kernel, outs, in_specs, scratch=(), name=None):
        return pl.pallas_call(
            kernel,
            out_shape=tuple(jax.ShapeDtypeStruct(shape, dtype) for shape, dtype in outs),
            in_specs=in_specs,
            out_specs=tuple(vmem for _ in outs),
            scratch_shapes=list(scratch),
            compiler_params=pltpu.CompilerParams(vmem_limit_bytes=VMEM_BYTES),
            name=name,
        )

    def from_others(value):
        return [value] + [
            lax.ppermute(value, "orbit", [((i + step) % orbits, i) for i in range(orbits)])
            for step in range(1, orbits)
        ]

    def from_neighbours(even, odd):
        if paired:
            even_pairs = [(i, i ^ 1) for i in range(bands)]
            odd_pairs = [(i, (i + 1 if i % 2 else i - 1) % bands) for i in range(bands)]
            return lax.ppermute(even, "lon", even_pairs), lax.ppermute(odd, "lon", odd_pairs)
        up = [(i, (i + 1) % bands) for i in range(bands)]
        down = [((i + 1) % bands, i) for i in range(bands)]
        return lax.ppermute(odd, "lon", down), lax.ppermute(even, "lon", up)

    matrices_in = interp.reshape(slots, observations, width)
    targets = block_map.reshape(slots)
    message, matrices = call(
        functools.partial(data_kernel, orbits),
        (((2 * slots + GROUP, width), F32), ((slots, observations, width), BF16)),
        [smem, smem, pl.BlockSpec(memory_space=pl.ANY), vmem, vmem],
        [pltpu.SemaphoreType.DMA((slots // GROUP,))],
        "data_terms",
    )(live_count.reshape(1), targets, matrices_in, obs_value, obs_weight)
    messages = from_others(message)
    (shifted,) = call(kappa_kernel, ((field_shape, F32),), [vmem], (), "kappa_rows")(kappa2)

    order = pltpu.VMEM((orbits * slots, width), F32)
    edge_width = -(-2 * orbits * slots // LANES) * LANES
    rim = ((3, pieces, width), F32)
    edge = ((2, pieces, width), F32)
    field = (field_shape, F32)
    start, right_side, precond, scatter, even, odd = call(
        functools.partial(start_kernel, orbits, parity),
        (field, field, field, ((cells, edge_width), BF16), rim, rim),
        [vmem] * (1 + orbits),
        [order],
        "start",
    )(shifted, *messages)

    def normal_slots(value, name):
        (out,) = call(
            normal_kernel,
            (((slots, width), F32),),
            [smem, vmem, vmem, vmem],
            [pltpu.VMEM((slots, width), F32)],
            name,
        )(targets, value.reshape(cells, width), obs_weight, matrices)
        return from_others(out)

    rim_even, rim_odd = from_neighbours(even, odd)
    terms = normal_slots(start, "normal_start")
    first, following, even, odd = call(
        functools.partial(first_kernel, parity, orbits),
        (field, field, edge, edge),
        [vmem] * (8 + orbits),
        [order],
        "first_image",
    )(start, shifted, rim_even, rim_odd, rim_even, rim_odd, scatter, *terms, precond)

    even, odd = from_neighbours(even, odd)
    terms = normal_slots(following, "normal_next")
    second, sums = call(
        functools.partial(second_kernel, parity, orbits),
        (field, ((orbits * bands, 1, width), F32)),
        [vmem] * (10 + orbits),
        [order],
        "second_image",
    )(following, shifted, even, odd, rim_even, rim_odd, scatter, *terms, start, right_side, first)
    sums = lax.all_to_all(sums, ("orbit", "lon"), 0, 0, tiled=True)
    return call(
        last_kernel,
        ((kappa2.shape, F32), (kappa2.shape, F32)),
        [vmem] * 6,
        (),
        "combine",
    )(sums, start, following, right_side, first, second)


def solution(mesh):
    in_specs = (
        P("orbit", "lon", None, None),
        P("orbit", "lon", None),
        P("orbit", "lon", None),
        P("orbit", "lon"),
        P("orbit", "lon"),
        P("lon", None),
    )
    out_specs = (P("lon", None), P("lon", None))
    body = functools.partial(per_device, mesh.shape["orbit"], mesh.shape["lon"])
    return jax.shard_map(
        body, mesh=mesh, in_specs=in_specs, out_specs=out_specs, check_vma=False
    )
```

```python
import functools

import jax
import jax.numpy as jnp
from jax import lax
from jax.experimental import pallas as pl
from jax.experimental.pallas import tpu as pltpu
from jax.sharding import PartitionSpec as P

PRIOR_WEIGHT = 0.0625
GROUP = 8
LANES = 128
F32 = jnp.float32
BF16 = jnp.bfloat16
VMEM_BYTES = 48 * 1024 * 1024
DATA_VMEM_BYTES = 59 * 1024 * 1024
CHUNK = 16
WORK = 1 << 32


def two_terms(value):
    high = value.astype(BF16)
    low = (value - high.astype(F32)).astype(BF16)
    return high, low


def stacked_terms(value):
    return jnp.concatenate(two_terms(value), axis=0)


def fold_terms(product):
    half = product.shape[0] // 2
    return product[:half] + product[half:]


def dot(left, right):
    return lax.dot_general(left, right, (((1,), (0,)), ((), ())), preferred_element_type=F32)


def dot_transposed(left, right):
    return lax.dot_general(left, right, (((1,), (1,)), ((), ())), preferred_element_type=F32)


def pick_row(total, product, slot):
    rows = lax.broadcasted_iota(jnp.int32, product.shape, 0)
    return jnp.where(rows == slot, product, total)


def lat_pair(field):
    pieces = field.shape[1]
    piece = lax.broadcasted_iota(jnp.int32, field.shape, 1)
    lane = lax.broadcasted_iota(jnp.int32, field.shape, 2)
    south = pltpu.roll(field, 1, 2)
    north = pltpu.roll(field, LANES - 1, 2)
    south_over = jnp.where(piece == 0, 0.0, pltpu.roll(south, 1, 1))
    north_over = jnp.where(piece == pieces - 1, 0.0, pltpu.roll(north, pieces - 1, 1))
    return jnp.where(lane == 0, south_over, south) + jnp.where(lane == LANES - 1, north_over, north)


def stencil(field, shifted):
    center = field[1:-1]
    return shifted * center - field[2:] - field[:-2] - lat_pair(center)


def data_kernel(
    orbits,
    count_in,
    map_in,
    interp_in,
    value_in,
    weight_in,
    message_ref,
    matrices_ref,
    weight_ref,
    pick_ref,
    count_ref,
    map_ref,
    value_rows,
    weight_rows,
    sems,
):
    slots = matrices_ref.shape[0]
    pairs = ((weight_in, weight_rows), (value_in, value_rows), (map_in, map_ref), (count_in, count_ref))
    small = [
        pltpu.make_async_copy(source, target, sems.at[index])
        for index, (source, target) in enumerate(pairs)
    ]
    large = []
    for index in range(slots // CHUNK):
        part = pl.ds(index * CHUNK, CHUNK)
        large.append(
            pltpu.make_async_copy(
                interp_in.at[part], matrices_ref.at[part], sems.at[len(small) + index]
            )
        )
    for copy in small + large:
        copy.start()
    for copy in small:
        copy.wait()
    orbit = lax.axis_index("orbit")
    total = orbits * slots
    place = lax.broadcasted_iota(jnp.int32, (GROUP, LANES), 0) * LANES
    place = place + lax.broadcasted_iota(jnp.int32, (GROUP, LANES), 1)
    slot_here = jnp.where(place >= total, place - total, place) - orbit * slots
    target_row = jnp.zeros((GROUP, LANES), jnp.int32)
    count = count_ref[0]
    for slot in range(slots):
        live_target = jnp.where(slot < count, map_ref[slot] + 1, 0)
        target_row = jnp.where(slot_here == slot, live_target, target_row)
    target_row = jnp.where(place < 2 * total, target_row, 0)
    message_ref[pl.ds(2 * slots, GROUP), :] = target_row.astype(F32)
    row = lax.broadcasted_iota(jnp.int32, (GROUP, pick_ref.shape[1]), 0)
    cell = lax.broadcasted_iota(jnp.int32, row.shape, 1)
    for group in range(slots // GROUP):
        target = jnp.zeros(row.shape, jnp.int32)
        for slot in range(GROUP):
            target = jnp.where(row == slot, map_ref[group * GROUP + slot], target)
        part = pl.ds(group * GROUP, GROUP)
        pick_ref[part, :] = jnp.where(cell == target, 1.0, 0.0).astype(BF16)
    for group in range(slots // GROUP):
        part = pl.ds(group * GROUP, GROUP)
        weights = weight_rows[part, 0, :]
        weight_ref[part, :] = weights
        scaled = (weights * value_rows[part, 0, :]).astype(BF16)
        high, low = two_terms(weights)
        rows = jnp.concatenate([scaled, high, low, low], axis=0)
        first = jnp.zeros((GROUP, LANES), F32)
        second = jnp.zeros((GROUP, LANES), F32)
        for slot in range(GROUP):
            index = group * GROUP + slot
            if index % CHUNK == 0:
                large[index // CHUNK].wait()
            matrix = matrices_ref[index]
            both = dot(rows, jnp.concatenate([matrix, matrix * matrix], axis=1))
            squares = both[GROUP : 2 * GROUP, LANES:] + both[2 * GROUP : 3 * GROUP, LANES:]
            first = pick_row(first, both[:GROUP, :LANES], slot)
            second = pick_row(second, squares, slot)
        message_ref[part, :] = first
        message_ref[pl.ds(slots + group * GROUP, GROUP), :] = second


def block_kernel(kappa_ref, matrices_ref, weight_ref, shifted_ref, blocks_ref):
    shifted_ref[...] = kappa_ref[...].reshape(shifted_ref.shape) + 4.0
    width = matrices_ref.shape[2]
    for slot in range(matrices_ref.shape[0]):
        matrix = matrices_ref[slot]
        weighted = matrix.T.astype(F32) * weight_ref[pl.ds(slot, 1), :]
        high, low = two_terms(fold_terms(dot(stacked_terms(weighted), matrix)))
        columns = pl.ds(slot % 2 * width, width)
        blocks_ref[slot // 2, pl.ds(0, width), columns] = high
        blocks_ref[slot // 2, pl.ds(width, width), columns] = low


def gather_messages(orbits, slots, message_refs, order_ref):
    orbit = lax.axis_index("orbit")
    for step in range(orbits):
        source = lax.rem(orbit + step, orbits)
        rows = pl.ds(pl.multiple_of(source * slots, slots), slots)
        order_ref[rows, :] = message_refs[step]


def start_kernel(
    orbits, parity, shifted_ref, *refs
):
    message_refs = refs[:orbits]
    field_ref, right_ref, precond_ref, scatter_ref, even_ref, odd_ref, order_ref = refs[orbits:]
    slots = (message_refs[0].shape[0] - GROUP) // 2
    cells = scatter_ref.shape[0]
    targets = message_refs[0][pl.ds(2 * slots, GROUP), :]
    for ref in message_refs[1:]:
        targets = targets + ref[pl.ds(2 * slots, GROUP), :]
    targets = targets.astype(jnp.int32) - 1
    row = lax.broadcasted_iota(jnp.int32, (cells, LANES), 0)
    for piece in range(scatter_ref.shape[1] // LANES):
        hit = row == targets[piece : piece + 1, :]
        scatter_ref[:, pl.ds(piece * LANES, LANES)] = jnp.where(hit, 1.0, 0.0).astype(BF16)
    sums = []
    for part in range(2):
        rows = pl.ds(part * slots, slots)
        gather_messages(orbits, slots, [ref[rows, :] for ref in message_refs], order_ref)
        sums.append(scattered(scatter_ref[...], order_ref[...]))
    right_side, obs_diag = (value.reshape(field_ref.shape) for value in sums)
    shifted = shifted_ref[...]
    precond = PRIOR_WEIGHT * (shifted * shifted + 4.0) + obs_diag
    field = right_side / precond
    right_ref[...] = right_side
    precond_ref[...] = precond
    field_ref[...] = field
    columns = field.shape[0]
    top = jnp.concatenate([field[:2], shifted[:1]], axis=0)
    bottom = jnp.concatenate([field[columns - 2 :], shifted[columns - 1 :]], axis=0)
    store_edges(parity, top, bottom, even_ref, odd_ref)


def scattered(one_hot, slots):
    terms = stacked_terms(slots)
    spare = one_hot.shape[1] - terms.shape[0]
    if spare:
        terms = jnp.concatenate([terms, jnp.zeros((spare, LANES), BF16)], axis=0)
    return dot(one_hot, terms)


def store_edges(parity, top, bottom, even_ref, odd_ref):
    flip = parity()
    used = top.shape[0]
    even_ref[...] = jnp.where(flip, top, bottom)
    odd_ref[:used] = jnp.where(flip, bottom, top)
    if odd_ref.shape[0] > used:
        odd_ref[used:] = jnp.zeros((odd_ref.shape[0] - used,) + top.shape[1:], F32)


def load_edges(parity, even_ref, odd_ref):
    flip = parity()
    even = even_ref[...]
    odd = odd_ref[: even.shape[0]]
    return jnp.where(flip, even, odd), jnp.where(flip, odd, even)


def normal_kernel(pick_ref, field_ref, blocks_ref, edge_ref, out_ref, edge_out_ref):
    edge_out_ref[...] = edge_ref[...]
    width = field_ref.shape[1]
    picked = dot(pick_ref[...], jnp.concatenate(two_terms(field_ref[...]), axis=1))
    picked = picked[:, :width] + picked[:, width:]
    for group in range(picked.shape[0] // GROUP):
        rows = stacked_terms(picked[group * GROUP : (group + 1) * GROUP])
        rows = jnp.concatenate([rows, rows], axis=1)
        total = jnp.zeros((GROUP, width), F32)
        for slot in range(0, GROUP, 2):
            product = fold_terms(dot(rows, blocks_ref[(group * GROUP + slot) // 2]))
            total = pick_row(total, product[:, :width], slot)
            total = pick_row(total, product[:, width:], slot + 1)
        out_ref[pl.ds(group * GROUP, GROUP), :] = total


def extended(field, top, bottom):
    return jnp.concatenate([top, field, bottom], axis=0)


def prior_parts(field, shifted, top, bottom, shifted_top, shifted_bottom):
    first = stencil(
        extended(field, top, bottom), extended(shifted, shifted_top, shifted_bottom)
    )
    return PRIOR_WEIGHT * stencil(first, shifted)


def system(parity, orbits, refs):
    (field_ref, shifted_ref, even_ref, odd_ref, rim_even_ref, rim_odd_ref, scatter_ref) = refs[:7]
    slot_refs = refs[7 : 7 + orbits]
    order_ref = refs[-1]
    slots = slot_refs[0].shape[0]
    gather_messages(orbits, slots, [ref[...] for ref in slot_refs], order_ref)
    normal = scattered(scatter_ref[...], order_ref[...]).reshape(field_ref.shape)
    top, bottom = load_edges(parity, even_ref, odd_ref)
    rim_top, rim_bottom = load_edges(parity, rim_even_ref, rim_odd_ref)
    prior = prior_parts(
        field_ref[...], shifted_ref[...], top[:2], bottom[:2], rim_top[2:], rim_bottom[2:]
    )
    return prior + normal, refs[7 + orbits : -1]


def first_kernel(parity, orbits, *refs):
    image, rest = system(parity, orbits, refs)
    precond_ref, image_ref, next_ref, even_ref, odd_ref = rest
    following = image / precond_ref[...]
    image_ref[...] = image
    next_ref[...] = following
    store_edges(parity, following[:2], following[following.shape[0] - 2 :], even_ref, odd_ref)


def second_kernel(parity, orbits, *refs):
    image, rest = system(parity, orbits, refs)
    start_ref, right_ref, first_ref, image_ref, sums_ref = rest
    field = refs[0][...]
    start, first = start_ref[...], first_ref[...]
    own = jnp.where(lax.axis_index("orbit") == 0, 1.0, 0.0)
    lane = lax.broadcasted_iota(jnp.int32, (1, LANES), 1)
    line = jnp.zeros((1, LANES), F32)
    pairs = ((right_ref[...], start), (start, first), (first, field), (field, image))
    for index, (left, right) in enumerate(pairs):
        by_lane = jnp.sum(jnp.sum(left * right, axis=0), axis=0, keepdims=True)
        value = jnp.sum(by_lane, axis=1, keepdims=True) * own
        line = jnp.where(lane == index, value, line)
    sums_ref[...] = jnp.broadcast_to(line[None], sums_ref.shape)
    image_ref[...] = image


def last_kernel(
    sums_ref, start_ref, next_ref, right_ref, first_ref, second_ref, out_ref, residual_ref
):
    line = jnp.sum(sums_ref[...], axis=0)
    lane = lax.broadcasted_iota(jnp.int32, line.shape, 1)
    product, energy, cross, following = (
        jnp.sum(jnp.where(lane == index, line, 0.0), axis=1, keepdims=True) for index in range(4)
    )
    alpha = product / energy
    later = product - 2.0 * alpha * energy + alpha * alpha * cross
    grown = 1.0 + later / product
    later_energy = (
        grown * grown * energy - 2.0 * alpha * grown * cross + alpha * alpha * following
    )
    later_alpha = later / later_energy
    on_start = alpha + later_alpha * grown
    on_next = -alpha * later_alpha
    out = on_start * start_ref[...] + on_next * next_ref[...]
    residual = right_ref[...] - on_start * first_ref[...] - on_next * second_ref[...]
    out_ref[...] = out.reshape(out_ref.shape)
    residual_ref[...] = residual.reshape(residual_ref.shape)


def per_device(orbits, bands, interp, obs_value, obs_weight, block_map, live_count, kappa2):
    slots, _, observations, width = interp.shape
    columns, latitudes = kappa2.shape
    pieces = latitudes // width
    cells = columns * pieces
    field_shape = (columns, pieces, width)
    paired = bands % 2 == 0

    def parity():
        return lax.rem(lax.axis_index("lon"), 2) == 1 if paired else False

    vmem = pl.BlockSpec(memory_space=pltpu.VMEM)
    anywhere = pl.BlockSpec(memory_space=pl.ANY)

    def call(kernel, outs, in_specs, scratch=(), name=None, limit=VMEM_BYTES, work=0):
        held = pltpu.VMEM if name != "combine" else jax.ShapeDtypeStruct
        cost = pl.CostEstimate(flops=work, bytes_accessed=0, transcendentals=0) if work else None
        return pl.pallas_call(
            kernel,
            out_shape=tuple(held(shape, dtype) for shape, dtype in outs),
            in_specs=in_specs,
            out_specs=tuple(vmem for _ in outs),
            scratch_shapes=list(scratch),
            compiler_params=pltpu.CompilerParams(vmem_limit_bytes=limit),
            cost_estimate=cost,
            name=name,
        )

    def from_others(value):
        return [value] + [
            lax.ppermute(value, "orbit", [((i + step) % orbits, i) for i in range(orbits)])
            for step in range(1, orbits)
        ]

    def from_neighbours(even, odd):
        if paired:
            even_pairs = [(i, i ^ 1) for i in range(bands)]
            odd_pairs = [(i, (i + 1 if i % 2 else i - 1) % bands) for i in range(bands)]
            return lax.ppermute(even, "lon", even_pairs), lax.ppermute(odd, "lon", odd_pairs)
        up = [(i, (i + 1) % bands) for i in range(bands)]
        down = [((i + 1) % bands, i) for i in range(bands)]
        return lax.ppermute(odd, "lon", down), lax.ppermute(even, "lon", up)

    matrices_in = interp.reshape(slots, observations, width)
    line = (slots, 1, observations)
    message, matrices, weights, pick = call(
        functools.partial(data_kernel, orbits),
        (
            ((2 * slots + GROUP, width), F32),
            ((slots, observations, width), BF16),
            ((slots, observations), F32),
            ((slots, cells), BF16),
        ),
        [anywhere] * 5,
        [
            pltpu.SMEM((1,), jnp.int32),
            pltpu.SMEM((slots,), jnp.int32),
            pltpu.VMEM(line, F32),
            pltpu.VMEM(line, F32),
            pltpu.SemaphoreType.DMA((4 + slots // CHUNK,)),
        ],
        "data_terms",
        DATA_VMEM_BYTES,
    )(live_count.reshape(1), block_map.reshape(slots), matrices_in, obs_value, obs_weight)
    messages = from_others(message)
    shifted, blocks = call(
        block_kernel,
        ((field_shape, F32), ((slots // 2, 2 * width, 2 * width), BF16)),
        [vmem] * 3,
        (),
        "blocks",
        work=WORK,
    )(kappa2, matrices, weights)

    order = pltpu.VMEM((orbits * slots, width), F32)
    edge_width = -(-2 * orbits * slots // LANES) * LANES
    rim = ((3, pieces, width), F32)
    edge = ((2, pieces, width), F32)
    wide_edge = ((max(slots // pieces + 1, rim[0][0]), pieces, width), F32)
    field = (field_shape, F32)
    start, right_side, precond, scatter, even, odd = call(
        functools.partial(start_kernel, orbits, parity),
        (field, field, field, ((cells, edge_width), BF16), rim, wide_edge),
        [vmem] * (1 + orbits),
        [order],
        "start",
    )(shifted, *messages)

    def exchanged(value, even, odd, name):
        terms, odd = call(
            normal_kernel,
            (((slots, width), F32), (odd.shape, F32)),
            [vmem] * 4,
            (),
            name,
            work=WORK,
        )(pick, value.reshape(cells, width), blocks, odd)
        return from_others(terms), from_neighbours(even, odd)

    terms, (rim_even, rim_odd) = exchanged(start, even, odd, "normal_start")
    first, following, even, odd = call(
        functools.partial(first_kernel, parity, orbits),
        (field, field, edge, wide_edge),
        [vmem] * (8 + orbits),
        [order],
        "first_image",
    )(start, shifted, rim_even, rim_odd, rim_even, rim_odd, scatter, *terms, precond)

    terms, (even, odd) = exchanged(following, even, odd, "normal_next")
    second, sums = call(
        functools.partial(second_kernel, parity, orbits),
        (field, ((orbits * bands, 1, width), F32)),
        [vmem] * (10 + orbits),
        [order],
        "second_image",
    )(following, shifted, even, odd, rim_even, rim_odd, scatter, *terms, start, right_side, first)
    sums = lax.all_to_all(sums, ("orbit", "lon"), 0, 0, tiled=True)
    return call(
        last_kernel,
        ((kappa2.shape, F32), (kappa2.shape, F32)),
        [vmem] * 6,
        (),
        "combine",
    )(sums, start, following, right_side, first, second)


def solution(mesh):
    in_specs = (
        P("orbit", "lon", None, None),
        P("orbit", "lon", None),
        P("orbit", "lon", None),
        P("orbit", "lon"),
        P("orbit", "lon"),
        P("lon", None),
    )
    out_specs = (P("lon", None), P("lon", None))
    body = functools.partial(per_device, mesh.shape["orbit"], mesh.shape["lon"])
    return jax.shard_map(
        body, mesh=mesh, in_specs=in_specs, out_specs=out_specs, check_vma=False
    )
```

```python
import functools

import jax
import jax.numpy as jnp
from jax import lax
from jax.experimental import pallas as pl
from jax.experimental.pallas import tpu as pltpu
from jax.sharding import PartitionSpec as P

PRIOR_WEIGHT = 0.0625
GROUP = 8
LANES = 128
F32 = jnp.float32
BF16 = jnp.bfloat16
VMEM_BYTES = 48 * 1024 * 1024
DATA_VMEM_BYTES = 59 * 1024 * 1024
CHUNK = 16
WORK = 1 << 32


def two_terms(value):
    high = value.astype(BF16)
    low = (value - high.astype(F32)).astype(BF16)
    return high, low


def stacked_terms(value):
    return jnp.concatenate(two_terms(value), axis=0)


def fold_terms(product):
    half = product.shape[0] // 2
    return product[:half] + product[half:]


def dot(left, right):
    return lax.dot_general(left, right, (((1,), (0,)), ((), ())), preferred_element_type=F32)


def dot_transposed(left, right):
    return lax.dot_general(left, right, (((1,), (1,)), ((), ())), preferred_element_type=F32)


def pick_row(total, product, slot):
    rows = lax.broadcasted_iota(jnp.int32, product.shape, 0)
    return jnp.where(rows == slot, product, total)


def lat_pair(field):
    pieces = field.shape[1]
    piece = lax.broadcasted_iota(jnp.int32, field.shape, 1)
    lane = lax.broadcasted_iota(jnp.int32, field.shape, 2)
    south = pltpu.roll(field, 1, 2)
    north = pltpu.roll(field, LANES - 1, 2)
    south_over = jnp.where(piece == 0, 0.0, pltpu.roll(south, 1, 1))
    north_over = jnp.where(piece == pieces - 1, 0.0, pltpu.roll(north, pieces - 1, 1))
    return jnp.where(lane == 0, south_over, south) + jnp.where(lane == LANES - 1, north_over, north)


def stencil(field, shifted):
    center = field[1:-1]
    return shifted * center - field[2:] - field[:-2] - lat_pair(center)


def data_kernel(
    orbits,
    count_in,
    map_in,
    interp_in,
    value_in,
    weight_in,
    message_ref,
    matrices_ref,
    weight_ref,
    pick_ref,
    count_ref,
    map_ref,
    value_rows,
    weight_rows,
    sems,
):
    slots = matrices_ref.shape[0]
    pairs = ((weight_in, weight_rows), (value_in, value_rows), (map_in, map_ref), (count_in, count_ref))
    small = [
        pltpu.make_async_copy(source, target, sems.at[index])
        for index, (source, target) in enumerate(pairs)
    ]
    large = []
    for index in range(slots // CHUNK):
        part = pl.ds(index * CHUNK, CHUNK)
        large.append(
            pltpu.make_async_copy(
                interp_in.at[part], matrices_ref.at[part], sems.at[len(small) + index]
            )
        )
    for copy in small + large:
        copy.start()
    for copy in small:
        copy.wait()
    orbit = lax.axis_index("orbit")
    total = orbits * slots
    place = lax.broadcasted_iota(jnp.int32, (GROUP, LANES), 0) * LANES
    place = place + lax.broadcasted_iota(jnp.int32, (GROUP, LANES), 1)
    slot_here = jnp.where(place >= total, place - total, place) - orbit * slots
    target_row = jnp.zeros((GROUP, LANES), jnp.int32)
    count = count_ref[0, 0]
    for slot in range(slots):
        live_target = jnp.where(slot < count, map_ref[slot] + 1, 0)
        target_row = jnp.where(slot_here == slot, live_target, target_row)
    target_row = jnp.where(place < 2 * total, target_row, 0)
    message_ref[pl.ds(2 * slots, GROUP), :] = target_row.astype(F32)
    row = lax.broadcasted_iota(jnp.int32, (GROUP, pick_ref.shape[1]), 0)
    cell = lax.broadcasted_iota(jnp.int32, row.shape, 1)
    for group in range(slots // GROUP):
        target = jnp.zeros(row.shape, jnp.int32)
        for slot in range(GROUP):
            index = group * GROUP + slot
            live_target = jnp.where(index < count, map_ref[index], -1)
            target = jnp.where(row == slot, live_target, target)
        part = pl.ds(group * GROUP, GROUP)
        pick_ref[part, :] = jnp.where(cell == target, 1.0, 0.0).astype(BF16)
    for group in range(slots // GROUP):
        part = pl.ds(group * GROUP, GROUP)
        weights = weight_rows[part, 0, :]
        weight_ref[part, :] = weights
        scaled = (weights * value_rows[part, 0, :]).astype(BF16)
        high, low = two_terms(weights)
        rows = jnp.concatenate([scaled, high, low, low], axis=0)
        first = jnp.zeros((GROUP, LANES), F32)
        second = jnp.zeros((GROUP, LANES), F32)
        for slot in range(GROUP):
            index = group * GROUP + slot
            if index % CHUNK == 0:
                large[index // CHUNK].wait()
            matrix = matrices_ref[index]
            both = dot(rows, jnp.concatenate([matrix, matrix * matrix], axis=1))
            squares = both[GROUP : 2 * GROUP, LANES:] + both[2 * GROUP : 3 * GROUP, LANES:]
            first = pick_row(first, both[:GROUP, :LANES], slot)
            second = pick_row(second, squares, slot)
        message_ref[part, :] = first
        message_ref[pl.ds(slots + group * GROUP, GROUP), :] = second


def block_kernel(kappa_ref, matrices_ref, weight_ref, shifted_ref, blocks_ref):
    shifted_ref[...] = kappa_ref[...].reshape(shifted_ref.shape) + 4.0
    width = matrices_ref.shape[2]
    for slot in range(matrices_ref.shape[0]):
        matrix = matrices_ref[slot]
        weighted = matrix.T.astype(F32) * weight_ref[pl.ds(slot, 1), :]
        high, low = two_terms(fold_terms(dot(stacked_terms(weighted), matrix)))
        columns = pl.ds(slot % 2 * width, width)
        blocks_ref[slot // 2, pl.ds(0, width), columns] = high
        blocks_ref[slot // 2, pl.ds(width, width), columns] = low


def gather_messages(orbits, slots, message_refs, order_ref):
    orbit = lax.axis_index("orbit")
    for step in range(orbits):
        source = lax.rem(orbit + step, orbits)
        rows = pl.ds(pl.multiple_of(source * slots, slots), slots)
        order_ref[rows, :] = message_refs[step]


def start_kernel(
    orbits, parity, shifted_ref, pick_ref, blocks_ref, *refs
):
    message_refs = refs[:orbits]
    (
        field_ref,
        right_ref,
        precond_ref,
        scatter_ref,
        even_ref,
        odd_ref,
        out_ref,
        order_ref,
    ) = refs[orbits:]
    slots = (message_refs[0].shape[0] - GROUP) // 2
    cells = scatter_ref.shape[0]
    targets = message_refs[0][pl.ds(2 * slots, GROUP), :]
    for ref in message_refs[1:]:
        targets = targets + ref[pl.ds(2 * slots, GROUP), :]
    targets = targets.astype(jnp.int32) - 1
    row = lax.broadcasted_iota(jnp.int32, (cells, LANES), 0)
    for piece in range(scatter_ref.shape[1] // LANES):
        hit = row == targets[piece : piece + 1, :]
        scatter_ref[:, pl.ds(piece * LANES, LANES)] = jnp.where(hit, 1.0, 0.0).astype(BF16)
    sums = []
    for part in range(2):
        rows = pl.ds(part * slots, slots)
        gather_messages(orbits, slots, [ref[rows, :] for ref in message_refs], order_ref)
        sums.append(scattered(scatter_ref[...], order_ref[...]))
    right_side, obs_diag = (value.reshape(field_ref.shape) for value in sums)
    shifted = shifted_ref[...]
    precond = PRIOR_WEIGHT * (shifted * shifted + 4.0) + obs_diag
    field = right_side / precond
    right_ref[...] = right_side
    precond_ref[...] = precond
    field_ref[...] = field
    columns = field.shape[0]
    top = jnp.concatenate([field[:2], shifted[:1]], axis=0)
    bottom = jnp.concatenate([field[columns - 2 :], shifted[columns - 1 :]], axis=0)
    store_edges(parity, top, bottom, even_ref, odd_ref)
    normal_slots(pick_ref, field, blocks_ref, out_ref)


def scattered(one_hot, slots):
    terms = stacked_terms(slots)
    spare = one_hot.shape[1] - terms.shape[0]
    if spare:
        terms = jnp.concatenate([terms, jnp.zeros((spare, LANES), BF16)], axis=0)
    return dot(one_hot, terms)


def store_edges(parity, top, bottom, even_ref, odd_ref):
    flip = parity()
    used = top.shape[0]
    even_ref[...] = jnp.where(flip, top, bottom)
    odd_ref[:used] = jnp.where(flip, bottom, top)
    if odd_ref.shape[0] > used:
        odd_ref[used:] = jnp.zeros((odd_ref.shape[0] - used,) + top.shape[1:], F32)


def load_edges(parity, even_ref, odd_ref):
    flip = parity()
    even = even_ref[...]
    odd = odd_ref[: even.shape[0]]
    return jnp.where(flip, even, odd), jnp.where(flip, odd, even)


def normal_slots(pick_ref, field, blocks_ref, out_ref):
    width = field.shape[-1]
    field = field.reshape(pick_ref.shape[1], width)
    picked = dot(pick_ref[...], jnp.concatenate(two_terms(field), axis=1))
    picked = picked[:, :width] + picked[:, width:]
    energy = jnp.zeros((GROUP, width), F32)
    for group in range(picked.shape[0] // GROUP):
        cells = picked[group * GROUP : (group + 1) * GROUP]
        rows = stacked_terms(cells)
        rows = jnp.concatenate([rows, rows], axis=1)
        total = jnp.zeros((GROUP, width), F32)
        for slot in range(0, GROUP, 2):
            product = fold_terms(dot(rows, blocks_ref[(group * GROUP + slot) // 2]))
            total = pick_row(total, product[:, :width], slot)
            total = pick_row(total, product[:, width:], slot + 1)
        out_ref[pl.ds(group * GROUP, GROUP), :] = total
        energy = energy + cells * total
    return energy


def extended(field, top, bottom):
    return jnp.concatenate([top, field, bottom], axis=0)


def prior_parts(field, shifted, top, bottom, shifted_top, shifted_bottom):
    first = stencil(
        extended(field, top, bottom), extended(shifted, shifted_top, shifted_bottom)
    )
    return PRIOR_WEIGHT * stencil(first, shifted)


def scattered_slots(orbits, scatter_ref, slot_refs, order_ref):
    slots = slot_refs[0].shape[0]
    gather_messages(orbits, slots, [ref[...] for ref in slot_refs], order_ref)
    return scattered(scatter_ref[...], order_ref[...])


def first_kernel(
    parity,
    orbits,
    field_ref,
    shifted_ref,
    even_ref,
    odd_ref,
    scatter_ref,
    precond_ref,
    *refs,
):
    slot_refs = refs[:orbits]
    image_ref, next_ref, edge_ref, order_ref = refs[orbits:]
    normal = scattered_slots(orbits, scatter_ref, slot_refs, order_ref)
    top, bottom = load_edges(parity, even_ref, odd_ref)
    prior = prior_parts(
        field_ref[...], shifted_ref[...], top[:2], bottom[:2], top[2:], bottom[2:]
    )
    image = prior + normal.reshape(field_ref.shape)
    following = image / precond_ref[...]
    image_ref[...] = image
    next_ref[...] = following
    edge_ref[...] = jnp.where(parity(), following[:2], following[following.shape[0] - 2 :])


def alone(field, shifted):
    zero = jnp.zeros((1,) + field.shape[1:], F32)
    return stencil(extended(field, zero, zero), shifted)


def inner_kernel(
    field_ref,
    shifted_ref,
    start_ref,
    right_ref,
    first_ref,
    pick_ref,
    blocks_ref,
    base_ref,
    ends_ref,
    parts_ref,
    out_ref,
):
    field, shifted = field_ref[...], shifted_ref[...]
    energy = normal_slots(pick_ref, field, blocks_ref, out_ref)
    start, first = start_ref[...], first_ref[...]
    once = alone(field, shifted)
    base_ref[...] = PRIOR_WEIGHT * alone(once, shifted)
    ends_ref[0] = once[0]
    ends_ref[1] = once[once.shape[0] - 1]
    own = jnp.where(lax.axis_index("orbit") == 0, 1.0, 0.0)
    parts_ref[0] = own * jnp.sum(right_ref[...] * start, axis=0)
    parts_ref[1] = own * jnp.sum(start * first, axis=0)
    parts_ref[2] = own * jnp.sum(first * field, axis=0)
    parts_ref[3] = own * PRIOR_WEIGHT * jnp.sum(once * once, axis=0) + energy


def sides(parity, top, bottom):
    flip = parity()
    return jnp.where(flip, top, bottom), jnp.where(flip, bottom, top)


def near_far(parity, even_ref):
    flip = parity()
    return jnp.where(flip, even_ref[1], even_ref[0]), jnp.where(flip, even_ref[0], even_ref[1])


def edge_kernel(parity, field_ref, even_ref, ends_ref, parts_ref, message_ref):
    columns = field_ref.shape[0]
    near, _ = near_far(parity, even_ref)
    even_end, odd_end = sides(parity, ends_ref[0], ends_ref[1])
    _, odd_field = sides(parity, field_ref[0], field_ref[columns - 1])
    orbit = lax.axis_index("orbit")
    own = jnp.where(orbit == 0, PRIOR_WEIGHT, 0.0)
    more = own * (near * (near - 2.0 * even_end) + odd_field * odd_field)
    sums = [jnp.sum(parts_ref[index], axis=0, keepdims=True) for index in range(3)]
    sums.append(jnp.sum(parts_ref[3] + more, axis=0, keepdims=True))
    sums = jnp.sum(jnp.concatenate(sums, axis=0), axis=1, keepdims=True)
    lane = lax.broadcasted_iota(jnp.int32, (4, LANES), 1)
    index = lax.broadcasted_iota(jnp.int32, (4, LANES), 0)
    line = jnp.sum(jnp.where(lane == index, sums, 0.0), axis=0, keepdims=True)
    row = jnp.concatenate([jnp.where(orbit == 0, odd_end, odd_field), line], axis=0)
    several = jnp.concatenate([row] * GROUP, axis=0)
    for index in range(message_ref.shape[0] // several.shape[0]):
        message_ref[pl.ds(index * several.shape[0], several.shape[0]), :] = several


def last_kernel(
    parity,
    orbits,
    bands,
    received_ref,
    start_ref,
    next_ref,
    right_ref,
    first_ref,
    base_ref,
    shifted_ref,
    even_ref,
    rim_ref,
    scatter_ref,
    *refs,
):
    slot_refs = refs[:orbits]
    out_ref, residual_ref, order_ref, second_ref = refs[orbits:]
    columns, pieces, _ = start_ref.shape
    rows = pieces + 1

    def end_of(band):
        return received_ref[pl.ds(band * rows, pieces), :]

    def field_of(band):
        return received_ref[pl.ds((bands + band) * rows, pieces), :]

    open_sides = jnp.zeros((pieces, LANES), F32)
    for band in range(1, bands, 2):
        above = (band + 1) % bands
        open_sides = open_sides + end_of(band) * field_of(above) + end_of(above) * field_of(band)
    open_sides = jnp.sum(jnp.sum(open_sides, axis=0, keepdims=True), axis=1, keepdims=True)
    lines = received_ref[pl.ds(pieces, orbits * bands, stride=rows), :]
    line = jnp.sum(lines, axis=0, keepdims=True)
    lane = lax.broadcasted_iota(jnp.int32, line.shape, 1)
    product, energy, cross, following = (
        jnp.sum(jnp.where(lane == index, line, 0.0), axis=1, keepdims=True) for index in range(4)
    )
    following = following - (2.0 * PRIOR_WEIGHT) * open_sides
    alpha = product / energy
    later = product - 2.0 * alpha * energy + alpha * alpha * cross
    grown = 1.0 + later / product
    later_energy = (
        grown * grown * energy - 2.0 * alpha * grown * cross + alpha * alpha * following
    )
    later_alpha = later / later_energy
    on_start = alpha + later_alpha * grown
    on_next = -alpha * later_alpha

    normal = scattered_slots(orbits, scatter_ref, slot_refs, order_ref)
    second_ref[...] = base_ref[...] + normal.reshape(second_ref.shape)
    flip = parity()
    band = lax.axis_index("lon")
    across = lax.rem(band + jnp.where(flip, 1, bands - 1), bands)
    even_field, odd_field = sides(parity, next_ref[0], next_ref[columns - 1])
    near, far = near_far(parity, even_ref)
    even_first = rim_ref[2] * near - far - even_field - lat_pair(near[None])[0]
    odd_near = field_of(across)
    odd_first = end_of(across) - odd_field
    ends = (
        (0, 1, jnp.where(flip, near, odd_near), jnp.where(flip, even_first, odd_first)),
        (
            columns - 1,
            columns - 2,
            jnp.where(flip, odd_near, near),
            jnp.where(flip, odd_first, even_first),
        ),
    )
    for end, inner, field, first in ends:
        change = lat_pair(field[None])[0] - shifted_ref[end] * field - first
        second_ref[end] = second_ref[end] + PRIOR_WEIGHT * change
        second_ref[inner] = second_ref[inner] + PRIOR_WEIGHT * field

    out = on_start * start_ref[...] + on_next * next_ref[...]
    residual = right_ref[...] - on_start * first_ref[...] - on_next * second_ref[...]
    out_ref[...] = out.reshape(out_ref.shape)
    residual_ref[...] = residual.reshape(residual_ref.shape)


def per_device(orbits, bands, interp, obs_value, obs_weight, block_map, live_count, kappa2):
    slots, _, observations, width = interp.shape
    columns, latitudes = kappa2.shape
    pieces = latitudes // width
    cells = columns * pieces
    field_shape = (columns, pieces, width)

    def parity():
        return lax.rem(lax.axis_index("lon"), 2) == 1

    vmem = pl.BlockSpec(memory_space=pltpu.VMEM)
    anywhere = pl.BlockSpec(memory_space=pl.ANY)

    def call(kernel, outs, in_specs, scratch=(), name=None, limit=VMEM_BYTES, work=0):
        held = pltpu.VMEM if name != "combine" else jax.ShapeDtypeStruct
        cost = pl.CostEstimate(flops=work, bytes_accessed=0, transcendentals=0) if work else None
        return pl.pallas_call(
            kernel,
            out_shape=tuple(held(shape, dtype) for shape, dtype in outs),
            in_specs=in_specs,
            out_specs=tuple(vmem for _ in outs),
            scratch_shapes=list(scratch),
            compiler_params=pltpu.CompilerParams(vmem_limit_bytes=limit),
            cost_estimate=cost,
            name=name,
        )

    def from_others(value):
        return [value] + [
            lax.ppermute(value, "orbit", [((i + step) % orbits, i) for i in range(orbits)])
            for step in range(1, orbits)
        ]

    even_pairs = [(i, i ^ 1) for i in range(bands)]
    odd_pairs = [(i, (i + 1 if i % 2 else i - 1) % bands) for i in range(bands)]

    matrices_in = interp.reshape(slots, observations, width)
    line = (slots, 1, observations)
    message, matrices, weights, pick = call(
        functools.partial(data_kernel, orbits),
        (
            ((2 * slots + GROUP, width), F32),
            ((slots, observations, width), BF16),
            ((slots, observations), F32),
            ((slots, cells), BF16),
        ),
        [anywhere] * 5,
        [
            pltpu.SMEM((1, 1), jnp.int32),
            pltpu.SMEM((slots,), jnp.int32),
            pltpu.VMEM(line, F32),
            pltpu.VMEM(line, F32),
            pltpu.SemaphoreType.DMA((4 + slots // CHUNK,)),
        ],
        "data_terms",
        DATA_VMEM_BYTES,
    )(live_count, block_map.reshape(slots), matrices_in, obs_value, obs_weight)
    messages = from_others(message)
    shifted, blocks = call(
        block_kernel,
        ((field_shape, F32), ((slots // 2, 2 * width, 2 * width), BF16)),
        [vmem] * 3,
        (),
        "blocks",
        work=WORK,
    )(kappa2, matrices, weights)

    order = pltpu.VMEM((orbits * slots, width), F32)
    edge_width = -(-2 * orbits * slots // LANES) * LANES
    rim = ((3, pieces, width), F32)
    edge = ((2, pieces, width), F32)
    wide_edge = ((max(slots // pieces + 1, rim[0][0]), pieces, width), F32)
    field = (field_shape, F32)
    slot_terms = ((slots, width), F32)
    start, right_side, precond, scatter, even, odd, terms = call(
        functools.partial(start_kernel, orbits, parity),
        (field, field, field, ((cells, edge_width), BF16), rim, wide_edge, slot_terms),
        [vmem] * (3 + orbits),
        [order],
        "start",
    )(shifted, pick, blocks, *messages)
    rim_odd = lax.ppermute(odd, "lon", odd_pairs)
    terms = from_others(terms)
    rim_even = lax.ppermute(even, "lon", even_pairs)
    first, following, even = call(
        functools.partial(first_kernel, parity, orbits),
        (field, field, edge),
        [vmem] * (6 + orbits),
        [order],
        "first_image",
    )(start, shifted, rim_even, rim_odd, scatter, precond, *terms)

    even = lax.ppermute(even, "lon", even_pairs)
    base, ends, parts, terms = call(
        inner_kernel,
        (field, edge, ((4, pieces, width), F32), slot_terms),
        [vmem] * 7,
        (),
        "inner_image",
        work=WORK,
    )(following, shifted, start, right_side, first, pick, blocks)
    terms = from_others(terms)
    message = ((orbits * bands * (pieces + 1), width), F32)
    (sums,) = call(
        functools.partial(edge_kernel, parity), (message,), [vmem] * 4, (), "edge_sums"
    )(following, even, ends, parts)
    sums = lax.all_to_all(sums[:, None], ("orbit", "lon"), 0, 0, tiled=True)[:, 0]
    return call(
        functools.partial(last_kernel, parity, orbits, bands),
        ((kappa2.shape, F32), (kappa2.shape, F32)),
        [vmem] * (10 + orbits),
        [order, pltpu.VMEM(field_shape, F32)],
        "combine",
    )(
        sums, start, following, right_side, first, base, shifted, even, rim_even, scatter, *terms
    )


def solution(mesh):
    in_specs = (
        P("orbit", "lon", None, None),
        P("orbit", "lon", None),
        P("orbit", "lon", None),
        P("orbit", "lon"),
        P("orbit", "lon"),
        P("lon", None),
    )
    out_specs = (P("lon", None), P("lon", None))
    body = functools.partial(per_device, mesh.shape["orbit"], mesh.shape["lon"])
    return jax.shard_map(
        body, mesh=mesh, in_specs=in_specs, out_specs=out_specs, check_vma=False
    )
```

```python
import functools

import jax
import jax.numpy as jnp
from jax import lax
from jax.experimental import pallas as pl
from jax.experimental.pallas import tpu as pltpu
from jax.sharding import PartitionSpec as P

PRIOR_WEIGHT = 0.0625
GROUP = 8
LANES = 128
F32 = jnp.float32
BF16 = jnp.bfloat16
VMEM_BYTES = 48 * 1024 * 1024
DATA_VMEM_BYTES = 59 * 1024 * 1024
CHUNK = 8
WORK = 1 << 32


def two_terms(value):
    high = value.astype(BF16)
    low = (value - high.astype(F32)).astype(BF16)
    return high, low


def stacked_terms(value):
    return jnp.concatenate(two_terms(value), axis=0)


def fold_terms(product):
    half = product.shape[0] // 2
    return product[:half] + product[half:]


def dot(left, right):
    return lax.dot_general(left, right, (((1,), (0,)), ((), ())), preferred_element_type=F32)


def dot_transposed(left, right):
    return lax.dot_general(left, right, (((1,), (1,)), ((), ())), preferred_element_type=F32)


def pick_row(total, product, slot):
    rows = lax.broadcasted_iota(jnp.int32, product.shape, 0)
    return jnp.where(rows == slot, product, total)


def lat_pair(field):
    pieces = field.shape[1]
    piece = lax.broadcasted_iota(jnp.int32, field.shape, 1)
    lane = lax.broadcasted_iota(jnp.int32, field.shape, 2)
    south = pltpu.roll(field, 1, 2)
    north = pltpu.roll(field, LANES - 1, 2)
    south_over = jnp.where(piece == 0, 0.0, pltpu.roll(south, 1, 1))
    north_over = jnp.where(piece == pieces - 1, 0.0, pltpu.roll(north, pieces - 1, 1))
    return jnp.where(lane == 0, south_over, south) + jnp.where(lane == LANES - 1, north_over, north)


def stencil(field, shifted):
    center = field[1:-1]
    return shifted * center - field[2:] - field[:-2] - lat_pair(center)


def data_kernel(
    orbits,
    count_ref,
    map_in,
    interp_in,
    value_in,
    weight_in,
    message_ref,
    matrices_ref,
    weight_ref,
    pick_ref,
    map_ref,
    value_rows,
    weight_rows,
    sems,
):
    slots = matrices_ref.shape[0]
    pairs = ((weight_in, weight_rows), (value_in, value_rows), (map_in, map_ref))
    small = [
        pltpu.make_async_copy(source, target, sems.at[index])
        for index, (source, target) in enumerate(pairs)
    ]
    large = []
    for index in range(slots // CHUNK):
        part = pl.ds(index * CHUNK, CHUNK)
        large.append(
            pltpu.make_async_copy(
                interp_in.at[part], matrices_ref.at[part], sems.at[len(small) + index]
            )
        )
    count = count_ref[0, 0]
    for copy in small:
        copy.start()
    for index, copy in enumerate(large):
        pl.when(index * CHUNK < count)(copy.start)
    for copy in small:
        copy.wait()
    orbit = lax.axis_index("orbit")
    total = orbits * slots
    place = lax.broadcasted_iota(jnp.int32, (GROUP, LANES), 0) * LANES
    place = place + lax.broadcasted_iota(jnp.int32, (GROUP, LANES), 1)
    slot_here = jnp.where(place >= total, place - total, place) - orbit * slots
    target_row = jnp.zeros((GROUP, LANES), jnp.int32)
    for slot in range(slots):
        live_target = jnp.where(slot < count, map_ref[slot] + 1, 0)
        target_row = jnp.where(slot_here == slot, live_target, target_row)
    target_row = jnp.where(place < 2 * total, target_row, 0)
    message_ref[pl.ds(2 * slots, GROUP), :] = target_row.astype(F32)
    row = lax.broadcasted_iota(jnp.int32, (GROUP, pick_ref.shape[1]), 0)
    cell = lax.broadcasted_iota(jnp.int32, row.shape, 1)
    for group in range(slots // GROUP):
        target = jnp.zeros(row.shape, jnp.int32)
        for slot in range(GROUP):
            index = group * GROUP + slot
            live_target = jnp.where(index < count, map_ref[index], -1)
            target = jnp.where(row == slot, live_target, target)
        part = pl.ds(group * GROUP, GROUP)
        pick_ref[part, :] = jnp.where(cell == target, 1.0, 0.0).astype(BF16)
    weight_ref[...] = weight_rows[:, 0, :]

    def work(index):
        large[index].wait()
        for group in range(index * CHUNK // GROUP, (index + 1) * CHUNK // GROUP):
            part = pl.ds(group * GROUP, GROUP)
            weights = weight_rows[part, 0, :]
            scaled = (weights * value_rows[part, 0, :]).astype(BF16)
            high, low = two_terms(weights)
            rows = jnp.concatenate([scaled, high, low, low], axis=0)
            first = jnp.zeros((GROUP, LANES), F32)
            second = jnp.zeros((GROUP, LANES), F32)
            for slot in range(GROUP):
                matrix = matrices_ref[group * GROUP + slot]
                both = dot(rows, jnp.concatenate([matrix, matrix * matrix], axis=1))
                squares = both[GROUP : 2 * GROUP, LANES:] + both[2 * GROUP : 3 * GROUP, LANES:]
                first = pick_row(first, both[:GROUP, :LANES], slot)
                second = pick_row(second, squares, slot)
            message_ref[part, :] = first
            message_ref[pl.ds(slots + group * GROUP, GROUP), :] = second

    def rest(index):
        part = pl.ds(index * CHUNK, CHUNK)
        matrices_ref[part] = jnp.zeros((CHUNK,) + matrices_ref.shape[1:], BF16)
        for start in (0, slots):
            part = pl.ds(start + index * CHUNK, CHUNK)
            message_ref[part, :] = jnp.zeros((CHUNK, LANES), F32)

    chunks = range(slots // CHUNK)
    for index in chunks:
        pl.when(index * CHUNK >= count)(functools.partial(rest, index))
    for index in chunks:
        pl.when(index * CHUNK < count)(functools.partial(work, index))


def block_kernel(kappa_ref, matrices_ref, weight_ref, shifted_ref, blocks_ref):
    shifted_ref[...] = kappa_ref[...].reshape(shifted_ref.shape) + 4.0
    width = matrices_ref.shape[2]
    for slot in range(matrices_ref.shape[0]):
        matrix = matrices_ref[slot]
        weighted = matrix.T.astype(F32) * weight_ref[pl.ds(slot, 1), :]
        high, low = two_terms(fold_terms(dot(stacked_terms(weighted), matrix)))
        columns = pl.ds(slot % 2 * width, width)
        blocks_ref[slot // 2, pl.ds(0, width), columns] = high
        blocks_ref[slot // 2, pl.ds(width, width), columns] = low


def gather_messages(orbits, slots, message_refs, order_ref):
    orbit = lax.axis_index("orbit")
    for step in range(orbits):
        source = lax.rem(orbit + step, orbits)
        rows = pl.ds(pl.multiple_of(source * slots, slots), slots)
        order_ref[rows, :] = message_refs[step]


def start_kernel(
    orbits, parity, shifted_ref, *refs
):
    message_refs = refs[:orbits]
    (
        field_ref,
        right_ref,
        precond_ref,
        scatter_ref,
        even_ref,
        odd_ref,
        order_ref,
    ) = refs[orbits:]
    slots = (message_refs[0].shape[0] - GROUP) // 2
    cells = scatter_ref.shape[0]
    targets = message_refs[0][pl.ds(2 * slots, GROUP), :]
    for ref in message_refs[1:]:
        targets = targets + ref[pl.ds(2 * slots, GROUP), :]
    targets = targets.astype(jnp.int32) - 1
    row = lax.broadcasted_iota(jnp.int32, (cells, LANES), 0)
    for piece in range(scatter_ref.shape[1] // LANES):
        hit = row == targets[piece : piece + 1, :]
        scatter_ref[:, pl.ds(piece * LANES, LANES)] = jnp.where(hit, 1.0, 0.0).astype(BF16)
    sums = []
    for part in range(2):
        rows = pl.ds(part * slots, slots)
        gather_messages(orbits, slots, [ref[rows, :] for ref in message_refs], order_ref)
        sums.append(scattered(scatter_ref[...], order_ref[...]))
    right_side, obs_diag = (value.reshape(field_ref.shape) for value in sums)
    shifted = shifted_ref[...]
    precond = PRIOR_WEIGHT * (shifted * shifted + 4.0) + obs_diag
    field = right_side / precond
    right_ref[...] = right_side
    precond_ref[...] = precond
    field_ref[...] = field
    columns = field.shape[0]
    top = jnp.concatenate([field[:2], shifted[:1]], axis=0)
    bottom = jnp.concatenate([field[columns - 2 :], shifted[columns - 1 :]], axis=0)
    store_edges(parity, top, bottom, even_ref, odd_ref)


def normal_kernel(pick_ref, field_ref, blocks_ref, even_ref, out_ref, even_out_ref):
    normal_slots(pick_ref, field_ref[...], blocks_ref, out_ref)
    even_out_ref[...] = even_ref[...]


def scattered(one_hot, slots):
    terms = stacked_terms(slots)
    spare = one_hot.shape[1] - terms.shape[0]
    if spare:
        terms = jnp.concatenate([terms, jnp.zeros((spare, LANES), BF16)], axis=0)
    return dot(one_hot, terms)


def store_edges(parity, top, bottom, even_ref, odd_ref):
    flip = parity()
    used = top.shape[0]
    even_ref[...] = jnp.where(flip, top, bottom)
    odd_ref[:used] = jnp.where(flip, bottom, top)
    if odd_ref.shape[0] > used:
        odd_ref[used:] = jnp.zeros((odd_ref.shape[0] - used,) + top.shape[1:], F32)


def load_edges(parity, even_ref, odd_ref):
    flip = parity()
    even = even_ref[...]
    odd = odd_ref[: even.shape[0]]
    return jnp.where(flip, even, odd), jnp.where(flip, odd, even)


def normal_slots(pick_ref, field, blocks_ref, out_ref):
    width = field.shape[-1]
    field = field.reshape(pick_ref.shape[1], width)
    picked = dot(pick_ref[...], jnp.concatenate(two_terms(field), axis=1))
    picked = picked[:, :width] + picked[:, width:]
    energy = jnp.zeros((GROUP, width), F32)
    for group in range(picked.shape[0] // GROUP):
        cells = picked[group * GROUP : (group + 1) * GROUP]
        rows = stacked_terms(cells)
        rows = jnp.concatenate([rows, rows], axis=1)
        total = jnp.zeros((GROUP, width), F32)
        for slot in range(0, GROUP, 2):
            product = fold_terms(dot(rows, blocks_ref[(group * GROUP + slot) // 2]))
            total = pick_row(total, product[:, :width], slot)
            total = pick_row(total, product[:, width:], slot + 1)
        out_ref[pl.ds(group * GROUP, GROUP), :] = total
        energy = energy + cells * total
    return energy


def extended(field, top, bottom):
    return jnp.concatenate([top, field, bottom], axis=0)


def prior_parts(field, shifted, top, bottom, shifted_top, shifted_bottom):
    first = stencil(
        extended(field, top, bottom), extended(shifted, shifted_top, shifted_bottom)
    )
    return PRIOR_WEIGHT * stencil(first, shifted)


def scattered_slots(orbits, scatter_ref, slot_refs, order_ref):
    slots = slot_refs[0].shape[0]
    gather_messages(orbits, slots, [ref[...] for ref in slot_refs], order_ref)
    return scattered(scatter_ref[...], order_ref[...])


def first_kernel(
    parity,
    orbits,
    field_ref,
    shifted_ref,
    even_ref,
    odd_ref,
    scatter_ref,
    precond_ref,
    *refs,
):
    slot_refs = refs[:orbits]
    image_ref, next_ref, edge_ref, order_ref = refs[orbits:]
    normal = scattered_slots(orbits, scatter_ref, slot_refs, order_ref)
    top, bottom = load_edges(parity, even_ref, odd_ref)
    prior = prior_parts(
        field_ref[...], shifted_ref[...], top[:2], bottom[:2], top[2:], bottom[2:]
    )
    image = prior + normal.reshape(field_ref.shape)
    following = image / precond_ref[...]
    image_ref[...] = image
    next_ref[...] = following
    edge_ref[...] = jnp.where(parity(), following[:2], following[following.shape[0] - 2 :])


def alone(field, shifted):
    zero = jnp.zeros((1,) + field.shape[1:], F32)
    return stencil(extended(field, zero, zero), shifted)


def inner_kernel(
    field_ref,
    shifted_ref,
    start_ref,
    right_ref,
    first_ref,
    pick_ref,
    blocks_ref,
    base_ref,
    ends_ref,
    parts_ref,
    out_ref,
):
    field, shifted = field_ref[...], shifted_ref[...]
    energy = normal_slots(pick_ref, field, blocks_ref, out_ref)
    start, first = start_ref[...], first_ref[...]
    once = alone(field, shifted)
    base_ref[...] = PRIOR_WEIGHT * alone(once, shifted)
    ends_ref[0] = once[0]
    ends_ref[1] = once[once.shape[0] - 1]
    own = jnp.where(lax.axis_index("orbit") == 0, 1.0, 0.0)
    parts_ref[0] = own * jnp.sum(right_ref[...] * start, axis=0)
    parts_ref[1] = own * jnp.sum(start * first, axis=0)
    parts_ref[2] = own * jnp.sum(first * field, axis=0)
    parts_ref[3] = own * PRIOR_WEIGHT * jnp.sum(once * once, axis=0) + energy


def sides(parity, top, bottom):
    flip = parity()
    return jnp.where(flip, top, bottom), jnp.where(flip, bottom, top)


def near_far(parity, even_ref):
    flip = parity()
    return jnp.where(flip, even_ref[1], even_ref[0]), jnp.where(flip, even_ref[0], even_ref[1])


def edge_kernel(parity, field_ref, even_ref, ends_ref, parts_ref, message_ref):
    columns = field_ref.shape[0]
    near, _ = near_far(parity, even_ref)
    even_end, odd_end = sides(parity, ends_ref[0], ends_ref[1])
    _, odd_field = sides(parity, field_ref[0], field_ref[columns - 1])
    orbit = lax.axis_index("orbit")
    own = jnp.where(orbit == 0, PRIOR_WEIGHT, 0.0)
    more = own * (near * (near - 2.0 * even_end) + odd_field * odd_field)
    sums = [jnp.sum(parts_ref[index], axis=0, keepdims=True) for index in range(3)]
    sums.append(jnp.sum(parts_ref[3] + more, axis=0, keepdims=True))
    sums = jnp.sum(jnp.concatenate(sums, axis=0), axis=1, keepdims=True)
    lane = lax.broadcasted_iota(jnp.int32, (4, LANES), 1)
    index = lax.broadcasted_iota(jnp.int32, (4, LANES), 0)
    line = jnp.sum(jnp.where(lane == index, sums, 0.0), axis=0, keepdims=True)
    row = jnp.concatenate([jnp.where(orbit == 0, odd_end, odd_field), line], axis=0)
    several = jnp.concatenate([row] * GROUP, axis=0)
    for index in range(message_ref.shape[0] // several.shape[0]):
        message_ref[pl.ds(index * several.shape[0], several.shape[0]), :] = several


def last_kernel(
    parity,
    orbits,
    bands,
    received_ref,
    start_ref,
    next_ref,
    right_ref,
    first_ref,
    base_ref,
    shifted_ref,
    even_ref,
    rim_ref,
    scatter_ref,
    *refs,
):
    slot_refs = refs[:orbits]
    out_ref, residual_ref, order_ref, second_ref = refs[orbits:]
    columns, pieces, _ = start_ref.shape
    rows = pieces + 1

    def end_of(band):
        return received_ref[pl.ds(band * rows, pieces), :]

    def field_of(band):
        return received_ref[pl.ds((bands + band) * rows, pieces), :]

    open_sides = jnp.zeros((pieces, LANES), F32)
    for band in range(1, bands, 2):
        above = (band + 1) % bands
        open_sides = open_sides + end_of(band) * field_of(above) + end_of(above) * field_of(band)
    open_sides = jnp.sum(jnp.sum(open_sides, axis=0, keepdims=True), axis=1, keepdims=True)
    lines = received_ref[pl.ds(pieces, orbits * bands, stride=rows), :]
    line = jnp.sum(lines, axis=0, keepdims=True)
    lane = lax.broadcasted_iota(jnp.int32, line.shape, 1)
    product, energy, cross, following = (
        jnp.sum(jnp.where(lane == index, line, 0.0), axis=1, keepdims=True) for index in range(4)
    )
    following = following - (2.0 * PRIOR_WEIGHT) * open_sides
    alpha = product / energy
    later = product - 2.0 * alpha * energy + alpha * alpha * cross
    grown = 1.0 + later / product
    later_energy = (
        grown * grown * energy - 2.0 * alpha * grown * cross + alpha * alpha * following
    )
    later_alpha = later / later_energy
    on_start = alpha + later_alpha * grown
    on_next = -alpha * later_alpha

    normal = scattered_slots(orbits, scatter_ref, slot_refs, order_ref)
    second_ref[...] = base_ref[...] + normal.reshape(second_ref.shape)
    flip = parity()
    band = lax.axis_index("lon")
    across = lax.rem(band + jnp.where(flip, 1, bands - 1), bands)
    even_field, odd_field = sides(parity, next_ref[0], next_ref[columns - 1])
    near, far = near_far(parity, even_ref)
    even_first = rim_ref[2] * near - far - even_field - lat_pair(near[None])[0]
    odd_near = field_of(across)
    odd_first = end_of(across) - odd_field
    ends = (
        (0, 1, jnp.where(flip, near, odd_near), jnp.where(flip, even_first, odd_first)),
        (
            columns - 1,
            columns - 2,
            jnp.where(flip, odd_near, near),
            jnp.where(flip, odd_first, even_first),
        ),
    )
    for end, inner, field, first in ends:
        change = lat_pair(field[None])[0] - shifted_ref[end] * field - first
        second_ref[end] = second_ref[end] + PRIOR_WEIGHT * change
        second_ref[inner] = second_ref[inner] + PRIOR_WEIGHT * field

    out = on_start * start_ref[...] + on_next * next_ref[...]
    residual = right_ref[...] - on_start * first_ref[...] - on_next * second_ref[...]
    out_ref[...] = out.reshape(out_ref.shape)
    residual_ref[...] = residual.reshape(residual_ref.shape)


def per_device(orbits, bands, interp, obs_value, obs_weight, block_map, live_count, kappa2):
    slots, _, observations, width = interp.shape
    columns, latitudes = kappa2.shape
    pieces = latitudes // width
    cells = columns * pieces
    field_shape = (columns, pieces, width)

    def parity():
        return lax.rem(lax.axis_index("lon"), 2) == 1

    vmem = pl.BlockSpec(memory_space=pltpu.VMEM)
    smem = pl.BlockSpec(memory_space=pltpu.SMEM)
    anywhere = pl.BlockSpec(memory_space=pl.ANY)

    def call(kernel, outs, in_specs, scratch=(), name=None, limit=VMEM_BYTES, work=0):
        held = pltpu.VMEM if name not in ("combine", "edge_sums") else jax.ShapeDtypeStruct
        cost = pl.CostEstimate(flops=work, bytes_accessed=0, transcendentals=0) if work else None
        return pl.pallas_call(
            kernel,
            out_shape=tuple(held(shape, dtype) for shape, dtype in outs),
            in_specs=in_specs,
            out_specs=tuple(vmem for _ in outs),
            scratch_shapes=list(scratch),
            compiler_params=pltpu.CompilerParams(vmem_limit_bytes=limit),
            cost_estimate=cost,
            name=name,
        )

    def from_others(value):
        return [value] + [
            lax.ppermute(value, "orbit", [((i + step) % orbits, i) for i in range(orbits)])
            for step in range(1, orbits)
        ]

    even_pairs = [(i, i ^ 1) for i in range(bands)]
    odd_pairs = [(i, (i + 1 if i % 2 else i - 1) % bands) for i in range(bands)]

    matrices_in = interp.reshape(slots, observations, width)
    line = (slots, 1, observations)
    message, matrices, weights, pick = call(
        functools.partial(data_kernel, orbits),
        (
            ((2 * slots + GROUP, width), F32),
            ((slots, observations, width), BF16),
            ((slots, observations), F32),
            ((slots, cells), BF16),
        ),
        [smem] + [anywhere] * 4,
        [
            pltpu.SMEM((slots,), jnp.int32),
            pltpu.VMEM(line, F32),
            pltpu.VMEM(line, F32),
            pltpu.SemaphoreType.DMA((3 + slots // CHUNK,)),
        ],
        "data_terms",
        DATA_VMEM_BYTES,
    )(live_count, block_map.reshape(slots), matrices_in, obs_value, obs_weight)
    messages = from_others(message)
    shifted, blocks = call(
        block_kernel,
        ((field_shape, F32), ((slots // 2, 2 * width, 2 * width), BF16)),
        [vmem] * 3,
        (),
        "blocks",
        work=WORK,
    )(kappa2, matrices, weights)

    order = pltpu.VMEM((orbits * slots, width), F32)
    edge_width = -(-2 * orbits * slots // LANES) * LANES
    rim = ((3, pieces, width), F32)
    edge = ((2, pieces, width), F32)
    wide_edge = ((max(slots // pieces + 1, rim[0][0]), pieces, width), F32)
    field = (field_shape, F32)
    slot_terms = ((slots, width), F32)
    start, right_side, precond, scatter, even, odd = call(
        functools.partial(start_kernel, orbits, parity),
        (field, field, field, ((cells, edge_width), BF16), rim, wide_edge),
        [vmem] * (1 + orbits),
        [order],
        "start",
    )(shifted, *messages)
    rim_odd = lax.ppermute(odd, "lon", odd_pairs)
    terms, even = call(normal_kernel, (slot_terms, rim), [vmem] * 4, (), "normal_start", work=WORK)(
        pick, start, blocks, even
    )
    terms = from_others(terms)
    rim_even = lax.ppermute(even, "lon", even_pairs)
    first, following, even = call(
        functools.partial(first_kernel, parity, orbits),
        (field, field, edge),
        [vmem] * (6 + orbits),
        [order],
        "first_image",
    )(start, shifted, rim_even, rim_odd, scatter, precond, *terms)

    even = lax.ppermute(even, "lon", even_pairs)
    base, ends, parts, terms = call(
        inner_kernel,
        (field, edge, ((4, pieces, width), F32), slot_terms),
        [vmem] * 7,
        (),
        "inner_image",
        work=WORK,
    )(following, shifted, start, right_side, first, pick, blocks)
    terms = from_others(terms)
    message = ((orbits * bands * (pieces + 1), width), F32)
    (sums,) = call(
        functools.partial(edge_kernel, parity), (message,), [vmem] * 4, (), "edge_sums"
    )(following, even, ends, parts)
    sums = lax.all_to_all(sums[:, None], ("orbit", "lon"), 0, 0, tiled=True)[:, 0]
    return call(
        functools.partial(last_kernel, parity, orbits, bands),
        ((kappa2.shape, F32), (kappa2.shape, F32)),
        [vmem] * (10 + orbits),
        [order, pltpu.VMEM(field_shape, F32)],
        "combine",
    )(
        sums, start, following, right_side, first, base, shifted, even, rim_even, scatter, *terms
    )


def solution(mesh):
    in_specs = (
        P("orbit", "lon", None, None),
        P("orbit", "lon", None),
        P("orbit", "lon", None),
        P("orbit", "lon"),
        P("orbit", "lon"),
        P("lon", None),
    )
    out_specs = (P("lon", None), P("lon", None))
    body = functools.partial(per_device, mesh.shape["orbit"], mesh.shape["lon"])
    return jax.shard_map(
        body, mesh=mesh, in_specs=in_specs, out_specs=out_specs, check_vma=False
    )
```

```python
import functools

import jax
import jax.numpy as jnp
from jax import lax
from jax.experimental import pallas as pl
from jax.experimental.pallas import tpu as pltpu
from jax.sharding import PartitionSpec as P

PRIOR_WEIGHT = 0.0625
GROUP = 8
LANES = 128
F32 = jnp.float32
BF16 = jnp.bfloat16
VMEM_BYTES = 48 * 1024 * 1024
DATA_VMEM_BYTES = 59 * 1024 * 1024
CHUNK = 8
WORK = 1 << 32


def two_terms(value):
    high = value.astype(BF16)
    low = (value - high.astype(F32)).astype(BF16)
    return high, low


def stacked_terms(value):
    return jnp.concatenate(two_terms(value), axis=0)


def fold_terms(product):
    half = product.shape[0] // 2
    return product[:half] + product[half:]


def dot(left, right):
    return lax.dot_general(left, right, (((1,), (0,)), ((), ())), preferred_element_type=F32)


def dot_transposed(left, right):
    return lax.dot_general(left, right, (((1,), (1,)), ((), ())), preferred_element_type=F32)


def pick_row(total, product, slot):
    rows = lax.broadcasted_iota(jnp.int32, product.shape, 0)
    return jnp.where(rows == slot, product, total)


def lat_pair(field):
    pieces = field.shape[1]
    piece = lax.broadcasted_iota(jnp.int32, field.shape, 1)
    lane = lax.broadcasted_iota(jnp.int32, field.shape, 2)
    south = pltpu.roll(field, 1, 2)
    north = pltpu.roll(field, LANES - 1, 2)
    south_over = jnp.where(piece == 0, 0.0, pltpu.roll(south, 1, 1))
    north_over = jnp.where(piece == pieces - 1, 0.0, pltpu.roll(north, pieces - 1, 1))
    return jnp.where(lane == 0, south_over, south) + jnp.where(lane == LANES - 1, north_over, north)


def stencil(field, shifted):
    center = field[1:-1]
    return shifted * center - field[2:] - field[:-2] - lat_pair(center)


def data_kernel(
    orbits,
    count_ref,
    map_in,
    interp_in,
    value_in,
    weight_in,
    message_ref,
    matrices_ref,
    weight_ref,
    pick_ref,
    map_ref,
    value_rows,
    weight_rows,
    sems,
):
    slots = matrices_ref.shape[0]
    pairs = ((weight_in, weight_rows), (value_in, value_rows), (map_in, map_ref))
    small = [
        pltpu.make_async_copy(source, target, sems.at[index])
        for index, (source, target) in enumerate(pairs)
    ]
    large = []
    for index in range(slots // CHUNK):
        part = pl.ds(index * CHUNK, CHUNK)
        large.append(
            pltpu.make_async_copy(
                interp_in.at[part], matrices_ref.at[part], sems.at[len(small) + index]
            )
        )
    count = count_ref[0, 0]
    for copy in small:
        copy.start()
    for index, copy in enumerate(large):
        pl.when(index * CHUNK < count)(copy.start)
    for copy in small:
        copy.wait()
    orbit = lax.axis_index("orbit")
    total = orbits * slots
    place = lax.broadcasted_iota(jnp.int32, (GROUP, LANES), 0) * LANES
    place = place + lax.broadcasted_iota(jnp.int32, (GROUP, LANES), 1)
    slot_here = jnp.where(place >= total, place - total, place) - orbit * slots
    target_row = jnp.zeros((GROUP, LANES), jnp.int32)
    for slot in range(slots):
        live_target = jnp.where(slot < count, map_ref[slot] + 1, 0)
        target_row = jnp.where(slot_here == slot, live_target, target_row)
    target_row = jnp.where(place < 2 * total, target_row, 0)
    message_ref[pl.ds(2 * slots, GROUP), :] = target_row.astype(F32)
    row = lax.broadcasted_iota(jnp.int32, (GROUP, pick_ref.shape[1]), 0)
    cell = lax.broadcasted_iota(jnp.int32, row.shape, 1)
    for group in range(slots // GROUP):
        target = jnp.zeros(row.shape, jnp.int32)
        for slot in range(GROUP):
            index = group * GROUP + slot
            live_target = jnp.where(index < count, map_ref[index], -1)
            target = jnp.where(row == slot, live_target, target)
        part = pl.ds(group * GROUP, GROUP)
        pick_ref[part, :] = jnp.where(cell == target, 1.0, 0.0).astype(BF16)
    weight_ref[...] = weight_rows[:, 0, :]

    def work(index):
        large[index].wait()
        for group in range(index * CHUNK // GROUP, (index + 1) * CHUNK // GROUP):
            part = pl.ds(group * GROUP, GROUP)
            weights = weight_rows[part, 0, :]
            scaled = (weights * value_rows[part, 0, :]).astype(BF16)
            high, low = two_terms(weights)
            rows = jnp.concatenate([scaled, high, low, low], axis=0)
            first = jnp.zeros((GROUP, LANES), F32)
            second = jnp.zeros((GROUP, LANES), F32)
            for slot in range(GROUP):
                matrix = matrices_ref[group * GROUP + slot]
                both = dot(rows, jnp.concatenate([matrix, matrix * matrix], axis=1))
                squares = both[GROUP : 2 * GROUP, LANES:] + both[2 * GROUP : 3 * GROUP, LANES:]
                first = pick_row(first, both[:GROUP, :LANES], slot)
                second = pick_row(second, squares, slot)
            message_ref[part, :] = first
            message_ref[pl.ds(slots + group * GROUP, GROUP), :] = second

    def rest(index):
        part = pl.ds(index * CHUNK, CHUNK)
        matrices_ref[part] = jnp.zeros((CHUNK,) + matrices_ref.shape[1:], BF16)
        for start in (0, slots):
            part = pl.ds(start + index * CHUNK, CHUNK)
            message_ref[part, :] = jnp.zeros((CHUNK, LANES), F32)

    chunks = range(slots // CHUNK)
    for index in chunks:
        pl.when(index * CHUNK >= count)(functools.partial(rest, index))
    for index in chunks:
        pl.when(index * CHUNK < count)(functools.partial(work, index))


def block_kernel(kappa_ref, matrices_ref, weight_ref, shifted_ref, blocks_ref):
    shifted_ref[...] = kappa_ref[...].reshape(shifted_ref.shape) + 4.0
    width = matrices_ref.shape[2]
    for slot in range(matrices_ref.shape[0]):
        matrix = matrices_ref[slot]
        weighted = matrix.T.astype(F32) * weight_ref[pl.ds(slot, 1), :]
        high, low = two_terms(fold_terms(dot(stacked_terms(weighted), matrix)))
        columns = pl.ds(slot % 2 * width, width)
        blocks_ref[slot // 2, pl.ds(0, width), columns] = high
        blocks_ref[slot // 2, pl.ds(width, width), columns] = low


def gather_messages(orbits, slots, message_refs, order_ref):
    orbit = lax.axis_index("orbit")
    for step in range(orbits):
        source = lax.rem(orbit + step, orbits)
        rows = pl.ds(pl.multiple_of(source * slots, slots), slots)
        order_ref[rows, :] = message_refs[step]


def start_kernel(
    orbits, parity, shifted_ref, *refs
):
    message_refs = refs[:orbits]
    (
        field_ref,
        right_ref,
        precond_ref,
        scatter_ref,
        even_ref,
        odd_ref,
        order_ref,
    ) = refs[orbits:]
    slots = (message_refs[0].shape[0] - GROUP) // 2
    cells = scatter_ref.shape[0]
    targets = message_refs[0][pl.ds(2 * slots, GROUP), :]
    for ref in message_refs[1:]:
        targets = targets + ref[pl.ds(2 * slots, GROUP), :]
    targets = targets.astype(jnp.int32) - 1
    row = lax.broadcasted_iota(jnp.int32, (cells, LANES), 0)
    for piece in range(scatter_ref.shape[1] // LANES):
        hit = row == targets[piece : piece + 1, :]
        scatter_ref[:, pl.ds(piece * LANES, LANES)] = jnp.where(hit, 1.0, 0.0).astype(BF16)
    sums = []
    for part in range(2):
        rows = pl.ds(part * slots, slots)
        gather_messages(orbits, slots, [ref[rows, :] for ref in message_refs], order_ref)
        sums.append(scattered(scatter_ref[...], order_ref[...]))
    right_side, obs_diag = (value.reshape(field_ref.shape) for value in sums)
    shifted = shifted_ref[...]
    precond = PRIOR_WEIGHT * (shifted * shifted + 4.0) + obs_diag
    field = right_side / precond
    right_ref[...] = right_side
    precond_ref[...] = precond
    field_ref[...] = field
    columns = field.shape[0]
    top = jnp.concatenate([field[:2], shifted[:1]], axis=0)
    bottom = jnp.concatenate([field[columns - 2 :], shifted[columns - 1 :]], axis=0)
    store_edges(parity, top, bottom, even_ref, odd_ref)


def normal_kernel(
    count_ref, pick_ref, field_ref, blocks_ref, even_ref, out_ref, even_out_ref
):
    even_out_ref[...] = even_ref[...]
    slots = pick_ref.shape[0]
    half = max(slots // (2 * GROUP), 1) * GROUP
    few = count_ref[0, 0] <= half

    @pl.when(few)
    def _():
        normal_slots(pick_ref, field_ref[...], blocks_ref, out_ref, half)

    @pl.when(jnp.logical_not(few))
    def _():
        normal_slots(pick_ref, field_ref[...], blocks_ref, out_ref)


def scattered(one_hot, slots):
    terms = stacked_terms(slots)
    spare = one_hot.shape[1] - terms.shape[0]
    if spare:
        terms = jnp.concatenate([terms, jnp.zeros((spare, LANES), BF16)], axis=0)
    return dot(one_hot, terms)


def store_edges(parity, top, bottom, even_ref, odd_ref):
    flip = parity()
    used = top.shape[0]
    even_ref[...] = jnp.where(flip, top, bottom)
    odd_ref[:used] = jnp.where(flip, bottom, top)
    if odd_ref.shape[0] > used:
        odd_ref[used:] = jnp.zeros((odd_ref.shape[0] - used,) + top.shape[1:], F32)


def load_edges(parity, even_ref, odd_ref):
    flip = parity()
    even = even_ref[...]
    odd = odd_ref[: even.shape[0]]
    return jnp.where(flip, even, odd), jnp.where(flip, odd, even)


def normal_slots(pick_ref, field, blocks_ref, out_ref, used=None):
    width = field.shape[-1]
    field = field.reshape(pick_ref.shape[1], width)
    used = used or pick_ref.shape[0]
    picked = dot(pick_ref[pl.ds(0, used), :], jnp.concatenate(two_terms(field), axis=1))
    picked = picked[:, :width] + picked[:, width:]
    energy = jnp.zeros((GROUP, width), F32)
    spare = pick_ref.shape[0] - used
    if spare:
        out_ref[pl.ds(used, spare), :] = jnp.zeros((spare, width), F32)
    for group in range(used // GROUP):
        cells = picked[group * GROUP : (group + 1) * GROUP]
        rows = stacked_terms(cells)
        rows = jnp.concatenate([rows, rows], axis=1)
        total = jnp.zeros((GROUP, width), F32)
        for slot in range(0, GROUP, 2):
            product = fold_terms(dot(rows, blocks_ref[(group * GROUP + slot) // 2]))
            total = pick_row(total, product[:, :width], slot)
            total = pick_row(total, product[:, width:], slot + 1)
        out_ref[pl.ds(group * GROUP, GROUP), :] = total
        energy = energy + cells * total
    return energy


def extended(field, top, bottom):
    return jnp.concatenate([top, field, bottom], axis=0)


def prior_parts(field, shifted, top, bottom, shifted_top, shifted_bottom):
    first = stencil(
        extended(field, top, bottom), extended(shifted, shifted_top, shifted_bottom)
    )
    return PRIOR_WEIGHT * stencil(first, shifted)


def scattered_slots(orbits, scatter_ref, slot_refs, order_ref):
    slots = slot_refs[0].shape[0]
    gather_messages(orbits, slots, [ref[...] for ref in slot_refs], order_ref)
    return scattered(scatter_ref[...], order_ref[...])


def pair_edge_kernel(
    parity,
    orbits,
    field_ref,
    shifted_ref,
    even_ref,
    odd_ref,
    scatter_ref,
    precond_ref,
    *refs,
):
    slot_refs = refs[:orbits]
    edge_ref, order_ref = refs[orbits:]
    slots = slot_refs[0].shape[0]
    gather_messages(orbits, slots, [ref[...] for ref in slot_refs], order_ref)
    columns, pieces, width = field_ref.shape
    flip = parity()
    top, bottom = load_edges(parity, even_ref, odd_ref)
    field = jnp.where(
        flip,
        extended(field_ref[pl.ds(0, 2)], top[:2], field_ref[pl.ds(2, 2)]),
        extended(field_ref[pl.ds(columns - 2, 2)], field_ref[pl.ds(columns - 4, 2)], bottom[:2]),
    )
    shifted = jnp.where(
        flip,
        jnp.concatenate([top[2:], shifted_ref[pl.ds(0, 3)]], axis=0),
        jnp.concatenate([shifted_ref[pl.ds(columns - 3, 3)], bottom[2:]], axis=0),
    )
    once = stencil(field, shifted)
    twice = stencil(once, shifted[1:-1])
    start = jnp.where(flip, 0, columns - 2)
    rows = pl.ds(pl.multiple_of(start * pieces, 2 * pieces), 2 * pieces)
    normal = scattered(scatter_ref[rows, :], order_ref[...]).reshape(twice.shape)
    edge_ref[...] = (PRIOR_WEIGHT * twice + normal) / precond_ref[pl.ds(start, 2)]


def alone(field, shifted):
    zero = jnp.zeros((1,) + field.shape[1:], F32)
    return stencil(extended(field, zero, zero), shifted)


def sides(parity, top, bottom):
    flip = parity()
    return jnp.where(flip, top, bottom), jnp.where(flip, bottom, top)


def near_far(parity, even_ref):
    flip = parity()
    return jnp.where(flip, even_ref[1], even_ref[0]), jnp.where(flip, even_ref[0], even_ref[1])


def chunks_of(rows):
    return jnp.concatenate([rows] * GROUP, axis=0)


def images_kernel(
    parity,
    orbits,
    field_ref,
    shifted_ref,
    even_ref,
    odd_ref,
    scatter_ref,
    precond_ref,
    right_ref,
    pick_ref,
    blocks_ref,
    *refs,
):
    slot_refs = refs[:orbits]
    image_ref, next_ref, base_ref, end_ref, parts_ref, chunks_ref, out_ref, order_ref = refs[orbits:]
    normal = scattered_slots(orbits, scatter_ref, slot_refs, order_ref)
    top, bottom = load_edges(parity, even_ref, odd_ref)
    start, shifted = field_ref[...], shifted_ref[...]
    prior = prior_parts(start, shifted, top[:2], bottom[:2], top[2:], bottom[2:])
    image = prior + normal.reshape(start.shape)
    field = image / precond_ref[...]
    image_ref[...] = image
    next_ref[...] = field
    energy = normal_slots(pick_ref, field, blocks_ref, out_ref)
    once = alone(field, shifted)
    base_ref[...] = PRIOR_WEIGHT * alone(once, shifted)
    last = once.shape[0] - 1
    even_end, odd_end = sides(parity, once[0], once[last])
    _, odd_field = sides(parity, field[0], field[last])
    end_ref[...] = even_end
    orbit = lax.axis_index("orbit")
    own = jnp.where(orbit == 0, 1.0, 0.0)
    squares = jnp.sum(once * once, axis=0) + odd_field * odd_field
    parts = (
        own * jnp.sum(right_ref[...] * start, axis=0),
        own * jnp.sum(start * image, axis=0),
        own * jnp.sum(image * field, axis=0),
        own * PRIOR_WEIGHT * squares + energy,
    )
    for index, part in enumerate(parts):
        parts_ref[pl.ds(index, 1), :] = jnp.sum(part, axis=0, keepdims=True)
    edge = jnp.where(orbit == 0, odd_end, odd_field)
    chunks_ref[...] = chunks_of(jnp.concatenate([edge, jnp.zeros((1, LANES), F32)], axis=0))


def edge_kernel(parity, even_ref, end_ref, parts_ref, chunks_ref, message_ref):
    near, _ = near_far(parity, even_ref)
    own = jnp.where(lax.axis_index("orbit") == 0, PRIOR_WEIGHT, 0.0)
    more = own * jnp.sum(near * (near - 2.0 * end_ref[...]), axis=0, keepdims=True)
    index = lax.broadcasted_iota(jnp.int32, (4, LANES), 0)
    lane = lax.broadcasted_iota(jnp.int32, (4, LANES), 1)
    sums = jnp.sum(parts_ref[...] + jnp.where(index == 3, more, 0.0), axis=1, keepdims=True)
    line = jnp.sum(jnp.where(lane == index, sums, 0.0), axis=0, keepdims=True)
    rows = chunks_ref.shape[0]
    period = rows // GROUP
    row = lax.broadcasted_iota(jnp.int32, (rows, LANES), 0)
    chunks = jnp.where(lax.rem(row, period) == period - 1, line, chunks_ref[...])
    for index in range(message_ref.shape[0] // rows):
        message_ref[pl.ds(index * rows, rows), :] = chunks


def last_kernel(
    parity,
    orbits,
    bands,
    received_ref,
    start_ref,
    next_ref,
    right_ref,
    first_ref,
    base_ref,
    shifted_ref,
    even_ref,
    rim_ref,
    scatter_ref,
    *refs,
):
    slot_refs = refs[:orbits]
    out_ref, residual_ref, order_ref, second_ref = refs[orbits:]
    columns, pieces, _ = start_ref.shape
    rows = pieces + 1

    def end_of(band):
        return received_ref[pl.ds(band * rows, pieces), :]

    def field_of(band):
        return received_ref[pl.ds((bands + band) * rows, pieces), :]

    open_sides = jnp.zeros((pieces, LANES), F32)
    for band in range(1, bands, 2):
        above = (band + 1) % bands
        open_sides = open_sides + end_of(band) * field_of(above) + end_of(above) * field_of(band)
    open_sides = jnp.sum(jnp.sum(open_sides, axis=0, keepdims=True), axis=1, keepdims=True)
    lines = received_ref[pl.ds(pieces, orbits * bands, stride=rows), :]
    line = jnp.sum(lines, axis=0, keepdims=True)
    lane = lax.broadcasted_iota(jnp.int32, line.shape, 1)
    product, energy, cross, following = (
        jnp.sum(jnp.where(lane == index, line, 0.0), axis=1, keepdims=True) for index in range(4)
    )
    following = following - (2.0 * PRIOR_WEIGHT) * open_sides
    alpha = product / energy
    later = product - 2.0 * alpha * energy + alpha * alpha * cross
    grown = 1.0 + later / product
    later_energy = (
        grown * grown * energy - 2.0 * alpha * grown * cross + alpha * alpha * following
    )
    later_alpha = later / later_energy
    on_start = alpha + later_alpha * grown
    on_next = -alpha * later_alpha

    normal = scattered_slots(orbits, scatter_ref, slot_refs, order_ref)
    second_ref[...] = base_ref[...] + normal.reshape(second_ref.shape)
    flip = parity()
    band = lax.axis_index("lon")
    across = lax.rem(band + jnp.where(flip, 1, bands - 1), bands)
    even_field, odd_field = sides(parity, next_ref[0], next_ref[columns - 1])
    near, far = near_far(parity, even_ref)
    even_first = rim_ref[2] * near - far - even_field - lat_pair(near[None])[0]
    odd_near = field_of(across)
    odd_first = end_of(across) - odd_field
    ends = (
        (0, 1, jnp.where(flip, near, odd_near), jnp.where(flip, even_first, odd_first)),
        (
            columns - 1,
            columns - 2,
            jnp.where(flip, odd_near, near),
            jnp.where(flip, odd_first, even_first),
        ),
    )
    for end, inner, field, first in ends:
        change = lat_pair(field[None])[0] - shifted_ref[end] * field - first
        second_ref[end] = second_ref[end] + PRIOR_WEIGHT * change
        second_ref[inner] = second_ref[inner] + PRIOR_WEIGHT * field

    out = on_start * start_ref[...] + on_next * next_ref[...]
    residual = right_ref[...] - on_start * first_ref[...] - on_next * second_ref[...]
    out_ref[...] = out.reshape(out_ref.shape)
    residual_ref[...] = residual.reshape(residual_ref.shape)


def per_device(orbits, bands, interp, obs_value, obs_weight, block_map, live_count, kappa2):
    slots, _, observations, width = interp.shape
    columns, latitudes = kappa2.shape
    pieces = latitudes // width
    cells = columns * pieces
    field_shape = (columns, pieces, width)

    def parity():
        return lax.rem(lax.axis_index("lon"), 2) == 1

    vmem = pl.BlockSpec(memory_space=pltpu.VMEM)
    smem = pl.BlockSpec(memory_space=pltpu.SMEM)
    anywhere = pl.BlockSpec(memory_space=pl.ANY)

    def call(kernel, outs, in_specs, scratch=(), name=None, limit=VMEM_BYTES, work=0):
        held = pltpu.VMEM if name not in ("combine", "edge_sums") else jax.ShapeDtypeStruct
        cost = pl.CostEstimate(flops=work, bytes_accessed=0, transcendentals=0) if work else None
        return pl.pallas_call(
            kernel,
            out_shape=tuple(held(shape, dtype) for shape, dtype in outs),
            in_specs=in_specs,
            out_specs=tuple(vmem for _ in outs),
            scratch_shapes=list(scratch),
            compiler_params=pltpu.CompilerParams(vmem_limit_bytes=limit),
            cost_estimate=cost,
            name=name,
        )

    def from_others(value):
        return [value] + [
            lax.ppermute(value, "orbit", [((i + step) % orbits, i) for i in range(orbits)])
            for step in range(1, orbits)
        ]

    even_pairs = [(i, i ^ 1) for i in range(bands)]
    odd_pairs = [(i, (i + 1 if i % 2 else i - 1) % bands) for i in range(bands)]

    matrices_in = interp.reshape(slots, observations, width)
    line = (slots, 1, observations)
    message, matrices, weights, pick = call(
        functools.partial(data_kernel, orbits),
        (
            ((2 * slots + GROUP, width), F32),
            ((slots, observations, width), BF16),
            ((slots, observations), F32),
            ((slots, cells), BF16),
        ),
        [smem] + [anywhere] * 4,
        [
            pltpu.SMEM((slots,), jnp.int32),
            pltpu.VMEM(line, F32),
            pltpu.VMEM(line, F32),
            pltpu.SemaphoreType.DMA((3 + slots // CHUNK,)),
        ],
        "data_terms",
        DATA_VMEM_BYTES,
    )(live_count, block_map.reshape(slots), matrices_in, obs_value, obs_weight)
    messages = from_others(message)
    shifted, blocks = call(
        block_kernel,
        ((field_shape, F32), ((slots // 2, 2 * width, 2 * width), BF16)),
        [vmem] * 3,
        (),
        "blocks",
        work=WORK,
    )(kappa2, matrices, weights)

    order = pltpu.VMEM((orbits * slots, width), F32)
    edge_width = -(-2 * orbits * slots // LANES) * LANES
    rim = ((3, pieces, width), F32)
    edge = ((2, pieces, width), F32)
    wide_edge = ((max(slots // pieces + 1, rim[0][0]), pieces, width), F32)
    field = (field_shape, F32)
    slot_terms = ((slots, width), F32)
    start, right_side, precond, scatter, even, odd = call(
        functools.partial(start_kernel, orbits, parity),
        (field, field, field, ((cells, edge_width), BF16), rim, wide_edge),
        [vmem] * (1 + orbits),
        [order],
        "start",
    )(shifted, *messages)
    rim_odd = lax.ppermute(odd, "lon", odd_pairs)
    terms, even = call(
        normal_kernel,
        (slot_terms, rim),
        [smem] + [vmem] * 4,
        (),
        "normal_start",
        work=WORK,
    )(live_count, pick, start, blocks, even)
    terms = from_others(terms)
    rim_even = lax.ppermute(even, "lon", even_pairs)
    image_inputs = (start, shifted, rim_even, rim_odd, scatter, precond, *terms)
    (even,) = call(
        functools.partial(pair_edge_kernel, parity, orbits),
        (edge,),
        [vmem] * (6 + orbits),
        [order],
        "pair_edge",
    )(*image_inputs)
    even = lax.ppermute(even, "lon", even_pairs)
    chunk = pieces + 1
    first, following, base, end, parts, chunks, terms = call(
        functools.partial(images_kernel, parity, orbits),
        (
            field,
            field,
            field,
            ((pieces, width), F32),
            ((4, width), F32),
            ((GROUP * chunk, width), F32),
            slot_terms,
        ),
        [vmem] * (9 + orbits),
        [order],
        "images",
        work=WORK,
    )(*image_inputs[:6], right_side, pick, blocks, *terms)
    terms = from_others(terms)
    message = ((orbits * bands * chunk, width), F32)
    (sums,) = call(
        functools.partial(edge_kernel, parity), (message,), [vmem] * 4, (), "edge_sums"
    )(even, end, parts, chunks)
    sums = lax.all_to_all(sums[:, None], ("orbit", "lon"), 0, 0, tiled=True)[:, 0]
    return call(
        functools.partial(last_kernel, parity, orbits, bands),
        ((kappa2.shape, F32), (kappa2.shape, F32)),
        [vmem] * (10 + orbits),
        [order, pltpu.VMEM(field_shape, F32)],
        "combine",
    )(
        sums, start, following, right_side, first, base, shifted, even, rim_even, scatter, *terms
    )


def solution(mesh):
    in_specs = (
        P("orbit", "lon", None, None),
        P("orbit", "lon", None),
        P("orbit", "lon", None),
        P("orbit", "lon"),
        P("orbit", "lon"),
        P("lon", None),
    )
    out_specs = (P("lon", None), P("lon", None))
    body = functools.partial(per_device, mesh.shape["orbit"], mesh.shape["lon"])
    return jax.shard_map(
        body, mesh=mesh, in_specs=in_specs, out_specs=out_specs, check_vma=False
    )
```

```python
import functools

import jax
import jax.numpy as jnp
from jax import lax
from jax.experimental import pallas as pl
from jax.experimental.pallas import tpu as pltpu
from jax.sharding import PartitionSpec as P

PRIOR_WEIGHT = 0.0625
GROUP = 8
LANES = 128
F32 = jnp.float32
BF16 = jnp.bfloat16
VMEM_BYTES = 48 * 1024 * 1024
DATA_VMEM_BYTES = 59 * 1024 * 1024
CHUNK = 8
WORK = 1 << 32


def two_terms(value):
    high = value.astype(BF16)
    low = (value - high.astype(F32)).astype(BF16)
    return high, low


def stacked_terms(value):
    return jnp.concatenate(two_terms(value), axis=0)


def fold_terms(product):
    half = product.shape[0] // 2
    return product[:half] + product[half:]


def dot(left, right):
    return lax.dot_general(left, right, (((1,), (0,)), ((), ())), preferred_element_type=F32)


def pick_row(total, product, slot):
    rows = lax.broadcasted_iota(jnp.int32, product.shape, 0)
    return jnp.where(rows == slot, product, total)


def lat_pair(field):
    pieces = field.shape[1]
    piece = lax.broadcasted_iota(jnp.int32, field.shape, 1)
    lane = lax.broadcasted_iota(jnp.int32, field.shape, 2)
    south = pltpu.roll(field, 1, 2)
    north = pltpu.roll(field, LANES - 1, 2)
    south_over = jnp.where(piece == 0, 0.0, pltpu.roll(south, 1, 1))
    north_over = jnp.where(piece == pieces - 1, 0.0, pltpu.roll(north, pieces - 1, 1))
    return jnp.where(lane == 0, south_over, south) + jnp.where(lane == LANES - 1, north_over, north)


def stencil(field, shifted):
    center = field[1:-1]
    return shifted * center - field[2:] - field[:-2] - lat_pair(center)


def data_kernel(
    orbits,
    count_ref,
    map_in,
    interp_in,
    value_in,
    weight_in,
    message_ref,
    matrices_ref,
    weight_ref,
    pick_ref,
    map_ref,
    value_rows,
    weight_rows,
    sems,
):
    slots = matrices_ref.shape[0]
    pairs = ((weight_in, weight_rows), (value_in, value_rows), (map_in, map_ref))
    small = [
        pltpu.make_async_copy(source, target, sems.at[index])
        for index, (source, target) in enumerate(pairs)
    ]
    large = []
    for index in range(slots // CHUNK):
        part = pl.ds(index * CHUNK, CHUNK)
        large.append(
            pltpu.make_async_copy(
                interp_in.at[part], matrices_ref.at[part], sems.at[len(small) + index]
            )
        )
    count = count_ref[0, 0]
    for copy in small:
        copy.start()
    for index, copy in enumerate(large):
        pl.when(index * CHUNK < count)(copy.start)
    for copy in small:
        copy.wait()
    orbit = lax.axis_index("orbit")
    total = orbits * slots
    place = lax.broadcasted_iota(jnp.int32, (GROUP, LANES), 0) * LANES
    place = place + lax.broadcasted_iota(jnp.int32, (GROUP, LANES), 1)
    slot_here = jnp.where(place >= total, place - total, place) - orbit * slots
    target_row = jnp.zeros((GROUP, LANES), jnp.int32)
    for slot in range(slots):
        live_target = jnp.where(slot < count, map_ref[slot] + 1, 0)
        target_row = jnp.where(slot_here == slot, live_target, target_row)
    target_row = jnp.where(place < 2 * total, target_row, 0)
    message_ref[pl.ds(2 * slots, GROUP), :] = target_row.astype(F32)
    row = lax.broadcasted_iota(jnp.int32, (GROUP, pick_ref.shape[1]), 0)
    cell = lax.broadcasted_iota(jnp.int32, row.shape, 1)
    for group in range(slots // GROUP):
        target = jnp.zeros(row.shape, jnp.int32)
        for slot in range(GROUP):
            index = group * GROUP + slot
            live_target = jnp.where(index < count, map_ref[index], -1)
            target = jnp.where(row == slot, live_target, target)
        part = pl.ds(group * GROUP, GROUP)
        pick_ref[part, :] = jnp.where(cell == target, 1.0, 0.0).astype(BF16)
    weight_ref[...] = weight_rows[:, 0, :]

    def work(index):
        large[index].wait()
        for group in range(index * CHUNK // GROUP, (index + 1) * CHUNK // GROUP):
            part = pl.ds(group * GROUP, GROUP)
            weights = weight_rows[part, 0, :]
            scaled = (weights * value_rows[part, 0, :]).astype(BF16)
            high, low = two_terms(weights)
            rows = jnp.concatenate([scaled, high, low, low], axis=0)
            first = jnp.zeros((GROUP, LANES), F32)
            second = jnp.zeros((GROUP, LANES), F32)
            for slot in range(GROUP):
                matrix = matrices_ref[group * GROUP + slot]
                both = dot(rows, jnp.concatenate([matrix, matrix * matrix], axis=1))
                squares = both[GROUP : 2 * GROUP, LANES:] + both[2 * GROUP : 3 * GROUP, LANES:]
                first = pick_row(first, both[:GROUP, :LANES], slot)
                second = pick_row(second, squares, slot)
            message_ref[part, :] = first
            message_ref[pl.ds(slots + group * GROUP, GROUP), :] = second

    def rest(index):
        part = pl.ds(index * CHUNK, CHUNK)
        matrices_ref[part] = jnp.zeros((CHUNK,) + matrices_ref.shape[1:], BF16)
        for start in (0, slots):
            part = pl.ds(start + index * CHUNK, CHUNK)
            message_ref[part, :] = jnp.zeros((CHUNK, LANES), F32)

    chunks = range(slots // CHUNK)
    for index in chunks:
        pl.when(index * CHUNK >= count)(functools.partial(rest, index))
    for index in chunks:
        pl.when(index * CHUNK < count)(functools.partial(work, index))


def block_kernel(kappa_ref, matrices_ref, weight_ref, shifted_ref, blocks_ref):
    shifted_ref[...] = kappa_ref[...].reshape(shifted_ref.shape) + 4.0
    width = matrices_ref.shape[2]
    for slot in range(matrices_ref.shape[0]):
        matrix = matrices_ref[slot]
        weighted = matrix.T.astype(F32) * weight_ref[pl.ds(slot, 1), :]
        high, low = two_terms(fold_terms(dot(stacked_terms(weighted), matrix)))
        columns = pl.ds(slot % 2 * width, width)
        blocks_ref[slot // 2, pl.ds(0, width), columns] = high
        blocks_ref[slot // 2, pl.ds(width, width), columns] = low


def gather_messages(orbits, slots, message_refs, order_ref):
    orbit = lax.axis_index("orbit")
    for step in range(orbits):
        source = lax.rem(orbit + step, orbits)
        rows = pl.ds(pl.multiple_of(source * slots, slots), slots)
        order_ref[rows, :] = message_refs[step]


def start_kernel(
    orbits, parity, shifted_ref, *refs
):
    message_refs = refs[:orbits]
    (
        field_ref,
        right_ref,
        precond_ref,
        scatter_ref,
        even_ref,
        odd_ref,
        order_ref,
    ) = refs[orbits:]
    slots = (message_refs[0].shape[0] - GROUP) // 2
    cells = scatter_ref.shape[0]
    targets = message_refs[0][pl.ds(2 * slots, GROUP), :]
    for ref in message_refs[1:]:
        targets = targets + ref[pl.ds(2 * slots, GROUP), :]
    targets = targets.astype(jnp.int32) - 1
    row = lax.broadcasted_iota(jnp.int32, (cells, LANES), 0)
    for piece in range(scatter_ref.shape[1] // LANES):
        hit = row == targets[piece : piece + 1, :]
        scatter_ref[:, pl.ds(piece * LANES, LANES)] = jnp.where(hit, 1.0, 0.0).astype(BF16)
    sums = []
    for part in range(2):
        rows = pl.ds(part * slots, slots)
        gather_messages(orbits, slots, [ref[rows, :] for ref in message_refs], order_ref)
        sums.append(scattered(scatter_ref[...], order_ref[...]))
    right_side, obs_diag = (value.reshape(field_ref.shape) for value in sums)
    shifted = shifted_ref[...]
    precond = PRIOR_WEIGHT * (shifted * shifted + 4.0) + obs_diag
    field = right_side / precond
    right_ref[...] = right_side
    precond_ref[...] = precond
    field_ref[...] = field
    columns = field.shape[0]
    top = jnp.concatenate([field[:2], shifted[:1]], axis=0)
    bottom = jnp.concatenate([field[columns - 2 :], shifted[columns - 1 :]], axis=0)
    store_edges(parity, top, bottom, even_ref, odd_ref)


def normal_kernel(
    count_ref, pick_ref, field_ref, blocks_ref, even_ref, out_ref, even_out_ref
):
    even_out_ref[...] = even_ref[...]
    slots = pick_ref.shape[0]
    half = max(slots // (2 * GROUP), 1) * GROUP
    few = count_ref[0, 0] <= half

    @pl.when(few)
    def _():
        normal_slots(pick_ref, field_ref[...], blocks_ref, out_ref, half)

    @pl.when(jnp.logical_not(few))
    def _():
        normal_slots(pick_ref, field_ref[...], blocks_ref, out_ref)


def scattered(one_hot, slots):
    terms = stacked_terms(slots)
    spare = one_hot.shape[1] - terms.shape[0]
    if spare:
        terms = jnp.concatenate([terms, jnp.zeros((spare, LANES), BF16)], axis=0)
    return dot(one_hot, terms)


def store_edges(parity, top, bottom, even_ref, odd_ref):
    flip = parity()
    used = top.shape[0]
    even_ref[...] = jnp.where(flip, top, bottom)
    odd_ref[:used] = jnp.where(flip, bottom, top)
    if odd_ref.shape[0] > used:
        odd_ref[used:] = jnp.zeros((odd_ref.shape[0] - used,) + top.shape[1:], F32)


def load_edges(parity, even_ref, odd_ref):
    flip = parity()
    even = even_ref[...]
    odd = odd_ref[: even.shape[0]]
    return jnp.where(flip, even, odd), jnp.where(flip, odd, even)


def normal_slots(pick_ref, field, blocks_ref, out_ref, used=None):
    width = field.shape[-1]
    field = field.reshape(pick_ref.shape[1], width)
    used = used or pick_ref.shape[0]
    picked = dot(pick_ref[pl.ds(0, used), :], jnp.concatenate(two_terms(field), axis=1))
    picked = picked[:, :width] + picked[:, width:]
    energy = jnp.zeros((GROUP, width), F32)
    spare = pick_ref.shape[0] - used
    if spare:
        out_ref[pl.ds(used, spare), :] = jnp.zeros((spare, width), F32)
    for group in range(used // GROUP):
        cells = picked[group * GROUP : (group + 1) * GROUP]
        rows = stacked_terms(cells)
        rows = jnp.concatenate([rows, rows], axis=1)
        total = jnp.zeros((GROUP, width), F32)
        for slot in range(0, GROUP, 2):
            product = fold_terms(dot(rows, blocks_ref[(group * GROUP + slot) // 2]))
            total = pick_row(total, product[:, :width], slot)
            total = pick_row(total, product[:, width:], slot + 1)
        out_ref[pl.ds(group * GROUP, GROUP), :] = total
        energy = energy + cells * total
    return energy


def extended(field, top, bottom):
    return jnp.concatenate([top, field, bottom], axis=0)


def prior_parts(field, shifted, top, bottom, shifted_top, shifted_bottom):
    first = stencil(
        extended(field, top, bottom), extended(shifted, shifted_top, shifted_bottom)
    )
    return PRIOR_WEIGHT * stencil(first, shifted)


def scattered_slots(orbits, scatter_ref, slot_refs, order_ref):
    slots = slot_refs[0].shape[0]
    gather_messages(orbits, slots, [ref[...] for ref in slot_refs], order_ref)
    return scattered(scatter_ref[...], order_ref[...])


def pair_edge_kernel(
    parity,
    orbits,
    field_ref,
    shifted_ref,
    even_ref,
    odd_ref,
    scatter_ref,
    precond_ref,
    *refs,
):
    slot_refs = refs[:orbits]
    edge_ref, order_ref = refs[orbits:]
    slots = slot_refs[0].shape[0]
    gather_messages(orbits, slots, [ref[...] for ref in slot_refs], order_ref)
    columns, pieces, width = field_ref.shape
    flip = parity()
    top, bottom = load_edges(parity, even_ref, odd_ref)
    field = jnp.where(
        flip,
        extended(field_ref[pl.ds(0, 2)], top[:2], field_ref[pl.ds(2, 2)]),
        extended(field_ref[pl.ds(columns - 2, 2)], field_ref[pl.ds(columns - 4, 2)], bottom[:2]),
    )
    shifted = jnp.where(
        flip,
        jnp.concatenate([top[2:], shifted_ref[pl.ds(0, 3)]], axis=0),
        jnp.concatenate([shifted_ref[pl.ds(columns - 3, 3)], bottom[2:]], axis=0),
    )
    once = stencil(field, shifted)
    twice = stencil(once, shifted[1:-1])
    start = jnp.where(flip, 0, columns - 2)
    rows = pl.ds(pl.multiple_of(start * pieces, 2 * pieces), 2 * pieces)
    normal = scattered(scatter_ref[rows, :], order_ref[...]).reshape(twice.shape)
    edge_ref[...] = (PRIOR_WEIGHT * twice + normal) / precond_ref[pl.ds(start, 2)]


def alone(field, shifted):
    zero = jnp.zeros((1,) + field.shape[1:], F32)
    return stencil(extended(field, zero, zero), shifted)


def sides(parity, top, bottom):
    flip = parity()
    return jnp.where(flip, top, bottom), jnp.where(flip, bottom, top)


def near_far(parity, even_ref):
    flip = parity()
    return jnp.where(flip, even_ref[1], even_ref[0]), jnp.where(flip, even_ref[0], even_ref[1])


def chunks_of(rows):
    return jnp.concatenate([rows] * GROUP, axis=0)


def images_kernel(
    parity,
    orbits,
    field_ref,
    shifted_ref,
    even_ref,
    odd_ref,
    scatter_ref,
    precond_ref,
    right_ref,
    pick_ref,
    blocks_ref,
    *refs,
):
    slot_refs = refs[:orbits]
    image_ref, next_ref, base_ref, end_ref, parts_ref, chunks_ref, out_ref, order_ref = refs[orbits:]
    normal = scattered_slots(orbits, scatter_ref, slot_refs, order_ref)
    top, bottom = load_edges(parity, even_ref, odd_ref)
    start, shifted = field_ref[...], shifted_ref[...]
    prior = prior_parts(start, shifted, top[:2], bottom[:2], top[2:], bottom[2:])
    image = prior + normal.reshape(start.shape)
    field = image / precond_ref[...]
    image_ref[...] = image
    next_ref[...] = field
    energy = normal_slots(pick_ref, field, blocks_ref, out_ref)
    once = alone(field, shifted)
    base_ref[...] = PRIOR_WEIGHT * alone(once, shifted)
    last = once.shape[0] - 1
    even_end, odd_end = sides(parity, once[0], once[last])
    _, odd_field = sides(parity, field[0], field[last])
    end_ref[...] = even_end
    orbit = lax.axis_index("orbit")
    own = jnp.where(orbit == 0, 1.0, 0.0)
    squares = jnp.sum(once * once, axis=0) + odd_field * odd_field
    parts = (
        own * jnp.sum(right_ref[...] * start, axis=0),
        own * jnp.sum(start * image, axis=0),
        own * jnp.sum(image * field, axis=0),
        own * PRIOR_WEIGHT * squares + energy,
    )
    for index, part in enumerate(parts):
        parts_ref[pl.ds(index, 1), :] = jnp.sum(part, axis=0, keepdims=True)
    edge = jnp.where(orbit == 0, odd_end, odd_field)
    chunks_ref[...] = chunks_of(jnp.concatenate([edge, jnp.zeros((1, LANES), F32)], axis=0))


def edge_kernel(parity, even_ref, end_ref, parts_ref, chunks_ref, message_ref):
    near, _ = near_far(parity, even_ref)
    own = jnp.where(lax.axis_index("orbit") == 0, PRIOR_WEIGHT, 0.0)
    more = own * jnp.sum(near * (near - 2.0 * end_ref[...]), axis=0, keepdims=True)
    index = lax.broadcasted_iota(jnp.int32, (4, LANES), 0)
    lane = lax.broadcasted_iota(jnp.int32, (4, LANES), 1)
    sums = jnp.sum(parts_ref[...] + jnp.where(index == 3, more, 0.0), axis=1, keepdims=True)
    line = jnp.sum(jnp.where(lane == index, sums, 0.0), axis=0, keepdims=True)
    rows = chunks_ref.shape[0]
    period = rows // GROUP
    row = lax.broadcasted_iota(jnp.int32, (rows, LANES), 0)
    chunks = jnp.where(lax.rem(row, period) == period - 1, line, chunks_ref[...])
    for index in range(message_ref.shape[0] // rows):
        message_ref[pl.ds(index * rows, rows), :] = chunks


def last_kernel(
    parity,
    orbits,
    bands,
    received_ref,
    start_ref,
    next_ref,
    right_ref,
    first_ref,
    base_ref,
    shifted_ref,
    even_ref,
    rim_ref,
    scatter_ref,
    *refs,
):
    slot_refs = refs[:orbits]
    out_ref, residual_ref, order_ref, second_ref = refs[orbits:]
    columns, pieces, _ = start_ref.shape
    rows = pieces + 1

    def end_of(band):
        return received_ref[pl.ds(band * rows, pieces), :]

    def field_of(band):
        return received_ref[pl.ds((bands + band) * rows, pieces), :]

    open_sides = jnp.zeros((pieces, LANES), F32)
    for band in range(1, bands, 2):
        above = (band + 1) % bands
        open_sides = open_sides + end_of(band) * field_of(above) + end_of(above) * field_of(band)
    open_sides = jnp.sum(jnp.sum(open_sides, axis=0, keepdims=True), axis=1, keepdims=True)
    lines = received_ref[pl.ds(pieces, orbits * bands, stride=rows), :]
    line = jnp.sum(lines, axis=0, keepdims=True)
    lane = lax.broadcasted_iota(jnp.int32, line.shape, 1)
    product, energy, cross, following = (
        jnp.sum(jnp.where(lane == index, line, 0.0), axis=1, keepdims=True) for index in range(4)
    )
    following = following - (2.0 * PRIOR_WEIGHT) * open_sides
    alpha = product / energy
    later = alpha * alpha * cross - product
    grown = 1.0 + later / product
    later_energy = alpha * alpha * following - grown * grown * energy
    later_alpha = later / later_energy
    on_start = alpha + later_alpha * grown
    on_next = -alpha * later_alpha

    normal = scattered_slots(orbits, scatter_ref, slot_refs, order_ref)
    second_ref[...] = base_ref[...] + normal.reshape(second_ref.shape)
    flip = parity()
    band = lax.axis_index("lon")
    across = lax.rem(band + jnp.where(flip, 1, bands - 1), bands)
    even_field, odd_field = sides(parity, next_ref[0], next_ref[columns - 1])
    near, far = near_far(parity, even_ref)
    even_first = rim_ref[2] * near - far - even_field - lat_pair(near[None])[0]
    odd_near = field_of(across)
    odd_first = end_of(across) - odd_field
    ends = (
        (0, 1, jnp.where(flip, near, odd_near), jnp.where(flip, even_first, odd_first)),
        (
            columns - 1,
            columns - 2,
            jnp.where(flip, odd_near, near),
            jnp.where(flip, odd_first, even_first),
        ),
    )
    for end, inner, field, first in ends:
        change = lat_pair(field[None])[0] - shifted_ref[end] * field - first
        second_ref[end] = second_ref[end] + PRIOR_WEIGHT * change
        second_ref[inner] = second_ref[inner] + PRIOR_WEIGHT * field

    out = on_start * start_ref[...] + on_next * next_ref[...]
    residual = right_ref[...] - on_start * first_ref[...] - on_next * second_ref[...]
    out_ref[...] = out.reshape(out_ref.shape)
    residual_ref[...] = residual.reshape(residual_ref.shape)


def per_device(orbits, bands, interp, obs_value, obs_weight, block_map, live_count, kappa2):
    slots, _, observations, width = interp.shape
    columns, latitudes = kappa2.shape
    pieces = latitudes // width
    cells = columns * pieces
    field_shape = (columns, pieces, width)

    def parity():
        return lax.rem(lax.axis_index("lon"), 2) == 1

    vmem = pl.BlockSpec(memory_space=pltpu.VMEM)
    smem = pl.BlockSpec(memory_space=pltpu.SMEM)
    anywhere = pl.BlockSpec(memory_space=pl.ANY)

    def call(kernel, outs, in_specs, scratch=(), name=None, limit=VMEM_BYTES, work=0):
        held = pltpu.VMEM if name not in ("combine", "edge_sums") else jax.ShapeDtypeStruct
        cost = pl.CostEstimate(flops=work, bytes_accessed=0, transcendentals=0) if work else None
        return pl.pallas_call(
            kernel,
            out_shape=tuple(held(shape, dtype) for shape, dtype in outs),
            in_specs=in_specs,
            out_specs=tuple(vmem for _ in outs),
            scratch_shapes=list(scratch),
            compiler_params=pltpu.CompilerParams(vmem_limit_bytes=limit),
            cost_estimate=cost,
            name=name,
        )

    def from_others(value):
        return [value] + [
            lax.ppermute(value, "orbit", [((i + step) % orbits, i) for i in range(orbits)])
            for step in range(1, orbits)
        ]

    even_pairs = [(i, i ^ 1) for i in range(bands)]
    odd_pairs = [(i, (i + 1 if i % 2 else i - 1) % bands) for i in range(bands)]

    matrices_in = interp.reshape(slots, observations, width)
    line = (slots, 1, observations)
    message, matrices, weights, pick = call(
        functools.partial(data_kernel, orbits),
        (
            ((2 * slots + GROUP, width), F32),
            ((slots, observations, width), BF16),
            ((slots, observations), F32),
            ((slots, cells), BF16),
        ),
        [smem] + [anywhere] * 4,
        [
            pltpu.SMEM((slots,), jnp.int32),
            pltpu.VMEM(line, F32),
            pltpu.VMEM(line, F32),
            pltpu.SemaphoreType.DMA((3 + slots // CHUNK,)),
        ],
        "data_terms",
        DATA_VMEM_BYTES,
    )(live_count, block_map.reshape(slots), matrices_in, obs_value, obs_weight)
    messages = from_others(message)
    shifted, blocks = call(
        block_kernel,
        ((field_shape, F32), ((slots // 2, 2 * width, 2 * width), BF16)),
        [vmem] * 3,
        (),
        "blocks",
        work=WORK,
    )(kappa2, matrices, weights)

    order = pltpu.VMEM((orbits * slots, width), F32)
    edge_width = -(-2 * orbits * slots // LANES) * LANES
    rim = ((3, pieces, width), F32)
    edge = ((2, pieces, width), F32)
    wide_edge = ((max(slots // pieces + 1, rim[0][0]), pieces, width), F32)
    field = (field_shape, F32)
    slot_terms = ((slots, width), F32)
    start, right_side, precond, scatter, even, odd = call(
        functools.partial(start_kernel, orbits, parity),
        (field, field, field, ((cells, edge_width), BF16), rim, wide_edge),
        [vmem] * (1 + orbits),
        [order],
        "start",
    )(shifted, *messages)
    rim_odd = lax.ppermute(odd, "lon", odd_pairs)
    terms, even = call(
        normal_kernel,
        (slot_terms, rim),
        [smem] + [vmem] * 4,
        (),
        "normal_start",
        work=WORK,
    )(live_count, pick, start, blocks, even)
    terms = from_others(terms)
    rim_even = lax.ppermute(even, "lon", even_pairs)
    image_inputs = (start, shifted, rim_even, rim_odd, scatter, precond, *terms)
    (even,) = call(
        functools.partial(pair_edge_kernel, parity, orbits),
        (edge,),
        [vmem] * (6 + orbits),
        [order],
        "pair_edge",
    )(*image_inputs)
    even = lax.ppermute(even, "lon", even_pairs)
    chunk = pieces + 1
    first, following, base, end, parts, chunks, terms = call(
        functools.partial(images_kernel, parity, orbits),
        (
            field,
            field,
            field,
            ((pieces, width), F32),
            ((4, width), F32),
            ((GROUP * chunk, width), F32),
            slot_terms,
        ),
        [vmem] * (9 + orbits),
        [order],
        "images",
        work=WORK,
    )(*image_inputs[:6], right_side, pick, blocks, *terms)
    terms = from_others(terms)
    message = ((orbits * bands * chunk, width), F32)
    (sums,) = call(
        functools.partial(edge_kernel, parity), (message,), [vmem] * 4, (), "edge_sums"
    )(even, end, parts, chunks)
    sums = lax.all_to_all(sums[:, None], ("orbit", "lon"), 0, 0, tiled=True)[:, 0]
    return call(
        functools.partial(last_kernel, parity, orbits, bands),
        ((kappa2.shape, F32), (kappa2.shape, F32)),
        [vmem] * (10 + orbits),
        [order, pltpu.VMEM(field_shape, F32)],
        "combine",
    )(
        sums, start, following, right_side, first, base, shifted, even, rim_even, scatter, *terms
    )


def solution(mesh):
    in_specs = (
        P("orbit", "lon", None, None),
        P("orbit", "lon", None),
        P("orbit", "lon", None),
        P("orbit", "lon"),
        P("orbit", "lon"),
        P("lon", None),
    )
    out_specs = (P("lon", None), P("lon", None))
    body = functools.partial(per_device, mesh.shape["orbit"], mesh.shape["lon"])
    return jax.shard_map(
        body, mesh=mesh, in_specs=in_specs, out_specs=out_specs, check_vma=False
    )
```

```python
import functools

import jax
import jax.numpy as jnp
from jax import lax
from jax.experimental import pallas as pl
from jax.experimental.pallas import tpu as pltpu
from jax.sharding import PartitionSpec as P

PRIOR_WEIGHT = 0.0625
GROUP = 8
LANES = 128
F32 = jnp.float32
BF16 = jnp.bfloat16
VMEM_BYTES = 48 * 1024 * 1024
DATA_VMEM_BYTES = 59 * 1024 * 1024
CHUNK = 8
WORK = 1 << 32


def two_terms(value):
    high = value.astype(BF16)
    low = (value - high.astype(F32)).astype(BF16)
    return high, low


def stacked_terms(value):
    return jnp.concatenate(two_terms(value), axis=0)


def fold_terms(product):
    half = product.shape[0] // 2
    return product[:half] + product[half:]


def dot(left, right):
    return lax.dot_general(left, right, (((1,), (0,)), ((), ())), preferred_element_type=F32)


def pick_row(total, product, slot):
    rows = lax.broadcasted_iota(jnp.int32, product.shape, 0)
    return jnp.where(rows == slot, product, total)


def lat_pair(field):
    pieces = field.shape[1]
    piece = lax.broadcasted_iota(jnp.int32, field.shape, 1)
    lane = lax.broadcasted_iota(jnp.int32, field.shape, 2)
    south = pltpu.roll(field, 1, 2)
    north = pltpu.roll(field, LANES - 1, 2)
    south_over = jnp.where(piece == 0, 0.0, pltpu.roll(south, 1, 1))
    north_over = jnp.where(piece == pieces - 1, 0.0, pltpu.roll(north, pieces - 1, 1))
    return jnp.where(lane == 0, south_over, south) + jnp.where(lane == LANES - 1, north_over, north)


def stencil(field, shifted):
    center = field[1:-1]
    return shifted * center - field[2:] - field[:-2] - lat_pair(center)


def data_kernel(
    orbits,
    count_ref,
    map_in,
    interp_in,
    value_in,
    weight_in,
    message_ref,
    matrices_ref,
    weight_ref,
    pick_ref,
    map_ref,
    value_rows,
    weight_rows,
    sems,
):
    slots = matrices_ref.shape[0]
    pairs = ((weight_in, weight_rows), (value_in, value_rows), (map_in, map_ref))
    small = [
        pltpu.make_async_copy(source, target, sems.at[index])
        for index, (source, target) in enumerate(pairs)
    ]
    large = []
    for index in range(slots // CHUNK):
        part = pl.ds(index * CHUNK, CHUNK)
        large.append(
            pltpu.make_async_copy(
                interp_in.at[part], matrices_ref.at[part], sems.at[len(small) + index]
            )
        )
    count = count_ref[0, 0]
    for copy in small:
        copy.start()
    for index, copy in enumerate(large):
        pl.when(index * CHUNK < count)(copy.start)
    for copy in small:
        copy.wait()
    orbit = lax.axis_index("orbit")
    total = orbits * slots
    place = lax.broadcasted_iota(jnp.int32, (GROUP, LANES), 0) * LANES
    place = place + lax.broadcasted_iota(jnp.int32, (GROUP, LANES), 1)
    slot_here = jnp.where(place >= total, place - total, place) - orbit * slots
    target_row = jnp.zeros((GROUP, LANES), jnp.int32)
    for slot in range(slots):
        live_target = jnp.where(slot < count, map_ref[slot] + 1, 0)
        target_row = jnp.where(slot_here == slot, live_target, target_row)
    target_row = jnp.where(place < 2 * total, target_row, 0)
    message_ref[pl.ds(2 * slots, GROUP), :] = target_row.astype(F32)
    row = lax.broadcasted_iota(jnp.int32, (GROUP, pick_ref.shape[1]), 0)
    cell = lax.broadcasted_iota(jnp.int32, row.shape, 1)
    for group in range(slots // GROUP):
        target = jnp.zeros(row.shape, jnp.int32)
        for slot in range(GROUP):
            index = group * GROUP + slot
            live_target = jnp.where(index < count, map_ref[index], -1)
            target = jnp.where(row == slot, live_target, target)
        part = pl.ds(group * GROUP, GROUP)
        pick_ref[part, :] = jnp.where(cell == target, 1.0, 0.0).astype(BF16)
    weight_ref[...] = weight_rows[:, 0, :]

    def work(index):
        large[index].wait()
        for group in range(index * CHUNK // GROUP, (index + 1) * CHUNK // GROUP):
            part = pl.ds(group * GROUP, GROUP)
            weights = weight_rows[part, 0, :]
            scaled = (weights * value_rows[part, 0, :]).astype(BF16)
            high, low = two_terms(weights)
            rows = jnp.concatenate([scaled, high, low, low], axis=0)
            first = jnp.zeros((GROUP, LANES), F32)
            second = jnp.zeros((GROUP, LANES), F32)
            for slot in range(GROUP):
                matrix = matrices_ref[group * GROUP + slot]
                both = dot(rows, jnp.concatenate([matrix, matrix * matrix], axis=1))
                squares = both[GROUP : 2 * GROUP, LANES:] + both[2 * GROUP : 3 * GROUP, LANES:]
                first = pick_row(first, both[:GROUP, :LANES], slot)
                second = pick_row(second, squares, slot)
            message_ref[part, :] = first
            message_ref[pl.ds(slots + group * GROUP, GROUP), :] = second

    def rest(index):
        part = pl.ds(index * CHUNK, CHUNK)
        matrices_ref[part] = jnp.zeros((CHUNK,) + matrices_ref.shape[1:], BF16)
        for start in (0, slots):
            part = pl.ds(start + index * CHUNK, CHUNK)
            message_ref[part, :] = jnp.zeros((CHUNK, LANES), F32)

    chunks = range(slots // CHUNK)
    for index in chunks:
        pl.when(index * CHUNK >= count)(functools.partial(rest, index))
    for index in chunks:
        pl.when(index * CHUNK < count)(functools.partial(work, index))


def block_kernel(count_ref, kappa_ref, matrices_ref, weight_ref, shifted_ref, blocks_ref):
    shifted_ref[...] = kappa_ref[...].reshape(shifted_ref.shape) + 4.0
    slots, _, width = matrices_ref.shape
    half = max(slots // (2 * GROUP), 1) * GROUP

    def work(used):
        for slot in range(used):
            matrix = matrices_ref[slot]
            weighted = matrix.T.astype(F32) * weight_ref[pl.ds(slot, 1), :]
            high, low = two_terms(fold_terms(dot(stacked_terms(weighted), matrix)))
            columns = pl.ds(slot % 2 * width, width)
            blocks_ref[slot // 2, pl.ds(0, width), columns] = high
            blocks_ref[slot // 2, pl.ds(width, width), columns] = low
        if used < slots:
            rest = (slots - used) // 2
            blocks_ref[pl.ds(used // 2, rest)] = jnp.zeros((rest,) + blocks_ref.shape[1:], BF16)

    few = count_ref[0, 0] <= half
    pl.when(few)(functools.partial(work, half))
    pl.when(jnp.logical_not(few))(functools.partial(work, slots))


def gather_messages(orbits, slots, message_refs, order_ref):
    orbit = lax.axis_index("orbit")
    for step in range(orbits):
        source = lax.rem(orbit + step, orbits)
        rows = pl.ds(pl.multiple_of(source * slots, slots), slots)
        order_ref[rows, :] = message_refs[step]


def start_kernel(
    orbits, parity, shifted_ref, *refs
):
    message_refs = refs[:orbits]
    (
        field_ref,
        right_ref,
        precond_ref,
        scatter_ref,
        even_ref,
        odd_ref,
        order_ref,
    ) = refs[orbits:]
    slots = (message_refs[0].shape[0] - GROUP) // 2
    cells = scatter_ref.shape[0]
    targets = message_refs[0][pl.ds(2 * slots, GROUP), :]
    for ref in message_refs[1:]:
        targets = targets + ref[pl.ds(2 * slots, GROUP), :]
    targets = targets.astype(jnp.int32) - 1
    row = lax.broadcasted_iota(jnp.int32, (cells, LANES), 0)
    for piece in range(scatter_ref.shape[1] // LANES):
        hit = row == targets[piece : piece + 1, :]
        scatter_ref[:, pl.ds(piece * LANES, LANES)] = jnp.where(hit, 1.0, 0.0).astype(BF16)
    sums = []
    for part in range(2):
        rows = pl.ds(part * slots, slots)
        gather_messages(orbits, slots, [ref[rows, :] for ref in message_refs], order_ref)
        sums.append(scattered(scatter_ref[...], order_ref[...]))
    right_side, obs_diag = (value.reshape(field_ref.shape) for value in sums)
    shifted = shifted_ref[...]
    precond = PRIOR_WEIGHT * (shifted * shifted + 4.0) + obs_diag
    field = right_side / precond
    right_ref[...] = right_side
    precond_ref[...] = precond
    field_ref[...] = field
    columns = field.shape[0]
    top = jnp.concatenate([field[:2], shifted[:1]], axis=0)
    bottom = jnp.concatenate([field[columns - 2 :], shifted[columns - 1 :]], axis=0)
    store_edges(parity, top, bottom, even_ref, odd_ref)


def normal_kernel(
    count_ref, pick_ref, field_ref, blocks_ref, even_ref, out_ref, even_out_ref
):
    even_out_ref[...] = even_ref[...]
    slots = pick_ref.shape[0]
    half = max(slots // (2 * GROUP), 1) * GROUP
    few = count_ref[0, 0] <= half

    @pl.when(few)
    def _():
        normal_slots(pick_ref, field_ref[...], blocks_ref, out_ref, half)

    @pl.when(jnp.logical_not(few))
    def _():
        normal_slots(pick_ref, field_ref[...], blocks_ref, out_ref)


def scattered(one_hot, slots):
    terms = stacked_terms(slots)
    spare = one_hot.shape[1] - terms.shape[0]
    if spare:
        terms = jnp.concatenate([terms, jnp.zeros((spare, LANES), BF16)], axis=0)
    return dot(one_hot, terms)


def store_edges(parity, top, bottom, even_ref, odd_ref):
    flip = parity()
    used = top.shape[0]
    even_ref[...] = jnp.where(flip, top, bottom)
    odd_ref[:used] = jnp.where(flip, bottom, top)
    if odd_ref.shape[0] > used:
        odd_ref[used:] = jnp.zeros((odd_ref.shape[0] - used,) + top.shape[1:], F32)


def load_edges(parity, even_ref, odd_ref):
    flip = parity()
    even = even_ref[...]
    odd = odd_ref[: even.shape[0]]
    return jnp.where(flip, even, odd), jnp.where(flip, odd, even)


def normal_slots(pick_ref, field, blocks_ref, out_ref, used=None):
    width = field.shape[-1]
    field = field.reshape(pick_ref.shape[1], width)
    used = used or pick_ref.shape[0]
    picked = dot(pick_ref[pl.ds(0, used), :], jnp.concatenate(two_terms(field), axis=1))
    picked = picked[:, :width] + picked[:, width:]
    energy = jnp.zeros((GROUP, width), F32)
    spare = pick_ref.shape[0] - used
    if spare:
        out_ref[pl.ds(used, spare), :] = jnp.zeros((spare, width), F32)
    for group in range(used // GROUP):
        cells = picked[group * GROUP : (group + 1) * GROUP]
        rows = stacked_terms(cells)
        rows = jnp.concatenate([rows, rows], axis=1)
        total = jnp.zeros((GROUP, width), F32)
        for slot in range(0, GROUP, 2):
            product = fold_terms(dot(rows, blocks_ref[(group * GROUP + slot) // 2]))
            total = pick_row(total, product[:, :width], slot)
            total = pick_row(total, product[:, width:], slot + 1)
        out_ref[pl.ds(group * GROUP, GROUP), :] = total
        energy = energy + cells * total
    return energy


def extended(field, top, bottom):
    return jnp.concatenate([top, field, bottom], axis=0)


def prior_parts(field, shifted, top, bottom, shifted_top, shifted_bottom):
    first = stencil(
        extended(field, top, bottom), extended(shifted, shifted_top, shifted_bottom)
    )
    return PRIOR_WEIGHT * stencil(first, shifted)


def scattered_slots(orbits, scatter_ref, slot_refs, order_ref):
    slots = slot_refs[0].shape[0]
    gather_messages(orbits, slots, [ref[...] for ref in slot_refs], order_ref)
    return scattered(scatter_ref[...], order_ref[...])


def pair_edge_kernel(
    parity,
    orbits,
    field_ref,
    shifted_ref,
    even_ref,
    odd_ref,
    scatter_ref,
    precond_ref,
    *refs,
):
    slot_refs = refs[:orbits]
    edge_ref, order_ref = refs[orbits:]
    slots = slot_refs[0].shape[0]
    gather_messages(orbits, slots, [ref[...] for ref in slot_refs], order_ref)
    columns, pieces, width = field_ref.shape
    flip = parity()
    top, bottom = load_edges(parity, even_ref, odd_ref)
    field = jnp.where(
        flip,
        extended(field_ref[pl.ds(0, 2)], top[:2], field_ref[pl.ds(2, 2)]),
        extended(field_ref[pl.ds(columns - 2, 2)], field_ref[pl.ds(columns - 4, 2)], bottom[:2]),
    )
    shifted = jnp.where(
        flip,
        jnp.concatenate([top[2:], shifted_ref[pl.ds(0, 3)]], axis=0),
        jnp.concatenate([shifted_ref[pl.ds(columns - 3, 3)], bottom[2:]], axis=0),
    )
    once = stencil(field, shifted)
    twice = stencil(once, shifted[1:-1])
    start = jnp.where(flip, 0, columns - 2)
    rows = pl.ds(pl.multiple_of(start * pieces, 2 * pieces), 2 * pieces)
    normal = scattered(scatter_ref[rows, :], order_ref[...]).reshape(twice.shape)
    edge_ref[...] = (PRIOR_WEIGHT * twice + normal) / precond_ref[pl.ds(start, 2)]


def alone(field, shifted):
    zero = jnp.zeros((1,) + field.shape[1:], F32)
    return stencil(extended(field, zero, zero), shifted)


def sides(parity, top, bottom):
    flip = parity()
    return jnp.where(flip, top, bottom), jnp.where(flip, bottom, top)


def near_far(parity, even_ref):
    flip = parity()
    return jnp.where(flip, even_ref[1], even_ref[0]), jnp.where(flip, even_ref[0], even_ref[1])


def chunks_of(rows):
    return jnp.concatenate([rows] * GROUP, axis=0)


def images_kernel(
    parity,
    orbits,
    field_ref,
    shifted_ref,
    even_ref,
    odd_ref,
    scatter_ref,
    precond_ref,
    right_ref,
    pick_ref,
    blocks_ref,
    *refs,
):
    slot_refs = refs[:orbits]
    image_ref, next_ref, base_ref, end_ref, parts_ref, chunks_ref, out_ref, order_ref = refs[orbits:]
    normal = scattered_slots(orbits, scatter_ref, slot_refs, order_ref)
    top, bottom = load_edges(parity, even_ref, odd_ref)
    start, shifted = field_ref[...], shifted_ref[...]
    prior = prior_parts(start, shifted, top[:2], bottom[:2], top[2:], bottom[2:])
    image = prior + normal.reshape(start.shape)
    field = image / precond_ref[...]
    image_ref[...] = image
    next_ref[...] = field
    energy = normal_slots(pick_ref, field, blocks_ref, out_ref)
    once = alone(field, shifted)
    base_ref[...] = PRIOR_WEIGHT * alone(once, shifted)
    last = once.shape[0] - 1
    even_end, odd_end = sides(parity, once[0], once[last])
    _, odd_field = sides(parity, field[0], field[last])
    end_ref[...] = even_end
    orbit = lax.axis_index("orbit")
    own = jnp.where(orbit == 0, 1.0, 0.0)
    squares = jnp.sum(once * once, axis=0) + odd_field * odd_field
    parts = (
        own * jnp.sum(right_ref[...] * start, axis=0),
        own * jnp.sum(start * image, axis=0),
        own * jnp.sum(image * field, axis=0),
        own * PRIOR_WEIGHT * squares + energy,
    )
    for index, part in enumerate(parts):
        parts_ref[pl.ds(index, 1), :] = jnp.sum(part, axis=0, keepdims=True)
    edge = jnp.where(orbit == 0, odd_end, odd_field)
    chunks_ref[...] = chunks_of(jnp.concatenate([edge, jnp.zeros((1, LANES), F32)], axis=0))


def edge_kernel(parity, even_ref, end_ref, parts_ref, chunks_ref, message_ref):
    near, _ = near_far(parity, even_ref)
    own = jnp.where(lax.axis_index("orbit") == 0, PRIOR_WEIGHT, 0.0)
    more = own * jnp.sum(near * (near - 2.0 * end_ref[...]), axis=0, keepdims=True)
    index = lax.broadcasted_iota(jnp.int32, (4, LANES), 0)
    lane = lax.broadcasted_iota(jnp.int32, (4, LANES), 1)
    sums = jnp.sum(parts_ref[...] + jnp.where(index == 3, more, 0.0), axis=1, keepdims=True)
    line = jnp.sum(jnp.where(lane == index, sums, 0.0), axis=0, keepdims=True)
    rows = chunks_ref.shape[0]
    period = rows // GROUP
    row = lax.broadcasted_iota(jnp.int32, (rows, LANES), 0)
    chunks = jnp.where(lax.rem(row, period) == period - 1, line, chunks_ref[...])
    for index in range(message_ref.shape[0] // rows):
        message_ref[pl.ds(index * rows, rows), :] = chunks


def last_kernel(
    parity,
    orbits,
    bands,
    received_ref,
    start_ref,
    next_ref,
    right_ref,
    first_ref,
    base_ref,
    shifted_ref,
    even_ref,
    rim_ref,
    scatter_ref,
    *refs,
):
    slot_refs = refs[:orbits]
    out_ref, residual_ref, order_ref, second_ref = refs[orbits:]
    columns, pieces, _ = start_ref.shape
    rows = pieces + 1

    def end_of(band):
        return received_ref[pl.ds(band * rows, pieces), :]

    def field_of(band):
        return received_ref[pl.ds((bands + band) * rows, pieces), :]

    open_sides = jnp.zeros((pieces, LANES), F32)
    for band in range(1, bands, 2):
        above = (band + 1) % bands
        open_sides = open_sides + end_of(band) * field_of(above) + end_of(above) * field_of(band)
    open_sides = jnp.sum(jnp.sum(open_sides, axis=0, keepdims=True), axis=1, keepdims=True)
    lines = received_ref[pl.ds(pieces, orbits * bands, stride=rows), :]
    line = jnp.sum(lines, axis=0, keepdims=True)
    lane = lax.broadcasted_iota(jnp.int32, line.shape, 1)
    product, energy, cross, following = (
        jnp.sum(jnp.where(lane == index, line, 0.0), axis=1, keepdims=True) for index in range(4)
    )
    following = following - (2.0 * PRIOR_WEIGHT) * open_sides
    alpha = product / energy
    later = alpha * alpha * cross - product
    grown = 1.0 + later / product
    later_energy = alpha * alpha * following - grown * grown * energy
    later_alpha = later / later_energy
    on_start = alpha + later_alpha * grown
    on_next = -alpha * later_alpha

    normal = scattered_slots(orbits, scatter_ref, slot_refs, order_ref)
    second_ref[...] = base_ref[...] + normal.reshape(second_ref.shape)
    flip = parity()
    band = lax.axis_index("lon")
    across = lax.rem(band + jnp.where(flip, 1, bands - 1), bands)
    even_field, odd_field = sides(parity, next_ref[0], next_ref[columns - 1])
    near, far = near_far(parity, even_ref)
    even_first = rim_ref[2] * near - far - even_field - lat_pair(near[None])[0]
    odd_near = field_of(across)
    odd_first = end_of(across) - odd_field
    ends = (
        (0, 1, jnp.where(flip, near, odd_near), jnp.where(flip, even_first, odd_first)),
        (
            columns - 1,
            columns - 2,
            jnp.where(flip, odd_near, near),
            jnp.where(flip, odd_first, even_first),
        ),
    )
    for end, inner, field, first in ends:
        change = lat_pair(field[None])[0] - shifted_ref[end] * field - first
        second_ref[end] = second_ref[end] + PRIOR_WEIGHT * change
        second_ref[inner] = second_ref[inner] + PRIOR_WEIGHT * field

    out = on_start * start_ref[...] + on_next * next_ref[...]
    residual = right_ref[...] - on_start * first_ref[...] - on_next * second_ref[...]
    out_ref[...] = out.reshape(out_ref.shape)
    residual_ref[...] = residual.reshape(residual_ref.shape)


def per_device(orbits, bands, interp, obs_value, obs_weight, block_map, live_count, kappa2):
    slots, _, observations, width = interp.shape
    columns, latitudes = kappa2.shape
    pieces = latitudes // width
    cells = columns * pieces
    field_shape = (columns, pieces, width)

    def parity():
        return lax.rem(lax.axis_index("lon"), 2) == 1

    vmem = pl.BlockSpec(memory_space=pltpu.VMEM)
    smem = pl.BlockSpec(memory_space=pltpu.SMEM)
    anywhere = pl.BlockSpec(memory_space=pl.ANY)

    def call(kernel, outs, in_specs, scratch=(), name=None, limit=VMEM_BYTES, work=0):
        held = pltpu.VMEM if name not in ("combine", "edge_sums") else jax.ShapeDtypeStruct
        cost = pl.CostEstimate(flops=work, bytes_accessed=0, transcendentals=0) if work else None
        return pl.pallas_call(
            kernel,
            out_shape=tuple(held(shape, dtype) for shape, dtype in outs),
            in_specs=in_specs,
            out_specs=tuple(vmem for _ in outs),
            scratch_shapes=list(scratch),
            compiler_params=pltpu.CompilerParams(vmem_limit_bytes=limit),
            cost_estimate=cost,
            name=name,
        )

    def from_others(value):
        return [value] + [
            lax.ppermute(value, "orbit", [((i + step) % orbits, i) for i in range(orbits)])
            for step in range(1, orbits)
        ]

    even_pairs = [(i, i ^ 1) for i in range(bands)]
    odd_pairs = [(i, (i + 1 if i % 2 else i - 1) % bands) for i in range(bands)]

    matrices_in = interp.reshape(slots, observations, width)
    line = (slots, 1, observations)
    message, matrices, weights, pick = call(
        functools.partial(data_kernel, orbits),
        (
            ((2 * slots + GROUP, width), F32),
            ((slots, observations, width), BF16),
            ((slots, observations), F32),
            ((slots, cells), BF16),
        ),
        [smem] + [anywhere] * 4,
        [
            pltpu.SMEM((slots,), jnp.int32),
            pltpu.VMEM(line, F32),
            pltpu.VMEM(line, F32),
            pltpu.SemaphoreType.DMA((3 + slots // CHUNK,)),
        ],
        "data_terms",
        DATA_VMEM_BYTES,
    )(live_count, block_map.reshape(slots), matrices_in, obs_value, obs_weight)
    messages = from_others(message)
    shifted, blocks = call(
        block_kernel,
        ((field_shape, F32), ((slots // 2, 2 * width, 2 * width), BF16)),
        [smem] + [vmem] * 3,
        (),
        "blocks",
        work=WORK,
    )(live_count, kappa2, matrices, weights)

    order = pltpu.VMEM((orbits * slots, width), F32)
    edge_width = -(-2 * orbits * slots // LANES) * LANES
    rim = ((3, pieces, width), F32)
    edge = ((2, pieces, width), F32)
    wide_edge = ((max(slots // pieces + 1, rim[0][0]), pieces, width), F32)
    field = (field_shape, F32)
    slot_terms = ((slots, width), F32)
    start, right_side, precond, scatter, even, odd = call(
        functools.partial(start_kernel, orbits, parity),
        (field, field, field, ((cells, edge_width), BF16), rim, wide_edge),
        [vmem] * (1 + orbits),
        [order],
        "start",
    )(shifted, *messages)
    rim_odd = lax.ppermute(odd, "lon", odd_pairs)
    terms, even = call(
        normal_kernel,
        (slot_terms, rim),
        [smem] + [vmem] * 4,
        (),
        "normal_start",
        work=WORK,
    )(live_count, pick, start, blocks, even)
    terms = from_others(terms)
    rim_even = lax.ppermute(even, "lon", even_pairs)
    image_inputs = (start, shifted, rim_even, rim_odd, scatter, precond, *terms)
    (even,) = call(
        functools.partial(pair_edge_kernel, parity, orbits),
        (edge,),
        [vmem] * (6 + orbits),
        [order],
        "pair_edge",
    )(*image_inputs)
    even = lax.ppermute(even, "lon", even_pairs)
    chunk = pieces + 1
    first, following, base, end, parts, chunks, terms = call(
        functools.partial(images_kernel, parity, orbits),
        (
            field,
            field,
            field,
            ((pieces, width), F32),
            ((4, width), F32),
            ((GROUP * chunk, width), F32),
            slot_terms,
        ),
        [vmem] * (9 + orbits),
        [order],
        "images",
        work=WORK,
    )(*image_inputs[:6], right_side, pick, blocks, *terms)
    terms = from_others(terms)
    message = ((orbits * bands * chunk, width), F32)
    (sums,) = call(
        functools.partial(edge_kernel, parity), (message,), [vmem] * 4, (), "edge_sums"
    )(even, end, parts, chunks)
    sums = lax.all_to_all(sums[:, None], ("orbit", "lon"), 0, 0, tiled=True)[:, 0]
    return call(
        functools.partial(last_kernel, parity, orbits, bands),
        ((kappa2.shape, F32), (kappa2.shape, F32)),
        [vmem] * (10 + orbits),
        [order, pltpu.VMEM(field_shape, F32)],
        "combine",
    )(
        sums, start, following, right_side, first, base, shifted, even, rim_even, scatter, *terms
    )


def solution(mesh):
    in_specs = (
        P("orbit", "lon", None, None),
        P("orbit", "lon", None),
        P("orbit", "lon", None),
        P("orbit", "lon"),
        P("orbit", "lon"),
        P("lon", None),
    )
    out_specs = (P("lon", None), P("lon", None))
    body = functools.partial(per_device, mesh.shape["orbit"], mesh.shape["lon"])
    return jax.shard_map(
        body, mesh=mesh, in_specs=in_specs, out_specs=out_specs, check_vma=False
    )
```

```python
import functools

import jax
import jax.numpy as jnp
from jax import lax
from jax.experimental import pallas as pl
from jax.experimental.pallas import tpu as pltpu
from jax.sharding import PartitionSpec as P

PRIOR_WEIGHT = 0.0625
GROUP = 8
LANES = 128
F32 = jnp.float32
BF16 = jnp.bfloat16
VMEM_BYTES = 48 * 1024 * 1024
DATA_VMEM_BYTES = 59 * 1024 * 1024
CHUNK = 8
WORK = 1 << 32


def two_terms(value):
    high = value.astype(BF16)
    low = (value - high.astype(F32)).astype(BF16)
    return high, low


def stacked_terms(value):
    return jnp.concatenate(two_terms(value), axis=0)


def fold_terms(product):
    half = product.shape[0] // 2
    return product[:half] + product[half:]


def dot(left, right):
    return lax.dot_general(left, right, (((1,), (0,)), ((), ())), preferred_element_type=F32)


def pick_row(total, product, slot):
    rows = lax.broadcasted_iota(jnp.int32, product.shape, 0)
    return jnp.where(rows == slot, product, total)


def lat_pair(field):
    pieces = field.shape[1]
    piece = lax.broadcasted_iota(jnp.int32, field.shape, 1)
    lane = lax.broadcasted_iota(jnp.int32, field.shape, 2)
    south = pltpu.roll(field, 1, 2)
    north = pltpu.roll(field, LANES - 1, 2)
    south_over = jnp.where(piece == 0, 0.0, pltpu.roll(south, 1, 1))
    north_over = jnp.where(piece == pieces - 1, 0.0, pltpu.roll(north, pieces - 1, 1))
    return jnp.where(lane == 0, south_over, south) + jnp.where(lane == LANES - 1, north_over, north)


def stencil(field, shifted):
    center = field[1:-1]
    return shifted * center - field[2:] - field[:-2] - lat_pair(center)


def data_kernel(
    orbits,
    count_ref,
    map_in,
    interp_in,
    value_in,
    weight_in,
    message_ref,
    matrices_ref,
    weight_ref,
    pick_ref,
    map_ref,
    value_rows,
    weight_rows,
    sems,
):
    slots = matrices_ref.shape[0]
    pairs = ((weight_in, weight_rows), (value_in, value_rows), (map_in, map_ref))
    small = [
        pltpu.make_async_copy(source, target, sems.at[index])
        for index, (source, target) in enumerate(pairs)
    ]
    large = []
    for index in range(slots // CHUNK):
        part = pl.ds(index * CHUNK, CHUNK)
        large.append(
            pltpu.make_async_copy(
                interp_in.at[part], matrices_ref.at[part], sems.at[len(small) + index]
            )
        )
    count = count_ref[0, 0]
    for copy in small:
        copy.start()
    for index, copy in enumerate(large):
        pl.when(index * CHUNK < count)(copy.start)
    for copy in small:
        copy.wait()
    orbit = lax.axis_index("orbit")
    total = orbits * slots
    place = lax.broadcasted_iota(jnp.int32, (GROUP, LANES), 0) * LANES
    place = place + lax.broadcasted_iota(jnp.int32, (GROUP, LANES), 1)
    slot_here = jnp.where(place >= total, place - total, place) - orbit * slots
    target_row = jnp.zeros((GROUP, LANES), jnp.int32)
    for slot in range(slots):
        live_target = jnp.where(slot < count, map_ref[slot] + 1, 0)
        target_row = jnp.where(slot_here == slot, live_target, target_row)
    target_row = jnp.where(place < 2 * total, target_row, 0)
    message_ref[pl.ds(2 * slots, GROUP), :] = target_row.astype(F32)
    row = lax.broadcasted_iota(jnp.int32, (GROUP, pick_ref.shape[1]), 0)
    cell = lax.broadcasted_iota(jnp.int32, row.shape, 1)
    for group in range(slots // GROUP):
        target = jnp.zeros(row.shape, jnp.int32)
        for slot in range(GROUP):
            index = group * GROUP + slot
            live_target = jnp.where(index < count, map_ref[index], -1)
            target = jnp.where(row == slot, live_target, target)
        part = pl.ds(group * GROUP, GROUP)
        pick_ref[part, :] = jnp.where(cell == target, 1.0, 0.0).astype(BF16)
    weight_ref[...] = weight_rows[:, 0, :]

    def work(index):
        large[index].wait()
        for group in range(index * CHUNK // GROUP, (index + 1) * CHUNK // GROUP):
            part = pl.ds(group * GROUP, GROUP)
            weights = weight_rows[part, 0, :]
            scaled = (weights * value_rows[part, 0, :]).astype(BF16)
            high, low = two_terms(weights)
            rows = jnp.concatenate([scaled, high, low, low], axis=0)
            first = jnp.zeros((GROUP, LANES), F32)
            second = jnp.zeros((GROUP, LANES), F32)
            for slot in range(GROUP):
                matrix = matrices_ref[group * GROUP + slot]
                both = dot(rows, jnp.concatenate([matrix, matrix * matrix], axis=1))
                squares = both[GROUP : 2 * GROUP, LANES:] + both[2 * GROUP : 3 * GROUP, LANES:]
                first = pick_row(first, both[:GROUP, :LANES], slot)
                second = pick_row(second, squares, slot)
            message_ref[part, :] = first
            message_ref[pl.ds(slots + group * GROUP, GROUP), :] = second

    def rest(index):
        part = pl.ds(index * CHUNK, CHUNK)
        matrices_ref[part] = jnp.zeros((CHUNK,) + matrices_ref.shape[1:], BF16)
        for start in (0, slots):
            part = pl.ds(start + index * CHUNK, CHUNK)
            message_ref[part, :] = jnp.zeros((CHUNK, LANES), F32)

    chunks = range(slots // CHUNK)
    for index in chunks:
        pl.when(index * CHUNK >= count)(functools.partial(rest, index))
    for index in chunks:
        pl.when(index * CHUNK < count)(functools.partial(work, index))


def block_kernel(kappa_ref, matrices_ref, weight_ref, shifted_ref, blocks_ref):
    shifted_ref[...] = kappa_ref[...].reshape(shifted_ref.shape) + 4.0
    width = matrices_ref.shape[2]
    for slot in range(matrices_ref.shape[0]):
        matrix = matrices_ref[slot]
        weighted = matrix.T.astype(F32) * weight_ref[pl.ds(slot, 1), :]
        high, low = two_terms(fold_terms(dot(stacked_terms(weighted), matrix)))
        columns = pl.ds(slot % 2 * width, width)
        blocks_ref[slot // 2, pl.ds(0, width), columns] = high
        blocks_ref[slot // 2, pl.ds(width, width), columns] = low


def gather_messages(orbits, slots, message_refs, order_ref):
    orbit = lax.axis_index("orbit")
    for step in range(orbits):
        source = lax.rem(orbit + step, orbits)
        rows = pl.ds(pl.multiple_of(source * slots, slots), slots)
        order_ref[rows, :] = message_refs[step]


def start_kernel(
    orbits, parity, ahead, shifted_ref, pick_ref, blocks_ref, *refs
):
    message_refs = refs[:orbits]
    (
        field_ref,
        right_ref,
        precond_ref,
        scatter_ref,
        even_ref,
        odd_ref,
        out_ref,
        order_ref,
    ) = refs[orbits:]
    slots = (message_refs[0].shape[0] - GROUP) // 2
    cells = scatter_ref.shape[0]
    targets = message_refs[0][pl.ds(2 * slots, GROUP), :]
    for ref in message_refs[1:]:
        targets = targets + ref[pl.ds(2 * slots, GROUP), :]
    targets = targets.astype(jnp.int32) - 1
    row = lax.broadcasted_iota(jnp.int32, (cells, LANES), 0)
    for piece in range(scatter_ref.shape[1] // LANES):
        hit = row == targets[piece : piece + 1, :]
        scatter_ref[:, pl.ds(piece * LANES, LANES)] = jnp.where(hit, 1.0, 0.0).astype(BF16)
    sums = []
    for part in range(2):
        rows = pl.ds(part * slots, slots)
        gather_messages(orbits, slots, [ref[rows, :] for ref in message_refs], order_ref)
        sums.append(scattered(scatter_ref[...], order_ref[...]))
    right_side, obs_diag = (value.reshape(field_ref.shape) for value in sums)
    shifted = shifted_ref[...]
    precond = PRIOR_WEIGHT * (shifted * shifted + 4.0) + obs_diag
    field = right_side / precond
    right_ref[...] = right_side
    precond_ref[...] = precond
    field_ref[...] = field
    columns = field.shape[0]
    top = jnp.concatenate([field[:2], shifted[:1]], axis=0)
    bottom = jnp.concatenate([field[columns - 2 :], shifted[columns - 1 :]], axis=0)
    store_edges(parity, top, bottom, even_ref, odd_ref)

    @pl.when(ahead())
    def _():
        normal_slots(pick_ref, field_ref[...], blocks_ref, out_ref)


def normal_kernel(
    ahead, count_ref, pick_ref, field_ref, blocks_ref, even_ref, done_ref, out_ref, even_out_ref
):
    even_out_ref[...] = even_ref[...]
    first = ahead()
    slots = pick_ref.shape[0]
    half = max(slots // (2 * GROUP), 1) * GROUP
    few = count_ref[0, 0] <= half

    @pl.when(first)
    def _():
        out_ref[...] = done_ref[...]

    @pl.when(jnp.logical_and(jnp.logical_not(first), few))
    def _():
        normal_slots(pick_ref, field_ref[...], blocks_ref, out_ref, half)

    @pl.when(jnp.logical_not(jnp.logical_or(first, few)))
    def _():
        normal_slots(pick_ref, field_ref[...], blocks_ref, out_ref)


def scattered(one_hot, slots):
    terms = stacked_terms(slots)
    spare = one_hot.shape[1] - terms.shape[0]
    if spare:
        terms = jnp.concatenate([terms, jnp.zeros((spare, LANES), BF16)], axis=0)
    return dot(one_hot, terms)


def store_edges(parity, top, bottom, even_ref, odd_ref):
    flip = parity()
    used = top.shape[0]
    even_ref[...] = jnp.where(flip, top, bottom)
    odd_ref[:used] = jnp.where(flip, bottom, top)
    if odd_ref.shape[0] > used:
        odd_ref[used:] = jnp.zeros((odd_ref.shape[0] - used,) + top.shape[1:], F32)


def load_edges(parity, even_ref, odd_ref):
    flip = parity()
    even = even_ref[...]
    odd = odd_ref[: even.shape[0]]
    return jnp.where(flip, even, odd), jnp.where(flip, odd, even)


def normal_slots(pick_ref, field, blocks_ref, out_ref, used=None):
    width = field.shape[-1]
    field = field.reshape(pick_ref.shape[1], width)
    used = used or pick_ref.shape[0]
    picked = dot(pick_ref[pl.ds(0, used), :], jnp.concatenate(two_terms(field), axis=1))
    picked = picked[:, :width] + picked[:, width:]
    energy = jnp.zeros((GROUP, width), F32)
    spare = pick_ref.shape[0] - used
    if spare:
        out_ref[pl.ds(used, spare), :] = jnp.zeros((spare, width), F32)
    for group in range(used // GROUP):
        cells = picked[group * GROUP : (group + 1) * GROUP]
        rows = stacked_terms(cells)
        rows = jnp.concatenate([rows, rows], axis=1)
        total = jnp.zeros((GROUP, width), F32)
        for slot in range(0, GROUP, 2):
            product = fold_terms(dot(rows, blocks_ref[(group * GROUP + slot) // 2]))
            total = pick_row(total, product[:, :width], slot)
            total = pick_row(total, product[:, width:], slot + 1)
        out_ref[pl.ds(group * GROUP, GROUP), :] = total
        energy = energy + cells * total
    return energy


def extended(field, top, bottom):
    return jnp.concatenate([top, field, bottom], axis=0)


def prior_parts(field, shifted, top, bottom, shifted_top, shifted_bottom):
    first = stencil(
        extended(field, top, bottom), extended(shifted, shifted_top, shifted_bottom)
    )
    return PRIOR_WEIGHT * stencil(first, shifted)


def scattered_slots(orbits, scatter_ref, slot_refs, order_ref):
    slots = slot_refs[0].shape[0]
    gather_messages(orbits, slots, [ref[...] for ref in slot_refs], order_ref)
    return scattered(scatter_ref[...], order_ref[...])


def pair_edge_kernel(
    parity,
    orbits,
    field_ref,
    shifted_ref,
    even_ref,
    odd_ref,
    scatter_ref,
    precond_ref,
    *refs,
):
    slot_refs = refs[:orbits]
    edge_ref, order_ref = refs[orbits:]
    slots = slot_refs[0].shape[0]
    gather_messages(orbits, slots, [ref[...] for ref in slot_refs], order_ref)
    columns, pieces, width = field_ref.shape
    flip = parity()
    top, bottom = load_edges(parity, even_ref, odd_ref)
    field = jnp.where(
        flip,
        extended(field_ref[pl.ds(0, 2)], top[:2], field_ref[pl.ds(2, 2)]),
        extended(field_ref[pl.ds(columns - 2, 2)], field_ref[pl.ds(columns - 4, 2)], bottom[:2]),
    )
    shifted = jnp.where(
        flip,
        jnp.concatenate([top[2:], shifted_ref[pl.ds(0, 3)]], axis=0),
        jnp.concatenate([shifted_ref[pl.ds(columns - 3, 3)], bottom[2:]], axis=0),
    )
    once = stencil(field, shifted)
    twice = stencil(once, shifted[1:-1])
    start = jnp.where(flip, 0, columns - 2)
    rows = pl.ds(pl.multiple_of(start * pieces, 2 * pieces), 2 * pieces)
    normal = scattered(scatter_ref[rows, :], order_ref[...]).reshape(twice.shape)
    edge_ref[...] = (PRIOR_WEIGHT * twice + normal) / precond_ref[pl.ds(start, 2)]


def alone(field, shifted):
    zero = jnp.zeros((1,) + field.shape[1:], F32)
    return stencil(extended(field, zero, zero), shifted)


def sides(parity, top, bottom):
    flip = parity()
    return jnp.where(flip, top, bottom), jnp.where(flip, bottom, top)


def near_far(parity, even_ref):
    flip = parity()
    return jnp.where(flip, even_ref[1], even_ref[0]), jnp.where(flip, even_ref[0], even_ref[1])


def chunks_of(rows):
    return jnp.concatenate([rows] * GROUP, axis=0)


def images_kernel(
    parity,
    orbits,
    field_ref,
    shifted_ref,
    even_ref,
    odd_ref,
    scatter_ref,
    precond_ref,
    right_ref,
    pick_ref,
    blocks_ref,
    *refs,
):
    slot_refs = refs[:orbits]
    image_ref, next_ref, base_ref, end_ref, parts_ref, chunks_ref, out_ref, order_ref = refs[orbits:]
    normal = scattered_slots(orbits, scatter_ref, slot_refs, order_ref)
    top, bottom = load_edges(parity, even_ref, odd_ref)
    start, shifted = field_ref[...], shifted_ref[...]
    prior = prior_parts(start, shifted, top[:2], bottom[:2], top[2:], bottom[2:])
    image = prior + normal.reshape(start.shape)
    field = image / precond_ref[...]
    image_ref[...] = image
    next_ref[...] = field
    energy = normal_slots(pick_ref, field, blocks_ref, out_ref)
    once = alone(field, shifted)
    base_ref[...] = PRIOR_WEIGHT * alone(once, shifted)
    last = once.shape[0] - 1
    even_end, odd_end = sides(parity, once[0], once[last])
    _, odd_field = sides(parity, field[0], field[last])
    end_ref[...] = even_end
    orbit = lax.axis_index("orbit")
    own = jnp.where(orbit == 0, 1.0, 0.0)
    squares = jnp.sum(once * once, axis=0) + odd_field * odd_field
    parts = (
        own * jnp.sum(right_ref[...] * start, axis=0),
        own * jnp.sum(start * image, axis=0),
        own * jnp.sum(image * field, axis=0),
        own * PRIOR_WEIGHT * squares + energy,
    )
    for index, part in enumerate(parts):
        parts_ref[pl.ds(index, 1), :] = jnp.sum(part, axis=0, keepdims=True)
    edge = jnp.where(orbit == 0, odd_end, odd_field)
    chunks_ref[...] = chunks_of(jnp.concatenate([edge, jnp.zeros((1, LANES), F32)], axis=0))


def edge_kernel(parity, even_ref, end_ref, parts_ref, chunks_ref, message_ref):
    near, _ = near_far(parity, even_ref)
    own = jnp.where(lax.axis_index("orbit") == 0, PRIOR_WEIGHT, 0.0)
    more = own * jnp.sum(near * (near - 2.0 * end_ref[...]), axis=0, keepdims=True)
    index = lax.broadcasted_iota(jnp.int32, (4, LANES), 0)
    lane = lax.broadcasted_iota(jnp.int32, (4, LANES), 1)
    sums = jnp.sum(parts_ref[...] + jnp.where(index == 3, more, 0.0), axis=1, keepdims=True)
    line = jnp.sum(jnp.where(lane == index, sums, 0.0), axis=0, keepdims=True)
    rows = chunks_ref.shape[0]
    period = rows // GROUP
    row = lax.broadcasted_iota(jnp.int32, (rows, LANES), 0)
    chunks = jnp.where(lax.rem(row, period) == period - 1, line, chunks_ref[...])
    for index in range(message_ref.shape[0] // rows):
        message_ref[pl.ds(index * rows, rows), :] = chunks


def last_kernel(
    parity,
    orbits,
    bands,
    received_ref,
    start_ref,
    next_ref,
    right_ref,
    first_ref,
    base_ref,
    shifted_ref,
    even_ref,
    rim_ref,
    scatter_ref,
    *refs,
):
    slot_refs = refs[:orbits]
    out_ref, residual_ref, order_ref, second_ref = refs[orbits:]
    columns, pieces, _ = start_ref.shape
    rows = pieces + 1

    def end_of(band):
        return received_ref[pl.ds(band * rows, pieces), :]

    def field_of(band):
        return received_ref[pl.ds((bands + band) * rows, pieces), :]

    open_sides = jnp.zeros((pieces, LANES), F32)
    for band in range(1, bands, 2):
        above = (band + 1) % bands
        open_sides = open_sides + end_of(band) * field_of(above) + end_of(above) * field_of(band)
    open_sides = jnp.sum(jnp.sum(open_sides, axis=0, keepdims=True), axis=1, keepdims=True)
    lines = received_ref[pl.ds(pieces, orbits * bands, stride=rows), :]
    line = jnp.sum(lines, axis=0, keepdims=True)
    lane = lax.broadcasted_iota(jnp.int32, line.shape, 1)
    product, energy, cross, following = (
        jnp.sum(jnp.where(lane == index, line, 0.0), axis=1, keepdims=True) for index in range(4)
    )
    following = following - (2.0 * PRIOR_WEIGHT) * open_sides
    alpha = product / energy
    later = alpha * alpha * cross - product
    grown = 1.0 + later / product
    later_energy = alpha * alpha * following - grown * grown * energy
    later_alpha = later / later_energy
    on_start = alpha + later_alpha * grown
    on_next = -alpha * later_alpha

    normal = scattered_slots(orbits, scatter_ref, slot_refs, order_ref)
    second_ref[...] = base_ref[...] + normal.reshape(second_ref.shape)
    flip = parity()
    band = lax.axis_index("lon")
    across = lax.rem(band + jnp.where(flip, 1, bands - 1), bands)
    even_field, odd_field = sides(parity, next_ref[0], next_ref[columns - 1])
    near, far = near_far(parity, even_ref)
    even_first = rim_ref[2] * near - far - even_field - lat_pair(near[None])[0]
    odd_near = field_of(across)
    odd_first = end_of(across) - odd_field
    ends = (
        (0, 1, jnp.where(flip, near, odd_near), jnp.where(flip, even_first, odd_first)),
        (
            columns - 1,
            columns - 2,
            jnp.where(flip, odd_near, near),
            jnp.where(flip, odd_first, even_first),
        ),
    )
    for end, inner, field, first in ends:
        change = lat_pair(field[None])[0] - shifted_ref[end] * field - first
        second_ref[end] = second_ref[end] + PRIOR_WEIGHT * change
        second_ref[inner] = second_ref[inner] + PRIOR_WEIGHT * field

    out = on_start * start_ref[...] + on_next * next_ref[...]
    residual = right_ref[...] - on_start * first_ref[...] - on_next * second_ref[...]
    out_ref[...] = out.reshape(out_ref.shape)
    residual_ref[...] = residual.reshape(residual_ref.shape)


def per_device(orbits, bands, interp, obs_value, obs_weight, block_map, live_count, kappa2):
    slots, _, observations, width = interp.shape
    columns, latitudes = kappa2.shape
    pieces = latitudes // width
    cells = columns * pieces
    field_shape = (columns, pieces, width)

    def parity():
        return lax.rem(lax.axis_index("lon"), 2) == 1

    def ahead():
        return lax.axis_index("lon") == 0

    vmem = pl.BlockSpec(memory_space=pltpu.VMEM)
    smem = pl.BlockSpec(memory_space=pltpu.SMEM)
    anywhere = pl.BlockSpec(memory_space=pl.ANY)

    def call(kernel, outs, in_specs, scratch=(), name=None, limit=VMEM_BYTES, work=0):
        held = pltpu.VMEM if name not in ("combine", "edge_sums") else jax.ShapeDtypeStruct
        cost = pl.CostEstimate(flops=work, bytes_accessed=0, transcendentals=0) if work else None
        return pl.pallas_call(
            kernel,
            out_shape=tuple(held(shape, dtype) for shape, dtype in outs),
            in_specs=in_specs,
            out_specs=tuple(vmem for _ in outs),
            scratch_shapes=list(scratch),
            compiler_params=pltpu.CompilerParams(vmem_limit_bytes=limit),
            cost_estimate=cost,
            name=name,
        )

    def from_others(value):
        return [value] + [
            lax.ppermute(value, "orbit", [((i + step) % orbits, i) for i in range(orbits)])
            for step in range(1, orbits)
        ]

    even_pairs = [(i, i ^ 1) for i in range(bands)]
    odd_pairs = [(i, (i + 1 if i % 2 else i - 1) % bands) for i in range(bands)]

    matrices_in = interp.reshape(slots, observations, width)
    line = (slots, 1, observations)
    message, matrices, weights, pick = call(
        functools.partial(data_kernel, orbits),
        (
            ((2 * slots + GROUP, width), F32),
            ((slots, observations, width), BF16),
            ((slots, observations), F32),
            ((slots, cells), BF16),
        ),
        [smem] + [anywhere] * 4,
        [
            pltpu.SMEM((slots,), jnp.int32),
            pltpu.VMEM(line, F32),
            pltpu.VMEM(line, F32),
            pltpu.SemaphoreType.DMA((3 + slots // CHUNK,)),
        ],
        "data_terms",
        DATA_VMEM_BYTES,
    )(live_count, block_map.reshape(slots), matrices_in, obs_value, obs_weight)
    messages = from_others(message)
    shifted, blocks = call(
        block_kernel,
        ((field_shape, F32), ((slots // 2, 2 * width, 2 * width), BF16)),
        [vmem] * 3,
        (),
        "blocks",
        work=WORK,
    )(kappa2, matrices, weights)

    order = pltpu.VMEM((orbits * slots, width), F32)
    edge_width = -(-2 * orbits * slots // LANES) * LANES
    rim = ((3, pieces, width), F32)
    edge = ((2, pieces, width), F32)
    wide_edge = ((max(slots // pieces + 1, rim[0][0]), pieces, width), F32)
    field = (field_shape, F32)
    slot_terms = ((slots, width), F32)
    start, right_side, precond, scatter, even, odd, terms = call(
        functools.partial(start_kernel, orbits, parity, ahead),
        (field, field, field, ((cells, edge_width), BF16), rim, wide_edge, slot_terms),
        [vmem] * (3 + orbits),
        [order],
        "start",
    )(shifted, pick, blocks, *messages)
    rim_odd = lax.ppermute(odd, "lon", odd_pairs)
    terms, even = call(
        functools.partial(normal_kernel, ahead),
        (slot_terms, rim),
        [smem] + [vmem] * 5,
        (),
        "normal_start",
        work=WORK,
    )(live_count, pick, start, blocks, even, terms)
    terms = from_others(terms)
    rim_even = lax.ppermute(even, "lon", even_pairs)
    image_inputs = (start, shifted, rim_even, rim_odd, scatter, precond, *terms)
    (even,) = call(
        functools.partial(pair_edge_kernel, parity, orbits),
        (edge,),
        [vmem] * (6 + orbits),
        [order],
        "pair_edge",
    )(*image_inputs)
    even = lax.ppermute(even, "lon", even_pairs)
    chunk = pieces + 1
    first, following, base, end, parts, chunks, terms = call(
        functools.partial(images_kernel, parity, orbits),
        (
            field,
            field,
            field,
            ((pieces, width), F32),
            ((4, width), F32),
            ((GROUP * chunk, width), F32),
            slot_terms,
        ),
        [vmem] * (9 + orbits),
        [order],
        "images",
        work=WORK,
    )(*image_inputs[:6], right_side, pick, blocks, *terms)
    terms = from_others(terms)
    message = ((orbits * bands * chunk, width), F32)
    (sums,) = call(
        functools.partial(edge_kernel, parity), (message,), [vmem] * 4, (), "edge_sums"
    )(even, end, parts, chunks)
    sums = lax.all_to_all(sums[:, None], ("orbit", "lon"), 0, 0, tiled=True)[:, 0]
    return call(
        functools.partial(last_kernel, parity, orbits, bands),
        ((kappa2.shape, F32), (kappa2.shape, F32)),
        [vmem] * (10 + orbits),
        [order, pltpu.VMEM(field_shape, F32)],
        "combine",
    )(
        sums, start, following, right_side, first, base, shifted, even, rim_even, scatter, *terms
    )


def solution(mesh):
    in_specs = (
        P("orbit", "lon", None, None),
        P("orbit", "lon", None),
        P("orbit", "lon", None),
        P("orbit", "lon"),
        P("orbit", "lon"),
        P("lon", None),
    )
    out_specs = (P("lon", None), P("lon", None))
    body = functools.partial(per_device, mesh.shape["orbit"], mesh.shape["lon"])
    return jax.shard_map(
        body, mesh=mesh, in_specs=in_specs, out_specs=out_specs, check_vma=False
    )
```

```python
import functools

import jax
import jax.numpy as jnp
from jax import lax
from jax.experimental import pallas as pl
from jax.experimental.pallas import tpu as pltpu
from jax.sharding import PartitionSpec as P

PRIOR_WEIGHT = 0.0625
GROUP = 8
LANES = 128
F32 = jnp.float32
BF16 = jnp.bfloat16
VMEM_BYTES = 48 * 1024 * 1024
DATA_VMEM_BYTES = 59 * 1024 * 1024
CHUNK = 8
WORK = 1 << 32


def two_terms(value):
    high = value.astype(BF16)
    low = (value - high.astype(F32)).astype(BF16)
    return high, low


def stacked_terms(value):
    return jnp.concatenate(two_terms(value), axis=0)


def fold_terms(product):
    half = product.shape[0] // 2
    return product[:half] + product[half:]


def dot(left, right):
    return lax.dot_general(left, right, (((1,), (0,)), ((), ())), preferred_element_type=F32)


def pick_row(total, product, slot):
    rows = lax.broadcasted_iota(jnp.int32, product.shape, 0)
    return jnp.where(rows == slot, product, total)


def lat_pair(field):
    pieces = field.shape[1]
    piece = lax.broadcasted_iota(jnp.int32, field.shape, 1)
    lane = lax.broadcasted_iota(jnp.int32, field.shape, 2)
    south = pltpu.roll(field, 1, 2)
    north = pltpu.roll(field, LANES - 1, 2)
    south_over = jnp.where(piece == 0, 0.0, pltpu.roll(south, 1, 1))
    north_over = jnp.where(piece == pieces - 1, 0.0, pltpu.roll(north, pieces - 1, 1))
    return jnp.where(lane == 0, south_over, south) + jnp.where(lane == LANES - 1, north_over, north)


def stencil(field, shifted):
    center = field[1:-1]
    return shifted * center - field[2:] - field[:-2] - lat_pair(center)


def data_kernel(
    orbits,
    count_ref,
    map_in,
    interp_in,
    value_in,
    weight_in,
    message_ref,
    matrices_ref,
    weight_ref,
    pick_ref,
    map_ref,
    value_rows,
    weight_rows,
    sems,
):
    slots = matrices_ref.shape[0]
    pairs = ((weight_in, weight_rows), (value_in, value_rows), (map_in, map_ref))
    small = [
        pltpu.make_async_copy(source, target, sems.at[index])
        for index, (source, target) in enumerate(pairs)
    ]
    large = []
    for index in range(slots // CHUNK):
        part = pl.ds(index * CHUNK, CHUNK)
        large.append(
            pltpu.make_async_copy(
                interp_in.at[part], matrices_ref.at[part], sems.at[len(small) + index]
            )
        )
    count = count_ref[0, 0]
    for copy in small:
        copy.start()
    for index, copy in enumerate(large):
        pl.when(index * CHUNK < count)(copy.start)
    for copy in small:
        copy.wait()
    orbit = lax.axis_index("orbit")
    total = orbits * slots
    place = lax.broadcasted_iota(jnp.int32, (GROUP, LANES), 0) * LANES
    place = place + lax.broadcasted_iota(jnp.int32, (GROUP, LANES), 1)
    slot_here = jnp.where(place >= total, place - total, place) - orbit * slots
    target_row = jnp.zeros((GROUP, LANES), jnp.int32)
    for slot in range(slots):
        live_target = jnp.where(slot < count, map_ref[slot] + 1, 0)
        target_row = jnp.where(slot_here == slot, live_target, target_row)
    target_row = jnp.where(place < 2 * total, target_row, 0)
    message_ref[pl.ds(2 * slots, GROUP), :] = target_row.astype(F32)
    row = lax.broadcasted_iota(jnp.int32, (GROUP, pick_ref.shape[1]), 0)
    cell = lax.broadcasted_iota(jnp.int32, row.shape, 1)
    for group in range(slots // GROUP):
        target = jnp.zeros(row.shape, jnp.int32)
        for slot in range(GROUP):
            index = group * GROUP + slot
            live_target = jnp.where(index < count, map_ref[index], -1)
            target = jnp.where(row == slot, live_target, target)
        part = pl.ds(group * GROUP, GROUP)
        pick_ref[part, :] = jnp.where(cell == target, 1.0, 0.0).astype(BF16)
    weight_ref[...] = weight_rows[:, 0, :]

    def work(index):
        large[index].wait()
        for group in range(index * CHUNK // GROUP, (index + 1) * CHUNK // GROUP):
            part = pl.ds(group * GROUP, GROUP)
            weights = weight_rows[part, 0, :]
            scaled = (weights * value_rows[part, 0, :]).astype(BF16)
            high, low = two_terms(weights)
            rows = jnp.concatenate([scaled, high, low, low], axis=0)
            first = jnp.zeros((GROUP, LANES), F32)
            second = jnp.zeros((GROUP, LANES), F32)
            for slot in range(GROUP):
                matrix = matrices_ref[group * GROUP + slot]
                both = dot(rows, jnp.concatenate([matrix, matrix * matrix], axis=1))
                squares = both[GROUP : 2 * GROUP, LANES:] + both[2 * GROUP : 3 * GROUP, LANES:]
                first = pick_row(first, both[:GROUP, :LANES], slot)
                second = pick_row(second, squares, slot)
            message_ref[part, :] = first
            message_ref[pl.ds(slots + group * GROUP, GROUP), :] = second

    def rest(index):
        part = pl.ds(index * CHUNK, CHUNK)
        matrices_ref[part] = jnp.zeros((CHUNK,) + matrices_ref.shape[1:], BF16)
        for start in (0, slots):
            part = pl.ds(start + index * CHUNK, CHUNK)
            message_ref[part, :] = jnp.zeros((CHUNK, LANES), F32)

    chunks = range(slots // CHUNK)
    for index in chunks:
        pl.when(index * CHUNK >= count)(functools.partial(rest, index))
    for index in chunks:
        pl.when(index * CHUNK < count)(functools.partial(work, index))


def block_kernel(kappa_ref, matrices_ref, weight_ref, shifted_ref, blocks_ref):
    shifted_ref[...] = kappa_ref[...].reshape(shifted_ref.shape) + 4.0
    width = matrices_ref.shape[2]
    for slot in range(matrices_ref.shape[0]):
        matrix = matrices_ref[slot]
        weighted = matrix.T.astype(F32) * weight_ref[pl.ds(slot, 1), :]
        high, low = two_terms(fold_terms(dot(stacked_terms(weighted), matrix)))
        columns = pl.ds(slot % 2 * width, width)
        blocks_ref[slot // 2, pl.ds(0, width), columns] = high
        blocks_ref[slot // 2, pl.ds(width, width), columns] = low


def gather_messages(orbits, slots, message_refs, order_ref):
    orbit = lax.axis_index("orbit")
    for step in range(orbits):
        source = lax.rem(orbit + step, orbits)
        rows = pl.ds(pl.multiple_of(source * slots, slots), slots)
        order_ref[rows, :] = message_refs[step]


def start_kernel(
    orbits, parity, shifted_ref, *refs
):
    message_refs = refs[:orbits]
    (
        field_ref,
        right_ref,
        precond_ref,
        scatter_ref,
        even_ref,
        odd_ref,
        order_ref,
    ) = refs[orbits:]
    slots = (message_refs[0].shape[0] - GROUP) // 2
    cells = scatter_ref.shape[0]
    targets = message_refs[0][pl.ds(2 * slots, GROUP), :]
    for ref in message_refs[1:]:
        targets = targets + ref[pl.ds(2 * slots, GROUP), :]
    targets = targets.astype(jnp.int32) - 1
    row = lax.broadcasted_iota(jnp.int32, (cells, LANES), 0)
    for piece in range(scatter_ref.shape[1] // LANES):
        hit = row == targets[piece : piece + 1, :]
        scatter_ref[:, pl.ds(piece * LANES, LANES)] = jnp.where(hit, 1.0, 0.0).astype(BF16)
    sums = []
    for part in range(2):
        rows = pl.ds(part * slots, slots)
        gather_messages(orbits, slots, [ref[rows, :] for ref in message_refs], order_ref)
        sums.append(scattered(scatter_ref[...], order_ref[...]))
    right_side, obs_diag = (value.reshape(field_ref.shape) for value in sums)
    shifted = shifted_ref[...]
    precond = PRIOR_WEIGHT * (shifted * shifted + 4.0) + obs_diag
    field = right_side / precond
    right_ref[...] = right_side
    precond_ref[...] = precond
    field_ref[...] = field
    columns = field.shape[0]
    top = jnp.concatenate([field[:2], shifted[:1]], axis=0)
    bottom = jnp.concatenate([field[columns - 2 :], shifted[columns - 1 :]], axis=0)
    store_edges(parity, top, bottom, even_ref, odd_ref)


def normal_kernel(
    count_ref, pick_ref, field_ref, blocks_ref, even_ref, out_ref, even_out_ref
):
    even_out_ref[...] = even_ref[...]
    slots = pick_ref.shape[0]
    half = max(slots // (2 * GROUP), 1) * GROUP
    few = count_ref[0, 0] <= half

    @pl.when(few)
    def _():
        normal_slots(pick_ref, field_ref[...], blocks_ref, out_ref, half)

    @pl.when(jnp.logical_not(few))
    def _():
        normal_slots(pick_ref, field_ref[...], blocks_ref, out_ref)


def scattered(one_hot, slots):
    terms = stacked_terms(slots)
    spare = one_hot.shape[1] - terms.shape[0]
    if spare:
        terms = jnp.concatenate([terms, jnp.zeros((spare, LANES), BF16)], axis=0)
    return dot(one_hot, terms)


def store_edges(parity, top, bottom, even_ref, odd_ref):
    flip = parity()
    used = top.shape[0]
    even_ref[...] = jnp.where(flip, top, bottom)
    odd_ref[:used] = jnp.where(flip, bottom, top)
    if odd_ref.shape[0] > used:
        odd_ref[used:] = jnp.zeros((odd_ref.shape[0] - used,) + top.shape[1:], F32)


def load_edges(parity, even_ref, odd_ref):
    flip = parity()
    even = even_ref[...]
    odd = odd_ref[: even.shape[0]]
    return jnp.where(flip, even, odd), jnp.where(flip, odd, even)


def normal_slots(pick_ref, field, blocks_ref, out_ref, used=None):
    width = field.shape[-1]
    field = field.reshape(pick_ref.shape[1], width)
    used = used or pick_ref.shape[0]
    picked = dot(pick_ref[pl.ds(0, used), :], jnp.concatenate(two_terms(field), axis=1))
    picked = picked[:, :width] + picked[:, width:]
    energy = jnp.zeros((GROUP, width), F32)
    spare = pick_ref.shape[0] - used
    if spare:
        out_ref[pl.ds(used, spare), :] = jnp.zeros((spare, width), F32)
    for group in range(used // GROUP):
        cells = picked[group * GROUP : (group + 1) * GROUP]
        rows = stacked_terms(cells)
        rows = jnp.concatenate([rows, rows], axis=1)
        total = jnp.zeros((GROUP, width), F32)
        for slot in range(0, GROUP, 2):
            product = fold_terms(dot(rows, blocks_ref[(group * GROUP + slot) // 2]))
            total = pick_row(total, product[:, :width], slot)
            total = pick_row(total, product[:, width:], slot + 1)
        out_ref[pl.ds(group * GROUP, GROUP), :] = total
        energy = energy + cells * total
    return energy


def extended(field, top, bottom):
    return jnp.concatenate([top, field, bottom], axis=0)


def prior_parts(field, shifted, top, bottom, shifted_top, shifted_bottom):
    first = stencil(
        extended(field, top, bottom), extended(shifted, shifted_top, shifted_bottom)
    )
    return PRIOR_WEIGHT * stencil(first, shifted)


def scattered_slots(orbits, scatter_ref, slot_refs, order_ref):
    slots = slot_refs[0].shape[0]
    gather_messages(orbits, slots, [ref[...] for ref in slot_refs], order_ref)
    return scattered(scatter_ref[...], order_ref[...])


def pair_edge_kernel(
    parity,
    orbits,
    field_ref,
    shifted_ref,
    even_ref,
    odd_ref,
    scatter_ref,
    precond_ref,
    *refs,
):
    slot_refs = refs[:orbits]
    edge_ref, order_ref = refs[orbits:]
    slots = slot_refs[0].shape[0]
    gather_messages(orbits, slots, [ref[...] for ref in slot_refs], order_ref)
    columns, pieces, width = field_ref.shape
    flip = parity()
    top, bottom = load_edges(parity, even_ref, odd_ref)
    field = jnp.where(
        flip,
        extended(field_ref[pl.ds(0, 2)], top[:2], field_ref[pl.ds(2, 2)]),
        extended(field_ref[pl.ds(columns - 2, 2)], field_ref[pl.ds(columns - 4, 2)], bottom[:2]),
    )
    shifted = jnp.where(
        flip,
        jnp.concatenate([top[2:], shifted_ref[pl.ds(0, 3)]], axis=0),
        jnp.concatenate([shifted_ref[pl.ds(columns - 3, 3)], bottom[2:]], axis=0),
    )
    once = stencil(field, shifted)
    twice = stencil(once, shifted[1:-1])
    start = jnp.where(flip, 0, columns - 2)
    rows = pl.ds(pl.multiple_of(start * pieces, 2 * pieces), 2 * pieces)
    normal = scattered(scatter_ref[rows, :], order_ref[...]).reshape(twice.shape)
    edge_ref[...] = (PRIOR_WEIGHT * twice + normal) / precond_ref[pl.ds(start, 2)]


def alone(field, shifted):
    zero = jnp.zeros((1,) + field.shape[1:], F32)
    return stencil(extended(field, zero, zero), shifted)


def sides(parity, top, bottom):
    flip = parity()
    return jnp.where(flip, top, bottom), jnp.where(flip, bottom, top)


def near_far(parity, even_ref):
    flip = parity()
    return jnp.where(flip, even_ref[1], even_ref[0]), jnp.where(flip, even_ref[0], even_ref[1])


def chunks_of(rows):
    return jnp.concatenate([rows] * GROUP, axis=0)


def images_kernel(
    parity,
    orbits,
    field_ref,
    shifted_ref,
    even_ref,
    odd_ref,
    scatter_ref,
    precond_ref,
    right_ref,
    pick_ref,
    blocks_ref,
    *refs,
):
    slot_refs = refs[:orbits]
    image_ref, next_ref, base_ref, end_ref, parts_ref, chunks_ref, out_ref, order_ref = refs[orbits:]
    normal = scattered_slots(orbits, scatter_ref, slot_refs, order_ref)
    top, bottom = load_edges(parity, even_ref, odd_ref)
    start, shifted = field_ref[...], shifted_ref[...]
    prior = prior_parts(start, shifted, top[:2], bottom[:2], top[2:], bottom[2:])
    image = prior + normal.reshape(start.shape)
    field = image / precond_ref[...]
    image_ref[...] = image
    next_ref[...] = field
    energy = normal_slots(pick_ref, field, blocks_ref, out_ref)
    once = alone(field, shifted)
    base_ref[...] = PRIOR_WEIGHT * alone(once, shifted)
    last = once.shape[0] - 1
    even_end, odd_end = sides(parity, once[0], once[last])
    _, odd_field = sides(parity, field[0], field[last])
    end_ref[...] = even_end
    orbit = lax.axis_index("orbit")
    own = jnp.where(orbit == 0, 1.0, 0.0)
    squares = jnp.sum(once * once, axis=0) + odd_field * odd_field
    parts = (
        own * jnp.sum(right_ref[...] * start, axis=0),
        own * jnp.sum(start * image, axis=0),
        own * jnp.sum(image * field, axis=0),
        own * PRIOR_WEIGHT * squares + energy,
    )
    for index, part in enumerate(parts):
        parts_ref[pl.ds(index, 1), :] = jnp.sum(part, axis=0, keepdims=True)
    edge = jnp.where(orbit == 0, odd_end, odd_field)
    chunks_ref[...] = chunks_of(jnp.concatenate([edge, jnp.zeros((1, LANES), F32)], axis=0))


def edge_kernel(
    parity, even_ref, end_ref, parts_ref, chunks_ref, message_ref, filled_ref, sems
):
    near, _ = near_far(parity, even_ref)
    own = jnp.where(lax.axis_index("orbit") == 0, PRIOR_WEIGHT, 0.0)
    more = own * jnp.sum(near * (near - 2.0 * end_ref[...]), axis=0, keepdims=True)
    index = lax.broadcasted_iota(jnp.int32, (4, LANES), 0)
    lane = lax.broadcasted_iota(jnp.int32, (4, LANES), 1)
    sums = jnp.sum(parts_ref[...] + jnp.where(index == 3, more, 0.0), axis=1, keepdims=True)
    line = jnp.sum(jnp.where(lane == index, sums, 0.0), axis=0, keepdims=True)
    rows = chunks_ref.shape[0]
    period = rows // GROUP
    row = lax.broadcasted_iota(jnp.int32, (rows, LANES), 0)
    filled_ref[...] = jnp.where(lax.rem(row, period) == period - 1, line, chunks_ref[...])
    copies = [
        pltpu.make_async_copy(
            filled_ref, message_ref.at[pl.ds(index * rows, rows)], sems.at[index]
        )
        for index in range(message_ref.shape[0] // rows)
    ]
    for copy in copies:
        copy.start()
    for copy in copies:
        copy.wait()


def last_kernel(
    parity,
    orbits,
    bands,
    received_ref,
    start_ref,
    next_ref,
    right_ref,
    first_ref,
    base_ref,
    shifted_ref,
    even_ref,
    rim_ref,
    scatter_ref,
    *refs,
):
    slot_refs = refs[:orbits]
    out_ref, residual_ref, order_ref, second_ref = refs[orbits:]
    columns, pieces, _ = start_ref.shape
    rows = pieces + 1

    def end_of(band):
        return received_ref[pl.ds(band * rows, pieces), :]

    def field_of(band):
        return received_ref[pl.ds((bands + band) * rows, pieces), :]

    open_sides = jnp.zeros((pieces, LANES), F32)
    for band in range(1, bands, 2):
        above = (band + 1) % bands
        open_sides = open_sides + end_of(band) * field_of(above) + end_of(above) * field_of(band)
    open_sides = jnp.sum(jnp.sum(open_sides, axis=0, keepdims=True), axis=1, keepdims=True)
    lines = received_ref[pl.ds(pieces, orbits * bands, stride=rows), :]
    line = jnp.sum(lines, axis=0, keepdims=True)
    lane = lax.broadcasted_iota(jnp.int32, line.shape, 1)
    product, energy, cross, following = (
        jnp.sum(jnp.where(lane == index, line, 0.0), axis=1, keepdims=True) for index in range(4)
    )
    following = following - (2.0 * PRIOR_WEIGHT) * open_sides
    alpha = product / energy
    later = alpha * alpha * cross - product
    grown = 1.0 + later / product
    later_energy = alpha * alpha * following - grown * grown * energy
    later_alpha = later / later_energy
    on_start = alpha + later_alpha * grown
    on_next = -alpha * later_alpha

    normal = scattered_slots(orbits, scatter_ref, slot_refs, order_ref)
    second_ref[...] = base_ref[...] + normal.reshape(second_ref.shape)
    flip = parity()
    band = lax.axis_index("lon")
    across = lax.rem(band + jnp.where(flip, 1, bands - 1), bands)
    even_field, odd_field = sides(parity, next_ref[0], next_ref[columns - 1])
    near, far = near_far(parity, even_ref)
    even_first = rim_ref[2] * near - far - even_field - lat_pair(near[None])[0]
    odd_near = field_of(across)
    odd_first = end_of(across) - odd_field
    ends = (
        (0, 1, jnp.where(flip, near, odd_near), jnp.where(flip, even_first, odd_first)),
        (
            columns - 1,
            columns - 2,
            jnp.where(flip, odd_near, near),
            jnp.where(flip, odd_first, even_first),
        ),
    )
    for end, inner, field, first in ends:
        change = lat_pair(field[None])[0] - shifted_ref[end] * field - first
        second_ref[end] = second_ref[end] + PRIOR_WEIGHT * change
        second_ref[inner] = second_ref[inner] + PRIOR_WEIGHT * field

    out = on_start * start_ref[...] + on_next * next_ref[...]
    residual = right_ref[...] - on_start * first_ref[...] - on_next * second_ref[...]
    out_ref[...] = out.reshape(out_ref.shape)
    residual_ref[...] = residual.reshape(residual_ref.shape)


def per_device(orbits, bands, interp, obs_value, obs_weight, block_map, live_count, kappa2):
    slots, _, observations, width = interp.shape
    columns, latitudes = kappa2.shape
    pieces = latitudes // width
    cells = columns * pieces
    field_shape = (columns, pieces, width)

    def parity():
        return lax.rem(lax.axis_index("lon"), 2) == 1

    vmem = pl.BlockSpec(memory_space=pltpu.VMEM)
    smem = pl.BlockSpec(memory_space=pltpu.SMEM)
    anywhere = pl.BlockSpec(memory_space=pl.ANY)

    def call(kernel, outs, in_specs, scratch=(), name=None, limit=VMEM_BYTES, work=0):
        held = pltpu.VMEM if name not in ("combine", "edge_sums") else jax.ShapeDtypeStruct
        cost = pl.CostEstimate(flops=work, bytes_accessed=0, transcendentals=0) if work else None
        return pl.pallas_call(
            kernel,
            out_shape=tuple(held(shape, dtype) for shape, dtype in outs),
            in_specs=in_specs,
            out_specs=tuple(anywhere if name == "edge_sums" else vmem for _ in outs),
            scratch_shapes=list(scratch),
            compiler_params=pltpu.CompilerParams(vmem_limit_bytes=limit),
            cost_estimate=cost,
            name=name,
        )

    def from_others(value):
        return [value] + [
            lax.ppermute(value, "orbit", [((i + step) % orbits, i) for i in range(orbits)])
            for step in range(1, orbits)
        ]

    even_pairs = [(i, i ^ 1) for i in range(bands)]
    odd_pairs = [(i, (i + 1 if i % 2 else i - 1) % bands) for i in range(bands)]

    matrices_in = interp.reshape(slots, observations, width)
    line = (slots, 1, observations)
    message, matrices, weights, pick = call(
        functools.partial(data_kernel, orbits),
        (
            ((2 * slots + GROUP, width), F32),
            ((slots, observations, width), BF16),
            ((slots, observations), F32),
            ((slots, cells), BF16),
        ),
        [smem] + [anywhere] * 4,
        [
            pltpu.SMEM((slots,), jnp.int32),
            pltpu.VMEM(line, F32),
            pltpu.VMEM(line, F32),
            pltpu.SemaphoreType.DMA((3 + slots // CHUNK,)),
        ],
        "data_terms",
        DATA_VMEM_BYTES,
    )(live_count, block_map.reshape(slots), matrices_in, obs_value, obs_weight)
    messages = from_others(message)
    shifted, blocks = call(
        block_kernel,
        ((field_shape, F32), ((slots // 2, 2 * width, 2 * width), BF16)),
        [vmem] * 3,
        (),
        "blocks",
        work=WORK,
    )(kappa2, matrices, weights)

    order = pltpu.VMEM((orbits * slots, width), F32)
    edge_width = -(-2 * orbits * slots // LANES) * LANES
    rim = ((3, pieces, width), F32)
    edge = ((2, pieces, width), F32)
    wide_edge = ((max(slots // pieces + 1, rim[0][0]), pieces, width), F32)
    field = (field_shape, F32)
    slot_terms = ((slots, width), F32)
    start, right_side, precond, scatter, even, odd = call(
        functools.partial(start_kernel, orbits, parity),
        (field, field, field, ((cells, edge_width), BF16), rim, wide_edge),
        [vmem] * (1 + orbits),
        [order],
        "start",
    )(shifted, *messages)
    rim_odd = lax.ppermute(odd, "lon", odd_pairs)
    terms, even = call(
        normal_kernel,
        (slot_terms, rim),
        [smem] + [vmem] * 4,
        (),
        "normal_start",
        work=WORK,
    )(live_count, pick, start, blocks, even)
    terms = from_others(terms)
    rim_even = lax.ppermute(even, "lon", even_pairs)
    image_inputs = (start, shifted, rim_even, rim_odd, scatter, precond, *terms)
    (even,) = call(
        functools.partial(pair_edge_kernel, parity, orbits),
        (edge,),
        [vmem] * (6 + orbits),
        [order],
        "pair_edge",
    )(*image_inputs)
    even = lax.ppermute(even, "lon", even_pairs)
    chunk = pieces + 1
    first, following, base, end, parts, chunks, terms = call(
        functools.partial(images_kernel, parity, orbits),
        (
            field,
            field,
            field,
            ((pieces, width), F32),
            ((4, width), F32),
            ((GROUP * chunk, width), F32),
            slot_terms,
        ),
        [vmem] * (9 + orbits),
        [order],
        "images",
        work=WORK,
    )(*image_inputs[:6], right_side, pick, blocks, *terms)
    terms = from_others(terms)
    message = ((orbits * bands * chunk, width), F32)
    (sums,) = call(
        functools.partial(edge_kernel, parity),
        (message,),
        [vmem] * 4,
        [
            pltpu.VMEM((GROUP * chunk, width), F32),
            pltpu.SemaphoreType.DMA((orbits * bands // GROUP,)),
        ],
        "edge_sums",
    )(even, end, parts, chunks)
    sums = lax.all_to_all(sums[:, None], ("orbit", "lon"), 0, 0, tiled=True)[:, 0]
    return call(
        functools.partial(last_kernel, parity, orbits, bands),
        ((kappa2.shape, F32), (kappa2.shape, F32)),
        [vmem] * (10 + orbits),
        [order, pltpu.VMEM(field_shape, F32)],
        "combine",
    )(
        sums, start, following, right_side, first, base, shifted, even, rim_even, scatter, *terms
    )


def solution(mesh):
    in_specs = (
        P("orbit", "lon", None, None),
        P("orbit", "lon", None),
        P("orbit", "lon", None),
        P("orbit", "lon"),
        P("orbit", "lon"),
        P("lon", None),
    )
    out_specs = (P("lon", None), P("lon", None))
    body = functools.partial(per_device, mesh.shape["orbit"], mesh.shape["lon"])
    return jax.shard_map(
        body, mesh=mesh, in_specs=in_specs, out_specs=out_specs, check_vma=False
    )
```
